32 devices in a mesh: fsdp: 32 (over z, y, x, core).
Axes of the slice: x: 2, y: 2, z: 4, core: 2. Of those that a mesh axis runs over, the one named last changes fastest.
Arguments:
- hidden: bfloat16 [32768, 768], P('fsdp'), may hold values from -6 to 6
- lengths: int32 [64], P('fsdp'), may hold values from 100 to 780, as said below
- w_qkv: bfloat16 [768, 2304], P('fsdp'), may hold values from -0.21875 to 0.21875
- bias_q: bfloat16 [768], P('fsdp'), may hold values from -2 to 2
- bias_v: bfloat16 [768], P('fsdp'), may hold values from -2 to 2
- w_out: bfloat16 [768, 768], P('fsdp'), may hold values from -0.75 to 0.75
- bias_out: bfloat16 [768], P('fsdp'), may hold values from -2 to 2
- norm1_gain: bfloat16 [768], P('fsdp'), may hold values from 0.5 to 1.5
- norm1_bias: bfloat16 [768], P('fsdp'), may hold values from -2 to 2
- w_up: bfloat16 [768, 3072], P('fsdp'), may hold values from -0.21875 to 0.21875
- bias_up: bfloat16 [3072], P('fsdp'), may hold values from -3 to 3
- w_down: bfloat16 [3072, 768], P('fsdp'), may hold values from -0.109375 to 0.109375
- bias_down: bfloat16 [768], P('fsdp'), may hold values from -2 to 2
- norm2_gain: bfloat16 [768], P('fsdp'), may hold values from 0.5 to 1.5
- norm2_bias: bfloat16 [768], P('fsdp'), may hold values from -2 to 2
- cotangent: bfloat16 [32768, 768], P('fsdp'), may hold values from -6 to 6
Outputs:
- output: float32 [32768, 768], P('fsdp')
- grad_hidden: float32 [32768, 768], P('fsdp')
- grad_w_qkv: float32 [768, 2304], P('fsdp')
- grad_bias_q: float32 [768], P('fsdp')
- grad_bias_v: float32 [768], P('fsdp')
- grad_w_out: float32 [768, 768], P('fsdp')
- grad_bias_out: float32 [768], P('fsdp')
- grad_norm1_gain: float32 [768], P('fsdp')
- grad_norm1_bias: float32 [768], P('fsdp')
- grad_w_up: float32 [768, 3072], P('fsdp')
- grad_bias_up: float32 [3072], P('fsdp')
- grad_w_down: float32 [3072, 768], P('fsdp')
- grad_bias_down: float32 [768], P('fsdp')
- grad_norm2_gain: float32 [768], P('fsdp')
- grad_norm2_bias: float32 [768], P('fsdp')
The draws below stay inside these ranges and needn't reach their ends.
Inputs may be any that keep to these rules, and one draw needn't show every extreme that they name: Block b of 1024 frames holds utterances b*2 to (b+1)*2 - 1 in order from its first frame; a block's lengths sum to at most 1024, the rest is padding. In every draw some utterance has exactly 780 frames.
All inputs are finite; a program needn't handle non-finite values.
Results may differ from the reference program's by a relative error of at most 0.013.
Values may be sent and summed in bfloat16 or wider, within the bound.
No kernel may reach another device: no remote copies, remote signals or barrier semaphores. Data moves between devices by JAX's collectives and lax.ppermute only.
A program may use at most 256 MiB of HBM per device.

```python
import jax
import jax.numpy as jnp
from jax import lax

D = 768
DH = 64
FF = 3072
UTT_DEV = 2
LMAX = 780
LMIN = 100
ROWS = 1024
FRAMES = 32768
UTTS = 64
N_FSDP = 32


def draw_lengths(key, part):
    key = jax.random.fold_in(key, 7)
    devices = UTTS // UTT_DEV
    chosen = jax.random.randint(jax.random.fold_in(key, 0), (), 0, devices)
    used = jnp.zeros((devices,), jnp.int32)
    columns = []
    for index in range(UTT_DEV):
        upper = jnp.minimum(LMAX, ROWS - used - (UTT_DEV - 1 - index) * LMIN)
        column = jax.random.randint(jax.random.fold_in(key, index + 1), (devices,), LMIN, upper + 1)
        if index == 0:
            column = jnp.where(jnp.arange(devices) == chosen, LMAX, column)
        used = used + column
        columns.append(column)
    return jnp.stack(columns, axis=1).reshape(UTTS).astype(jnp.int32)


def block_scale(own_key, shape, split, smallest, top_value):
    def one(dim, parts):
        steps = jax.random.uniform(jax.random.fold_in(jax.random.fold_in(own_key, 6), dim), (parts,), jnp.float32, smallest / len(split), top_value / len(split))
        return jnp.repeat(jnp.exp(steps), shape[dim] // parts).reshape((-1,) + (1,) * (len(shape) - dim - 1))

    level = one(*split[0])
    for cut in split[1:]:
        level = level * one(*cut)
    return level


def normal_values(key, dims, scale, bound, pieces=(), held_as=jnp.bfloat16):
    level = block_scale(key, dims, pieces, -0.22, 0.18) if pieces else 1.0
    values = jax.random.normal(key, dims, jnp.float32) * scale * level
    return jnp.minimum(jnp.maximum(values, -bound), bound).astype(held_as)


def setup_inputs(seed: int = 0) -> dict:
    key_list = jax.random.split(jax.random.key(seed), 17)
    hidden = normal_values(key_list[0], (FRAMES, D), 1.0, 6.0, ((0, 32),))
    lengths = draw_lengths(jax.random.fold_in(key_list[16], 71), 0)
    w_qkv = normal_values(key_list[2], (D, 3 * D), D ** -0.5, 0.21875, ((0, 32),))
    bias_q = normal_values(key_list[3], (D,), 0.3, 2.0, ((0, 32),))
    bias_v = normal_values(key_list[4], (D,), 0.3, 2.0, ((0, 32),))
    w_out = normal_values(key_list[5], (D, D), DH ** -0.5, 0.75, ((0, 32),))
    bias_out = normal_values(key_list[6], (D,), 0.3, 2.0, ((0, 32),))
    norm1_gain = jnp.clip(1.0 + 0.1 * jax.random.normal(key_list[7], (D,), jnp.float32), 0.5, 1.5).astype(jnp.bfloat16)
    norm1_bias = normal_values(key_list[8], (D,), 0.3, 2.0, ((0, 32),))
    w_up = normal_values(key_list[9], (D, FF), D ** -0.5, 0.21875, ((0, 32),))
    bias_up = normal_values(key_list[10], (FF,), 0.5, 3.0, ((0, 32),))
    w_down = normal_values(key_list[11], (FF, D), FF ** -0.5, 0.109375, ((0, 32),))
    bias_down = normal_values(key_list[12], (D,), 0.3, 2.0, ((0, 32),))
    norm2_gain = jnp.clip(1.0 + 0.1 * jax.random.normal(key_list[13], (D,), jnp.float32), 0.5, 1.5).astype(jnp.bfloat16)
    norm2_bias = normal_values(key_list[14], (D,), 0.3, 2.0, ((0, 32),))
    cotangent = normal_values(key_list[15], (FRAMES, D), 1.0, 6.0, ((0, 32),))
    return dict(hidden=hidden, lengths=lengths, w_qkv=w_qkv, bias_q=bias_q, bias_v=bias_v, w_out=w_out, bias_out=bias_out, norm1_gain=norm1_gain, norm1_bias=norm1_bias, w_up=w_up, bias_up=bias_up, w_down=w_down, bias_down=bias_down, norm2_gain=norm2_gain, norm2_bias=norm2_bias, cotangent=cotangent)


@jax.custom_vjp
def low(v):
    return lax.optimization_barrier(v.astype(jnp.bfloat16)).astype(jnp.float32)

@jax.custom_vjp
def low_back(v):
    return v

def low_keep(v):
    return (low(v), None)

def low_pass(kept, grad):
    return (grad,)

def back_keep(v):
    return (v, None)

def back_low(kept, grad):
    return (low(grad),)
low.defvjp(low_keep, low_pass)
low_back.defvjp(back_keep, back_low)
EPSILON = 1e-05
PRECISE = lax.Precision.HIGHEST

def segments_of(lengths_here, count_rows):
    bounds = jnp.cumsum(lengths_here)
    position = jnp.arange(count_rows, dtype=jnp.int32)
    segment = lax.optimization_barrier(jnp.sum((position[:, None] >= bounds[None, :]).astype(jnp.int32), axis=1))
    return (segment, (segment < lengths_here.shape[0]).astype(jnp.float32))

def layer_norm(values_in, gain, shift):
    centre = lax.optimization_barrier(jnp.mean(values_in, axis=-1, keepdims=True))
    centered = values_in - centre
    spread = lax.optimization_barrier(jnp.mean(centered * centered, axis=-1, keepdims=True))
    return centered * lax.rsqrt(spread + EPSILON) * gain + shift

def layer(frames, weights, segment, present):
    w_qkv, bias_q, bias_v, w_out, bias_out, gain_one, shift_one, w_up, bias_up, w_down, bias_down, gain_two, shift_two = weights
    count_rows = frames.shape[0]
    heads = D // DH
    projected = jnp.dot(frames, w_qkv, precision=PRECISE)
    stacked = jnp.concatenate([projected[:, :D] + bias_q, projected[:, D:2 * D], projected[:, 2 * D:] + bias_v], axis=1)
    stacked = low(low_back(stacked))
    queries = stacked[:, :D].reshape(count_rows, heads, DH)
    key_rows = stacked[:, D:2 * D].reshape(count_rows, heads, DH)
    value_rows = stacked[:, 2 * D:].reshape(count_rows, heads, DH)
    scores = jnp.einsum('qhd,khd->hqk', queries, key_rows, precision=PRECISE) * DH ** (-0.5)
    scores = low_back(scores)
    same = segment[:, None] == segment[None, :]
    scores = jnp.where(same[None], scores, -1e+30)
    probs = jax.nn.softmax(scores, axis=-1)
    mixed = jnp.einsum('hqk,khd->qhd', low(probs), value_rows, precision=PRECISE).reshape(count_rows, D)
    mixed = low(low_back(mixed))
    branch = low_back(jnp.dot(mixed, w_out, precision=PRECISE) + bias_out)
    first = layer_norm(frames + branch, gain_one, shift_one)
    inner = low_back(jnp.dot(low(first), w_up, precision=PRECISE) + bias_up)
    activated = low(jax.nn.gelu(inner, approximate=False))
    second = low_back(jnp.dot(activated, w_down, precision=PRECISE) + bias_down)
    result = layer_norm(first + second, gain_two, shift_two)
    return result * present[:, None]

def reference(hidden, lengths, w_qkv, bias_q, bias_v, w_out, bias_out, norm1_gain, norm1_bias, w_up, bias_up, w_down, bias_down, norm2_gain, norm2_bias, cotangent):
    params = tuple((weight.astype(jnp.float32) for weight in (w_qkv, bias_q, bias_v, w_out, bias_out, norm1_gain, norm1_bias, w_up, bias_up, w_down, bias_down, norm2_gain, norm2_bias)))
    frames = hidden.astype(jnp.float32).reshape(N_FSDP, ROWS, D)
    upstream = cotangent.astype(jnp.float32).reshape(N_FSDP, ROWS, D)
    lengths_all = lengths.reshape(N_FSDP, UTT_DEV)

    def advance(totals, entry):
        frame_block, upstream_block, lengths_here = entry
        segment, present = segments_of(lengths_here, ROWS)

        def forward(frames_in, *weights):
            return layer(frames_in, weights, segment, present)
        result, pullback = jax.vjp(forward, frame_block, *params)
        gradients = pullback(upstream_block)
        totals = tuple((total + gradient for total, gradient in zip(totals, gradients[1:])))
        return (totals, (result, gradients[0]))
    zeros = tuple((jnp.zeros_like(param) for param in params))
    totals, (results, grad_frames) = lax.scan(advance, zeros, (frames, upstream, lengths_all))
    return (results.reshape(FRAMES, D), grad_frames.reshape(FRAMES, D), totals[0], totals[1], totals[2], totals[3], totals[4], totals[5], totals[6], totals[7], totals[8], totals[9], totals[10], totals[11], totals[12])
```

```python
import functools
import math

import jax
import jax.numpy as jnp
from jax import lax
from jax.experimental import pallas as pl
from jax.experimental.pallas import tpu as pltpu
from jax.sharding import PartitionSpec as P

DH = 64
PAIR = 2 * DH
BF = jnp.bfloat16
F32 = jnp.float32
NEG = -1e30
EPSILON = 1e-05
ROOT_HALF = 0.7071067811865476
INV_ROOT_TWO_PI = 0.3989422804014327
LAST_LAST = (((1,), (1,)), ((), ()))
VMEM_BYTES = 56 * 2**20


def norm_forward(values_in, gain, shift):
    centre = jnp.mean(values_in, axis=-1, keepdims=True)
    centered = values_in - centre
    spread = jnp.mean(centered * centered, axis=-1, keepdims=True)
    rstd_rows = lax.rsqrt(spread + EPSILON)
    normed = centered * rstd_rows
    return (normed * gain + shift, normed, rstd_rows)


def norm_backward(upstream, normed, rstd_rows, gain):
    scaled = upstream * gain
    plain_mean = jnp.mean(scaled, axis=-1, keepdims=True)
    cross_mean = jnp.mean(scaled * normed, axis=-1, keepdims=True)
    grad_in = rstd_rows * (scaled - plain_mean - normed * cross_mean)
    return (grad_in, jnp.sum(upstream * normed, axis=0), jnp.sum(upstream, axis=0))


def gelu_slope(inner):
    normal_cdf = 0.5 * (1.0 + lax.erf(inner * ROOT_HALF))
    return normal_cdf + inner * jnp.exp(-0.5 * inner * inner) * INV_ROOT_TWO_PI


def dot_last(a, b):
    return lax.dot_general(a, b, LAST_LAST, preferred_element_type=F32)


def dot(a, b):
    return jnp.dot(a, b, preferred_element_type=F32)


def segment_at(position, bounds_ref):
    segment = jnp.zeros(position.shape, jnp.int32)
    for index in range(bounds_ref.shape[0]):
        segment += (position >= bounds_ref[index]).astype(jnp.int32)
    return segment


def attention_forward_kernel(bounds_ref, q_ref, k_ref, v_ref, mixed_ref, logsum_ref, *, span, scale):
    rows = q_ref.shape[0]
    first_head = lax.broadcasted_iota(jnp.int32, (1, PAIR), 1) < DH
    key_segment = segment_at(lax.broadcasted_iota(jnp.int32, (1, rows), 1), bounds_ref)
    keys = k_ref[...]
    values = v_ref[...]
    for block in range(rows // span):
        here = pl.ds(block * span, span)
        queries = q_ref[here, :] * jnp.asarray(scale, BF)
        row = lax.broadcasted_iota(jnp.int32, (span, 1), 0) + block * span
        same = segment_at(row, bounds_ref) == key_segment
        mixed = []
        logsum = []
        for head in range(2):
            mine = first_head if head == 0 else jnp.logical_not(first_head)
            scores = dot_last(jnp.where(mine, queries, jnp.zeros_like(queries)), keys)
            scores = jnp.where(same, scores, NEG)
            highest = jnp.max(scores, axis=1, keepdims=True)
            exps = jnp.exp(scores - highest)
            total = jnp.sum(exps, axis=1, keepdims=True)
            mixed.append(dot(exps.astype(BF), values) * (1.0 / total))
            logsum.append(highest + jnp.log(total))
        mixed_ref[here, :] = jnp.where(first_head, mixed[0], mixed[1]).astype(BF)
        turned = jnp.transpose(jnp.where(first_head, logsum[0], logsum[1]))
        logsum_ref[0, 0:1, here] = turned[0:1]
        logsum_ref[0, 1:2, here] = turned[DH : DH + 1]


def pair_spec(rows, offset):
    return pl.BlockSpec((rows, PAIR), lambda pair, bounds: (0, offset + pair))


def attention_forward(bounds, stacked, span=512):
    rows, width = stacked.shape[0], stacked.shape[1] // 3
    pairs = width // PAIR
    return pl.pallas_call(
        functools.partial(attention_forward_kernel, span=span, scale=1.0 / math.sqrt(DH)),
        grid_spec=pltpu.PrefetchScalarGridSpec(
            num_scalar_prefetch=1,
            grid=(pairs,),
            in_specs=[pair_spec(rows, 0), pair_spec(rows, pairs), pair_spec(rows, 2 * pairs)],
            out_specs=[
                pair_spec(rows, 0),
                pl.BlockSpec((1, 8, rows), lambda pair, bounds: (pair, 0, 0)),
            ],
        ),
        out_shape=[
            jax.ShapeDtypeStruct((rows, width), BF),
            jax.ShapeDtypeStruct((pairs, 8, rows), F32),
        ],
        compiler_params=pltpu.CompilerParams(vmem_limit_bytes=VMEM_BYTES),
        cost_estimate=pl.CostEstimate(
            flops=4 * rows * rows * width * 4, bytes_accessed=8 * rows * width, transcendentals=0
        ),
        name="attention_forward",
    )(bounds, stacked, stacked, stacked)


def attention_backward_kernel(
    bounds_ref, q_ref, k_ref, v_ref, mixed_ref, grad_ref, logsum_ref, dq_ref, dk_ref, dv_ref, dk_sum, dv_sum, *, span, scale
):
    rows = q_ref.shape[0]
    first_head = lax.broadcasted_iota(jnp.int32, (1, PAIR), 1) < DH
    key_segment = segment_at(lax.broadcasted_iota(jnp.int32, (rows, 1), 0), bounds_ref)
    keys = k_ref[...]
    values = v_ref[...]
    keys_turned = jnp.transpose(keys)
    picks = (
        lax.broadcasted_iota(jnp.int32, (8, PAIR), 1) // DH
        == lax.broadcasted_iota(jnp.int32, (8, PAIR), 0)
    ).astype(F32)
    for block in range(rows // span):
        here = pl.ds(block * span, span)
        queries = q_ref[here, :]
        grads = grad_ref[here, :]
        weighted = lax.dot_general(
            picks,
            grads.astype(F32) * mixed_ref[here, :].astype(F32),
            LAST_LAST,
            preferred_element_type=F32,
            precision=lax.Precision.HIGHEST,
        )
        column = lax.broadcasted_iota(jnp.int32, (1, span), 1) + block * span
        same = key_segment == segment_at(column, bounds_ref)
        all_probs, all_scores, all_grads, all_queries, grad_queries = [], [], [], [], []
        for head in range(2):
            mine = first_head if head == 0 else jnp.logical_not(first_head)
            my_queries = jnp.where(mine, queries, jnp.zeros_like(queries)) * jnp.asarray(scale, BF)
            my_grads = jnp.where(mine, grads, jnp.zeros_like(grads))
            scores = dot_last(keys, my_queries) - logsum_ref[0, head : head + 1, here]
            probs = jnp.exp(jnp.where(same, scores, NEG))
            grad_probs = dot_last(values, my_grads)
            grad_scores = (probs * (grad_probs - weighted[head : head + 1])).astype(BF)
            all_probs.append(probs.astype(BF))
            all_scores.append(grad_scores)
            all_grads.append(my_grads)
            all_queries.append(my_queries)
            grad_queries.append(dot(keys_turned[DH * head : DH * (head + 1)], grad_scores))
        turned = jnp.concatenate(grad_queries, axis=0) * scale
        dq_ref[here, :] = jnp.transpose(turned).astype(BF)
        dv = dot(jnp.concatenate(all_probs, axis=1), jnp.concatenate(all_grads, axis=0))
        dk = dot(jnp.concatenate(all_scores, axis=1), jnp.concatenate(all_queries, axis=0))
        if block == 0:
            dv_sum[...] = dv
            dk_sum[...] = dk
        else:
            dv_sum[...] += dv
            dk_sum[...] += dk
    dk_ref[...] = dk_sum[...].astype(BF)
    dv_ref[...] = dv_sum[...].astype(BF)


def attention_backward(bounds, stacked, mixed, grad_mixed, logsum, span=256):
    rows, width = mixed.shape
    pairs = width // PAIR
    return pl.pallas_call(
        functools.partial(attention_backward_kernel, span=span, scale=1.0 / math.sqrt(DH)),
        grid_spec=pltpu.PrefetchScalarGridSpec(
            num_scalar_prefetch=1,
            grid=(pairs,),
            in_specs=[
                pair_spec(rows, 0),
                pair_spec(rows, pairs),
                pair_spec(rows, 2 * pairs),
                pair_spec(rows, 0),
                pair_spec(rows, 0),
                pl.BlockSpec((1, 8, rows), lambda pair, bounds: (pair, 0, 0)),
            ],
            out_specs=[pair_spec(rows, 0), pair_spec(rows, 0), pair_spec(rows, 0)],
            scratch_shapes=[pltpu.VMEM((rows, PAIR), F32), pltpu.VMEM((rows, PAIR), F32)],
        ),
        out_shape=[jax.ShapeDtypeStruct((rows, width), BF)] * 3,
        compiler_params=pltpu.CompilerParams(vmem_limit_bytes=VMEM_BYTES),
        cost_estimate=pl.CostEstimate(
            flops=10 * rows * rows * width * 4, bytes_accessed=16 * rows * width, transcendentals=0
        ),
        name="attention_backward",
    )(bounds, stacked, stacked, stacked, mixed, grad_mixed, logsum)


def on_device(
    hidden,
    lengths,
    w_qkv,
    bias_q,
    bias_v,
    w_out,
    bias_out,
    norm1_gain,
    norm1_bias,
    w_up,
    bias_up,
    w_down,
    bias_down,
    norm2_gain,
    norm2_bias,
    cotangent,
):
    count_rows, width = hidden.shape
    hidden_units = w_up.shape[1]
    n = lax.axis_size("fsdp")
    part = width // n
    inner_part = hidden_units // n
    wide = hidden_units // width
    bounds = jnp.cumsum(lengths)
    present = (jnp.arange(count_rows, dtype=jnp.int32) < bounds[-1]).astype(F32)[:, None]

    vectors = (bias_q, bias_v, bias_out, norm1_gain, norm1_bias, bias_up, bias_down, norm2_gain, norm2_bias)
    sizes = [vector.shape[0] for vector in vectors]
    starts = [sum(sizes[:i]) for i in range(len(sizes))]
    whole_qkv = lax.all_gather(w_qkv, "fsdp", axis=0, tiled=True)
    whole_vectors = lax.all_gather(jnp.concatenate(vectors)[None], "fsdp", axis=0, tiled=True)
    (
        whole_bias_q,
        whole_bias_v,
        whole_bias_out,
        whole_gain_one,
        whole_shift_one,
        whole_bias_up,
        whole_bias_down,
        whole_gain_two,
        whole_shift_two,
    ) = (
        whole_vectors[:, start : start + size].reshape(n * size).astype(F32)
        for start, size in zip(starts, sizes)
    )
    packed = jnp.concatenate(
        [w_out]
        + [w_up[:, width * i : width * (i + 1)] for i in range(wide)]
        + [w_down],
        axis=0,
    )
    gathered = lax.all_gather(packed, "fsdp", axis=0, tiled=True).reshape(n, -1, width)
    whole_out = gathered[:, :part].reshape(width, width)
    whole_up = (
        gathered[:, part : part * (1 + wide)]
        .reshape(n, wide, part, width)
        .transpose(0, 2, 1, 3)
        .reshape(width, hidden_units)
    )
    whole_down = gathered[:, part * (1 + wide) :].reshape(hidden_units, width)

    projected = jnp.dot(hidden, whole_qkv, preferred_element_type=F32)
    whole_bias = jnp.concatenate([whole_bias_q, jnp.zeros_like(whole_bias_q), whole_bias_v])
    stacked = (projected + whole_bias).astype(BF)
    mixed, logsum = attention_forward(bounds, stacked)
    branch = jnp.dot(mixed, whole_out, preferred_element_type=F32) + whole_bias_out
    first, normed_one, rstd_one = norm_forward(
        hidden.astype(F32) + branch, whole_gain_one, whole_shift_one
    )
    first_low = first.astype(BF)
    inner = jnp.dot(first_low, whole_up, preferred_element_type=F32) + whole_bias_up
    activated = jax.nn.gelu(inner, approximate=False).astype(BF)
    second = jnp.dot(activated, whole_down, preferred_element_type=F32) + whole_bias_down
    result, normed_two, rstd_two = norm_forward(first + second, whole_gain_two, whole_shift_two)
    output = result * present
    upstream = cotangent.astype(F32) * present
    grad_second, grad_gain_two, grad_shift_two = norm_backward(
        upstream, normed_two, rstd_two, whole_gain_two
    )
    grad_branch_two = grad_second.astype(BF)
    grad_w_down = jnp.einsum("rf,rd->fd", activated, grad_branch_two, preferred_element_type=F32)
    grad_bias_down = jnp.sum(grad_branch_two.astype(F32), axis=0)
    grad_activated = jnp.einsum(
        "rd,fd->rf", grad_branch_two, whole_down, preferred_element_type=F32
    )
    grad_inner = (grad_activated * gelu_slope(inner)).astype(BF)
    grad_w_up = jnp.einsum("rd,rf->df", first_low, grad_inner, preferred_element_type=F32)
    grad_bias_up = jnp.sum(grad_inner.astype(F32), axis=0)
    grad_first = grad_second + jnp.einsum(
        "rf,df->rd", grad_inner, whole_up, preferred_element_type=F32
    )
    grad_sum_one, grad_gain_one, grad_shift_one = norm_backward(
        grad_first, normed_one, rstd_one, whole_gain_one
    )
    grad_branch_one = grad_sum_one.astype(BF)
    grad_w_out = jnp.einsum("rd,re->de", mixed, grad_branch_one, preferred_element_type=F32)
    grad_bias_out = jnp.sum(grad_branch_one.astype(F32), axis=0)
    grad_mixed = jnp.einsum(
        "re,de->rd", grad_branch_one, whole_out, preferred_element_type=F32
    ).astype(BF)
    grads_packed = jnp.concatenate(
        [
            grad_w_out.astype(BF).reshape(n, part, width),
            grad_w_up.astype(BF)
            .reshape(n, part, wide, width)
            .transpose(0, 2, 1, 3)
            .reshape(n, wide * part, width),
            grad_w_down.astype(BF).reshape(n, inner_part, width),
        ],
        axis=1,
    )
    summed = lax.psum_scatter(
        grads_packed.reshape(-1, width), "fsdp", scatter_dimension=0, tiled=True
    ).astype(F32)
    my_out = summed[:part]
    my_up = (
        summed[part : part * (1 + wide)]
        .reshape(wide, part, width)
        .transpose(1, 0, 2)
        .reshape(part, hidden_units)
    )
    my_down = summed[part * (1 + wide) :]

    grad_stack = jnp.concatenate(
        attention_backward(bounds, stacked, mixed, grad_mixed, logsum), axis=1
    )
    grad_w_qkv = jnp.einsum("rd,re->de", hidden, grad_stack, preferred_element_type=F32)
    stack_sums = jnp.sum(grad_stack.astype(F32), axis=0)
    grad_hidden = grad_sum_one + jnp.einsum(
        "re,de->rd", grad_stack, whole_qkv, preferred_element_type=F32
    )
    vector_grads = jnp.concatenate(
        [
            grad.reshape(n, -1)
            for grad in (
                stack_sums[:width],
                stack_sums[2 * width :],
                grad_bias_out,
                grad_gain_one,
                grad_shift_one,
                grad_bias_up,
                grad_bias_down,
                grad_gain_two,
                grad_shift_two,
            )
        ],
        axis=1,
    )
    my_qkv = lax.psum_scatter(
        grad_w_qkv.astype(BF), "fsdp", scatter_dimension=0, tiled=True
    ).astype(F32)
    every_vector = lax.psum(vector_grads, "fsdp")
    my_vectors = lax.dynamic_index_in_dim(every_vector, lax.axis_index("fsdp"), 0, keepdims=False)
    (my_bias_q, my_bias_v, my_bias_out, my_gain_one, my_shift_one, my_bias_up, my_bias_down, my_gain_two, my_shift_two) = (
        my_vectors[start : start + size] for start, size in zip(starts, sizes)
    )
    return (
        output,
        grad_hidden,
        my_qkv,
        my_bias_q,
        my_bias_v,
        my_out,
        my_bias_out,
        my_gain_one,
        my_shift_one,
        my_up,
        my_bias_up,
        my_down,
        my_bias_down,
        my_gain_two,
        my_shift_two,
    )


def solution(mesh):
    rows = P("fsdp", None)
    flat = P("fsdp")
    weights = (rows, flat, flat, rows, flat, flat, flat, rows, flat, rows, flat, flat, flat)
    return jax.shard_map(
        on_device,
        mesh=mesh,
        in_specs=(rows, flat) + weights + (rows,),
        out_specs=(rows, rows) + weights,
        check_vma=False,
    )
```

```python
import functools
import math

import jax
import jax.numpy as jnp
from jax import lax
from jax.experimental import pallas as pl
from jax.experimental.pallas import tpu as pltpu
from jax.sharding import PartitionSpec as P

DH = 64
PAIR = 2 * DH
BF = jnp.bfloat16
F32 = jnp.float32
NEG = -1e30
EPSILON = 1e-05
ROOT_HALF = 0.7071067811865476
INV_ROOT_TWO_PI = 0.3989422804014327
LAST_LAST = (((1,), (1,)), ((), ()))
VMEM_BYTES = 56 * 2**20


def norm_forward(values_in, gain, shift):
    centre = jnp.mean(values_in, axis=-1, keepdims=True)
    centered = values_in - centre
    spread = jnp.mean(centered * centered, axis=-1, keepdims=True)
    rstd_rows = lax.rsqrt(spread + EPSILON)
    normed = centered * rstd_rows
    return (normed * gain + shift, normed, rstd_rows)


def norm_backward(upstream, normed, rstd_rows, gain):
    scaled = upstream * gain
    plain_mean = jnp.mean(scaled, axis=-1, keepdims=True)
    cross_mean = jnp.mean(scaled * normed, axis=-1, keepdims=True)
    grad_in = rstd_rows * (scaled - plain_mean - normed * cross_mean)
    return (grad_in, jnp.sum(upstream * normed, axis=0), jnp.sum(upstream, axis=0))


def gelu_slope(inner):
    normal_cdf = 0.5 * (1.0 + lax.erf(inner * ROOT_HALF))
    return normal_cdf + inner * jnp.exp(-0.5 * inner * inner) * INV_ROOT_TWO_PI


def dot_last(a, b):
    return lax.dot_general(a, b, LAST_LAST, preferred_element_type=F32)


def dot(a, b):
    return jnp.dot(a, b, preferred_element_type=F32)


def segment_at(position, bounds_ref):
    segment = jnp.zeros(position.shape, jnp.int32)
    for index in range(bounds_ref.shape[0]):
        segment += (position >= bounds_ref[index]).astype(jnp.int32)
    return segment


def attention_forward_kernel(bounds_ref, q_ref, k_ref, v_ref, mixed_ref, logsum_ref, *, span, scale):
    rows = q_ref.shape[0]
    first_head = lax.broadcasted_iota(jnp.int32, (1, PAIR), 1) < DH
    key_segment = segment_at(lax.broadcasted_iota(jnp.int32, (1, rows), 1), bounds_ref)
    keys = k_ref[...]
    values = v_ref[...]
    for block in range(rows // span):
        here = pl.ds(block * span, span)
        queries = q_ref[here, :] * jnp.asarray(scale, BF)
        row = lax.broadcasted_iota(jnp.int32, (span, 1), 0) + block * span
        same = segment_at(row, bounds_ref) == key_segment
        mixed = []
        logsum = []
        for head in range(2):
            mine = first_head if head == 0 else jnp.logical_not(first_head)
            scores = dot_last(jnp.where(mine, queries, jnp.zeros_like(queries)), keys)
            scores = jnp.where(same, scores, NEG)
            highest = jnp.max(scores, axis=1, keepdims=True)
            exps = jnp.exp(scores - highest)
            total = jnp.sum(exps, axis=1, keepdims=True)
            mixed.append(dot(exps.astype(BF), values) * (1.0 / total))
            logsum.append(highest + jnp.log(total))
        mixed_ref[here, :] = jnp.where(first_head, mixed[0], mixed[1]).astype(BF)
        turned = jnp.transpose(jnp.where(first_head, logsum[0], logsum[1]))
        logsum_ref[0, 0:1, here] = turned[0:1]
        logsum_ref[0, 1:2, here] = turned[DH : DH + 1]


def pair_spec(rows, offset):
    return pl.BlockSpec((rows, PAIR), lambda pair, bounds: (0, offset + pair))


def attention_forward(bounds, stacked, span=512):
    rows, width = stacked.shape[0], stacked.shape[1] // 3
    pairs = width // PAIR
    return pl.pallas_call(
        functools.partial(attention_forward_kernel, span=span, scale=1.0 / math.sqrt(DH)),
        grid_spec=pltpu.PrefetchScalarGridSpec(
            num_scalar_prefetch=1,
            grid=(pairs,),
            in_specs=[pair_spec(rows, 0), pair_spec(rows, pairs), pair_spec(rows, 2 * pairs)],
            out_specs=[
                pair_spec(rows, 0),
                pl.BlockSpec((1, 8, rows), lambda pair, bounds: (pair, 0, 0)),
            ],
        ),
        out_shape=[
            jax.ShapeDtypeStruct((rows, width), BF),
            jax.ShapeDtypeStruct((pairs, 8, rows), F32),
        ],
        compiler_params=pltpu.CompilerParams(vmem_limit_bytes=VMEM_BYTES),
        cost_estimate=pl.CostEstimate(
            flops=4 * rows * rows * width * 4, bytes_accessed=8 * rows * width, transcendentals=0
        ),
        name="attention_forward",
    )(bounds, stacked, stacked, stacked)


def attention_backward_kernel(
    bounds_ref, q_ref, k_ref, v_ref, mixed_ref, grad_ref, logsum_ref, dq_ref, dk_ref, dv_ref, dk_sum, dv_sum, *, span, scale
):
    rows = q_ref.shape[0]
    first_head = lax.broadcasted_iota(jnp.int32, (1, PAIR), 1) < DH
    key_segment = segment_at(lax.broadcasted_iota(jnp.int32, (rows, 1), 0), bounds_ref)
    keys = k_ref[...]
    values = v_ref[...]
    keys_turned = jnp.transpose(keys)
    picks = (
        lax.broadcasted_iota(jnp.int32, (8, PAIR), 1) // DH
        == lax.broadcasted_iota(jnp.int32, (8, PAIR), 0)
    ).astype(F32)
    for block in range(rows // span):
        here = pl.ds(block * span, span)
        queries = q_ref[here, :]
        grads = grad_ref[here, :]
        weighted = lax.dot_general(
            picks,
            grads.astype(F32) * mixed_ref[here, :].astype(F32),
            LAST_LAST,
            preferred_element_type=F32,
            precision=lax.Precision.HIGHEST,
        )
        column = lax.broadcasted_iota(jnp.int32, (1, span), 1) + block * span
        same = key_segment == segment_at(column, bounds_ref)
        all_probs, all_scores, all_grads, all_queries, grad_queries = [], [], [], [], []
        for head in range(2):
            mine = first_head if head == 0 else jnp.logical_not(first_head)
            my_queries = jnp.where(mine, queries, jnp.zeros_like(queries)) * jnp.asarray(scale, BF)
            my_grads = jnp.where(mine, grads, jnp.zeros_like(grads))
            scores = dot_last(keys, my_queries) - logsum_ref[0, head : head + 1, here]
            probs = jnp.exp(jnp.where(same, scores, NEG))
            grad_probs = dot_last(values, my_grads)
            grad_scores = (probs * (grad_probs - weighted[head : head + 1])).astype(BF)
            all_probs.append(probs.astype(BF))
            all_scores.append(grad_scores)
            all_grads.append(my_grads)
            all_queries.append(my_queries)
            grad_queries.append(dot(keys_turned[DH * head : DH * (head + 1)], grad_scores))
        turned = jnp.concatenate(grad_queries, axis=0) * scale
        dq_ref[here, :] = jnp.transpose(turned).astype(BF)
        dv = dot(jnp.concatenate(all_probs, axis=1), jnp.concatenate(all_grads, axis=0))
        dk = dot(jnp.concatenate(all_scores, axis=1), jnp.concatenate(all_queries, axis=0))
        if block == 0:
            dv_sum[...] = dv
            dk_sum[...] = dk
        else:
            dv_sum[...] += dv
            dk_sum[...] += dk
    dk_ref[...] = dk_sum[...].astype(BF)
    dv_ref[...] = dv_sum[...].astype(BF)


def attention_backward(bounds, stacked, mixed, grad_mixed, logsum, start=0, count=None, span=256):
    rows, width = mixed.shape
    pairs = width // PAIR
    count = pairs if count is None else count
    return pl.pallas_call(
        functools.partial(attention_backward_kernel, span=span, scale=1.0 / math.sqrt(DH)),
        grid_spec=pltpu.PrefetchScalarGridSpec(
            num_scalar_prefetch=1,
            grid=(count,),
            in_specs=[
                pair_spec(rows, start),
                pair_spec(rows, pairs + start),
                pair_spec(rows, 2 * pairs + start),
                pair_spec(rows, start),
                pair_spec(rows, start),
                pl.BlockSpec((1, 8, rows), lambda pair, bounds: (start + pair, 0, 0)),
            ],
            out_specs=[pair_spec(rows, 0), pair_spec(rows, 0), pair_spec(rows, 0)],
            scratch_shapes=[pltpu.VMEM((rows, PAIR), F32), pltpu.VMEM((rows, PAIR), F32)],
        ),
        out_shape=[jax.ShapeDtypeStruct((rows, count * PAIR), BF)] * 3,
        compiler_params=pltpu.CompilerParams(vmem_limit_bytes=VMEM_BYTES),
        cost_estimate=pl.CostEstimate(
            flops=40 * rows * rows * count * PAIR, bytes_accessed=16 * rows * count * PAIR, transcendentals=0
        ),
        name="attention_backward",
    )(bounds, stacked, stacked, stacked, mixed, grad_mixed, logsum)


def general_layer(
    hidden,
    lengths,
    w_qkv,
    bias_q,
    bias_v,
    w_out,
    bias_out,
    norm1_gain,
    norm1_bias,
    w_up,
    bias_up,
    w_down,
    bias_down,
    norm2_gain,
    norm2_bias,
    cotangent,
):
    count_rows, width = hidden.shape
    hidden_units = w_up.shape[1]
    n = lax.axis_size("fsdp")
    part = width // n
    inner_part = hidden_units // n
    wide = hidden_units // width
    bounds = jnp.cumsum(lengths)
    present = (jnp.arange(count_rows, dtype=jnp.int32) < bounds[-1]).astype(F32)[:, None]

    vectors = (bias_q, bias_v, bias_out, norm1_gain, norm1_bias, bias_up, bias_down, norm2_gain, norm2_bias)
    sizes = [vector.shape[0] for vector in vectors]
    starts = [sum(sizes[:i]) for i in range(len(sizes))]
    whole_qkv = lax.all_gather(w_qkv, "fsdp", axis=0, tiled=True)
    whole_vectors = lax.all_gather(jnp.concatenate(vectors)[None], "fsdp", axis=0, tiled=True)
    (
        whole_bias_q,
        whole_bias_v,
        whole_bias_out,
        whole_gain_one,
        whole_shift_one,
        whole_bias_up,
        whole_bias_down,
        whole_gain_two,
        whole_shift_two,
    ) = (
        whole_vectors[:, start : start + size].reshape(n * size).astype(F32)
        for start, size in zip(starts, sizes)
    )
    packed = jnp.concatenate(
        [w_out]
        + [w_up[:, width * i : width * (i + 1)] for i in range(wide)]
        + [w_down],
        axis=0,
    )
    gathered = lax.all_gather(packed, "fsdp", axis=0, tiled=True).reshape(n, -1, width)
    whole_out = gathered[:, :part].reshape(width, width)
    whole_up = (
        gathered[:, part : part * (1 + wide)]
        .reshape(n, wide, part, width)
        .transpose(0, 2, 1, 3)
        .reshape(width, hidden_units)
    )
    whole_down = gathered[:, part * (1 + wide) :].reshape(hidden_units, width)

    projected = jnp.dot(hidden, whole_qkv, preferred_element_type=F32)
    whole_bias = jnp.concatenate([whole_bias_q, jnp.zeros_like(whole_bias_q), whole_bias_v])
    stacked = (projected + whole_bias).astype(BF)
    mixed, logsum = attention_forward(bounds, stacked)
    branch = jnp.dot(mixed, whole_out, preferred_element_type=F32) + whole_bias_out
    first, normed_one, rstd_one = norm_forward(
        hidden.astype(F32) + branch, whole_gain_one, whole_shift_one
    )
    first_low = first.astype(BF)
    inner = jnp.dot(first_low, whole_up, preferred_element_type=F32) + whole_bias_up
    activated = jax.nn.gelu(inner, approximate=False).astype(BF)
    second = jnp.dot(activated, whole_down, preferred_element_type=F32) + whole_bias_down
    result, normed_two, rstd_two = norm_forward(first + second, whole_gain_two, whole_shift_two)
    output = result * present
    upstream = cotangent.astype(F32) * present
    grad_second, grad_gain_two, grad_shift_two = norm_backward(
        upstream, normed_two, rstd_two, whole_gain_two
    )
    grad_branch_two = grad_second.astype(BF)
    grad_w_down = jnp.einsum("rf,rd->fd", activated, grad_branch_two, preferred_element_type=F32)
    grad_bias_down = jnp.sum(grad_branch_two.astype(F32), axis=0)
    grad_activated = jnp.einsum(
        "rd,fd->rf", grad_branch_two, whole_down, preferred_element_type=F32
    )
    grad_inner = (grad_activated * gelu_slope(inner)).astype(BF)
    grad_w_up = jnp.einsum("rd,rf->df", first_low, grad_inner, preferred_element_type=F32)
    grad_bias_up = jnp.sum(grad_inner.astype(F32), axis=0)
    grad_first = grad_second + jnp.einsum(
        "rf,df->rd", grad_inner, whole_up, preferred_element_type=F32
    )
    grad_sum_one, grad_gain_one, grad_shift_one = norm_backward(
        grad_first, normed_one, rstd_one, whole_gain_one
    )
    grad_branch_one = grad_sum_one.astype(BF)
    grad_w_out = jnp.einsum("rd,re->de", mixed, grad_branch_one, preferred_element_type=F32)
    grad_bias_out = jnp.sum(grad_branch_one.astype(F32), axis=0)
    grad_mixed = jnp.einsum(
        "re,de->rd", grad_branch_one, whole_out, preferred_element_type=F32
    ).astype(BF)
    grads_packed = jnp.concatenate(
        [
            grad_w_out.astype(BF).reshape(n, part, width),
            grad_w_up.astype(BF)
            .reshape(n, part, wide, width)
            .transpose(0, 2, 1, 3)
            .reshape(n, wide * part, width),
            grad_w_down.astype(BF).reshape(n, inner_part, width),
        ],
        axis=1,
    )
    summed = lax.psum_scatter(
        grads_packed.reshape(-1, width), "fsdp", scatter_dimension=0, tiled=True
    ).astype(F32)
    my_out = summed[:part]
    my_up = (
        summed[part : part * (1 + wide)]
        .reshape(wide, part, width)
        .transpose(1, 0, 2)
        .reshape(part, hidden_units)
    )
    my_down = summed[part * (1 + wide) :]

    grad_stack = jnp.concatenate(
        attention_backward(bounds, stacked, mixed, grad_mixed, logsum), axis=1
    )
    grad_w_qkv = jnp.einsum("rd,re->de", hidden, grad_stack, preferred_element_type=F32)
    stack_sums = jnp.sum(grad_stack.astype(F32), axis=0)
    grad_hidden = grad_sum_one + jnp.einsum(
        "re,de->rd", grad_stack, whole_qkv, preferred_element_type=F32
    )
    vector_grads = jnp.concatenate(
        [
            grad.reshape(n, -1)
            for grad in (
                stack_sums[:width],
                stack_sums[2 * width :],
                grad_bias_out,
                grad_gain_one,
                grad_shift_one,
                grad_bias_up,
                grad_bias_down,
                grad_gain_two,
                grad_shift_two,
            )
        ],
        axis=1,
    )
    my_qkv = lax.psum_scatter(
        grad_w_qkv.astype(BF), "fsdp", scatter_dimension=0, tiled=True
    ).astype(F32)
    every_vector = lax.psum(vector_grads, "fsdp")
    my_vectors = lax.dynamic_index_in_dim(every_vector, lax.axis_index("fsdp"), 0, keepdims=False)
    (my_bias_q, my_bias_v, my_bias_out, my_gain_one, my_shift_one, my_bias_up, my_bias_down, my_gain_two, my_shift_two) = (
        my_vectors[start : start + size] for start, size in zip(starts, sizes)
    )
    return (
        output,
        grad_hidden,
        my_qkv,
        my_bias_q,
        my_bias_v,
        my_out,
        my_bias_out,
        my_gain_one,
        my_shift_one,
        my_up,
        my_bias_up,
        my_down,
        my_bias_down,
        my_gain_two,
        my_shift_two,
    )


CHIPS = (4, 2, 2, 2)


def coordinates(index):
    _, ys, xs, cores = CHIPS
    return (index // (cores * xs * ys), index // (cores * xs) % ys, index // cores % xs, index % cores)


def moved(array, step):
    sizes = CHIPS
    pairs = []
    for source in range(math.prod(sizes)):
        target = 0
        for place, by, size in zip(coordinates(source), step, sizes):
            target = target * size + (place + by) % size
        pairs.append((source, target))
    return lax.ppermute(array, "fsdp", pairs)


def pack_weights_kernel(down_ref, up_ref, out_ref, packed_ref):
    width = down_ref.shape[1]
    wide = up_ref.shape[1] // width
    parts = [down_ref[...]] + [up_ref[:, width * i : width * (i + 1)] for i in range(wide)]
    parts = [part.astype(F32) for part in parts + [out_ref[...]]]
    fill = packed_ref.shape[0] - sum(part.shape[0] for part in parts)
    parts.append(jnp.zeros((fill, width), F32))
    packed_ref[...] = jnp.concatenate(parts, axis=0).astype(BF)


def pack_weights(w_down, w_up, w_out):
    rows = w_down.shape[0] + w_up.size // w_out.shape[1] + w_out.shape[0]
    return pl.pallas_call(
        pack_weights_kernel,
        out_shape=jax.ShapeDtypeStruct((rows + -rows % 16, w_out.shape[1]), BF),
        name="pack_weights",
    )(w_down, w_up, w_out)


def pack_front_kernel(qkv_ref, vector_ref, up_ref, packed_ref):
    width = packed_ref.shape[1]
    parts = [qkv_ref[:, width * i : width * (i + 1)].astype(F32) for i in range(3)]
    extra = jnp.zeros((8, width), F32)
    lanes = lax.broadcasted_iota(jnp.int32, (8, PAIR), 1)
    rows = lax.broadcasted_iota(jnp.int32, (8, PAIR), 0)
    part, inner_part = vector_ref.shape[1], up_ref.shape[1]
    vectors = jnp.concatenate(
        [vector_ref[...].astype(F32), jnp.zeros((8, PAIR - part), F32)], axis=1
    )
    long = jnp.concatenate([up_ref[...].astype(F32), jnp.zeros((1, PAIR - inner_part), F32)], axis=1)
    long = jnp.where((rows == 0) & (lanes < inner_part), long, 0.0)
    extra = jnp.concatenate([vectors, long, extra[:, 2 * PAIR :]], axis=1)
    packed_ref[...] = jnp.concatenate(parts + [extra], axis=0).astype(BF)


def pack_front(w_qkv, vectors, bias_up):
    part, width = w_qkv.shape[0], w_qkv.shape[1] // 3
    return pl.pallas_call(
        pack_front_kernel,
        out_shape=jax.ShapeDtypeStruct((3 * part + 8, width), BF),
        name="pack_front",
    )(w_qkv, vectors, bias_up)


def gather_pieces(packed):
    column = jnp.stack([packed] + [moved(packed, (step, 0, 0, 0)) for step in range(1, CHIPS[0])])
    pieces = [column] + [moved(column, step) for step in ((0, 0, 1, 0), (0, 1, 0, 0), (0, 1, 1, 0))]
    return pieces, [moved(piece, (0, 0, 0, 1)) for piece in pieces]


NEAR = ((0, 0, 1, 0), (0, 1, 0, 0), (0, 1, 1, 0))


def near_sum_kernel(place_ref, *refs, cuts):
    pairs = [(refs[2 * i], refs[2 * i + 1]) for i in range(len(cuts))]
    outs = refs[2 * len(cuts) :]
    ys, xs = CHIPS[1:3]
    for out_ref, (_, step_y, step_x, _) in zip(outs, ((0, 0, 0, 0),) + NEAR):
        chip = (place_ref[1] + step_y) % ys * xs + (place_ref[2] + step_x) % xs
        for (keep_ref, came_ref), (start, size) in zip(pairs, cuts):
            total = keep_ref[chip].astype(F32) + came_ref[chip].astype(F32)
            out_ref[0, start : start + size, :] = total.astype(BF)


def near_sum(place, *pairs):
    zs, ys, xs, _ = CHIPS
    near = ys * xs
    sizes = [keep.shape[1] for keep, _ in pairs]
    cuts = [(sum(sizes[:i]), size) for i, size in enumerate(sizes)]
    width = pairs[0][0].shape[2]
    out = jax.ShapeDtypeStruct((zs, sum(sizes), width), BF)
    return pl.pallas_call(
        functools.partial(near_sum_kernel, cuts=cuts),
        grid_spec=pltpu.PrefetchScalarGridSpec(
            num_scalar_prefetch=1,
            grid=(zs,),
            in_specs=[
                pl.BlockSpec((near, size, width), lambda step, place: (step, 0, 0))
                for size in sizes
                for _ in range(2)
            ],
            out_specs=[pl.BlockSpec((1, sum(sizes), width), lambda step, place: (step, 0, 0))] * 4,
        ),
        out_shape=[out] * 4,
        compiler_params=params(48),
        cost_estimate=pl.CostEstimate(
            flops=out.size, bytes_accessed=out.size, transcendentals=0
        ),
        name="near_sum",
    )(place, *(array for pair in pairs for array in pair))


def send_near(sends):
    return [moved(array, step) for array, step in zip(sends, NEAR)]


def far_sum(parts):
    zs, ys, xs, cores = CHIPS
    across = ys * xs * cores
    groups = [[level * across + i for level in range(zs)] for i in range(across)]
    total = sum(part.astype(F32) for part in parts).astype(BF)
    return lax.psum_scatter(
        total, "fsdp", scatter_dimension=0, axis_index_groups=groups, tiled=False
    ).astype(F32)


def reduce_far(parts, place):
    z, zs = place[0], CHIPS[0]

    def at(level):
        return sum(
            lax.dynamic_index_in_dim(part, level, 0, keepdims=False).astype(F32) for part in parts
        )

    return at(z), [at((z + step) % zs).astype(BF) for step in range(1, zs)]


def send_far(sends):
    return [moved(array, (step, 0, 0, 0)) for step, array in enumerate(sends, 1)]


def total_of(mine, came):
    return mine + sum(array.astype(F32) for array in came)


def after(value, *first):
    return lax.optimization_barrier((value, *first))[0]


def params(megabytes):
    return pltpu.CompilerParams(vmem_limit_bytes=megabytes * 2**20)


def whole_block(array):
    return pl.BlockSpec(array.shape, lambda *step: (0,) * array.ndim)


def project_kernel(
    place_ref, hidden_ref, *refs, part, inner_part
):
    pieces = refs[: len(refs) - 4]
    stacked_ref, weight_ref, vector_ref, up_ref = refs[len(refs) - 4 :]
    z, y, x, core = (place_ref[i] for i in range(4))
    zs, ys, xs, cores = CHIPS
    width = hidden_ref.shape[1]
    lanes = lax.broadcasted_iota(jnp.int32, (8, width), 1)
    up_lanes = lax.broadcasted_iota(jnp.int32, (8, up_ref.shape[1]), 1)
    vectors = jnp.zeros((8, width), F32)
    ups = jnp.zeros(up_ref.shape, F32)
    steps = ((0, 0), (0, 1), (1, 0), (1, 1))
    for kind, (step_y, step_x) in enumerate(steps):
        for step_z in range(zs):
            chip = ((z + zs - step_z) % zs * ys + (y + step_y) % ys) * xs + (x + step_x) % xs
            mine = pieces[kind][step_z].astype(F32)
            other = pieces[len(steps) + kind][step_z].astype(F32)
            low = jnp.where(core == 0, mine, other)
            high = jnp.where(core == 0, other, mine)
            rows = pl.ds(pl.multiple_of(chip * (cores * part), cores * part), cores * part)
            for third in range(3):
                cut = slice(third * part, (third + 1) * part)
                weight_ref[rows, third * width : (third + 1) * width] = jnp.concatenate(
                    [low[cut], high[cut]], axis=0
                ).astype(BF)
            for owner, piece in ((chip * cores, low), (chip * cores + 1, high)):
                extra = piece[3 * part :]
                vectors += pltpu.roll(jnp.where(lanes < part, extra, 0.0), owner * part, 1)
                long = jnp.concatenate(
                    [extra[:, PAIR:]] + [jnp.zeros((8, up_ref.shape[1] - width + PAIR), F32)], axis=1
                )
                ups += pltpu.roll(jnp.where(up_lanes < inner_part, long, 0.0), owner * inner_part, 1)
    vector_ref[...] = vectors
    up_ref[...] = ups
    hidden = hidden_ref[...]
    for third, bias in ((0, vectors[0:1]), (1, None), (2, vectors[1:2])):
        cut = slice(third * width, (third + 1) * width)
        projected = dot(hidden, weight_ref[:, cut])
        stacked_ref[:, cut] = (projected if bias is None else projected + bias).astype(BF)


def project(place, hidden, pieces, hidden_units, count):
    rows, width = hidden.shape
    outs = [
        jax.ShapeDtypeStruct((rows, 3 * width), BF),
        jax.ShapeDtypeStruct((width, 3 * width), BF),
        jax.ShapeDtypeStruct((8, width), F32),
        jax.ShapeDtypeStruct((8, hidden_units), F32),
    ]
    return pl.pallas_call(
        functools.partial(project_kernel, part=width // count, inner_part=hidden_units // count),
        grid_spec=pltpu.PrefetchScalarGridSpec(
            num_scalar_prefetch=1,
            grid=(1,),
            in_specs=[whole_block(hidden)] + [whole_block(piece) for piece in pieces],
            out_specs=[whole_block(out) for out in outs],
        ),
        out_shape=outs,
        compiler_params=params(48),
        name="project",
    )(place, hidden, *pieces)


def gelu_and_slope(inner):
    near = 1.0 / (1.0 + (0.3275911 * ROOT_HALF) * jnp.abs(inner))
    bell = jnp.exp(-0.5 * inner * inner)
    series = 0.7107068705 + near * (-0.7265760135 + near * 0.5307027145)
    series = near * (0.127414796 + near * (-0.142248368 + near * series))
    tail = series * bell
    normal_cdf = jnp.where(inner >= 0, 1.0 - tail, tail)
    return inner * normal_cdf, normal_cdf + inner * bell * INV_ROOT_TWO_PI


def norm_back(upstream, normed, rstd_rows, gain):
    scaled = upstream * gain
    plain_mean = jnp.mean(scaled, axis=-1, keepdims=True)
    cross_mean = jnp.mean(scaled * normed, axis=-1, keepdims=True)
    return rstd_rows * (scaled - plain_mean - normed * cross_mean)


def column_sum(values):
    return jnp.sum(values, axis=0, keepdims=True)


def row_pass_kernel(
    bounds_ref, mixed_ref, hidden_ref, cotangent_ref, vector_ref, bias_up_ref, gathered_ref,
    output_ref, first_turned_ref, mixed_turned_ref, activated_turned_ref, grad_second_ref,
    grad_inner_ref, grad_sum_ref, grad_branch_ref, grad_mixed_ref, sums_ref, up_sums_ref,
    w_out, w_up, w_down, staged, slope, sems, *, part, chunk
):
    step = pl.program_id(0)
    span, width = mixed_ref.shape
    count, inner_part = w_down.shape[0], w_down.shape[1]
    hidden_units = w_up.shape[1]
    wide = hidden_units // width

    @pl.when(step == 0)
    def _():
        narrow = pltpu.make_async_copy(
            gathered_ref.at[:, pl.ds(inner_part, staged.shape[1]), :], staged, sems.at[0]
        )
        down = pltpu.make_async_copy(
            gathered_ref.at[:, pl.ds(0, inner_part), :], w_down, sems.at[1]
        )
        narrow.start()
        down.start()
        narrow.wait()
        for pair in range(count // 2):
            low = staged[2 * pair].astype(F32)
            high = staged[2 * pair + 1].astype(F32)
            rows = slice(2 * pair * part, 2 * (pair + 1) * part)
            for group in range(wide + 1):
                cut = slice(group * part, (group + 1) * part)
                both = jnp.concatenate([low[cut], high[cut]], axis=0).astype(BF)
                if group < wide:
                    w_up[rows, group * width : (group + 1) * width] = both
                else:
                    w_out[rows, :] = both
        down.wait()

    def down_rows(cut):
        owners = slice(cut.start // inner_part, cut.stop // inner_part)
        return w_down[owners].reshape(cut.stop - cut.start, width)

    bias_out, gain_one, shift_one, bias_down, gain_two, shift_two = (
        vector_ref[i : i + 1, :] for i in range(2, 8)
    )
    mixed = mixed_ref[...]
    branch = dot(mixed, w_out[...]) + bias_out
    first, normed_one, rstd_one = norm_forward(
        hidden_ref[...].astype(F32) + branch, gain_one, shift_one
    )
    first_low = first.astype(BF)
    first_turned_ref[...] = jnp.transpose(first_low)
    mixed_turned_ref[...] = jnp.transpose(mixed)
    cuts = [slice(start, start + chunk) for start in range(0, hidden_units, chunk)]
    second = jnp.zeros(first.shape, F32)
    for cut in cuts:
        inner = dot(first_low, w_up[:, cut]) + bias_up_ref[0:1, cut]
        activated, slopes = gelu_and_slope(inner)
        activated = activated.astype(BF)
        slope[:, cut] = slopes
        activated_turned_ref[cut, :] = jnp.transpose(activated)
        second += dot(activated, down_rows(cut))
    result, normed_two, rstd_two = norm_forward(
        first + (second + bias_down), gain_two, shift_two
    )
    row = lax.broadcasted_iota(jnp.int32, (span, 1), 0) + step * span
    present = (row < bounds_ref[bounds_ref.shape[0] - 1]).astype(F32)
    output_ref[...] = result * present
    upstream = cotangent_ref[...].astype(F32) * present
    grad_second = norm_back(upstream, normed_two, rstd_two, gain_two)
    grad_second_low = grad_second.astype(BF)
    grad_second_ref[...] = grad_second_low
    grad_first = grad_second
    up_sums = []
    for cut in cuts:
        grad_activated = dot_last(grad_second_low, down_rows(cut))
        grad_inner = (grad_activated * slope[:, cut]).astype(BF)
        grad_inner_ref[:, cut] = grad_inner
        up_sums.append(column_sum(grad_inner.astype(F32)))
        grad_first += dot_last(grad_inner, w_up[:, cut])
    grad_sum = norm_back(grad_first, normed_one, rstd_one, gain_one)
    grad_sum_ref[...] = grad_sum
    grad_branch = grad_sum.astype(BF)
    grad_branch_ref[...] = grad_branch
    grad_mixed_ref[...] = dot_last(grad_branch, w_out[...]).astype(BF)
    sums = jnp.concatenate(
        [
            column_sum(grad_branch.astype(F32)),
            column_sum(grad_first * normed_one),
            column_sum(grad_first),
            column_sum(grad_second_low.astype(F32)),
            column_sum(upstream * normed_two),
            column_sum(upstream),
            jnp.zeros((2, width), F32),
        ],
        axis=0,
    )
    up_sums = jnp.concatenate(
        [jnp.concatenate(up_sums, axis=1), jnp.zeros((7, hidden_units), F32)], axis=0
    )

    @pl.when(step == 0)
    def _():
        sums_ref[...] = sums
        up_sums_ref[...] = up_sums

    @pl.when(step > 0)
    def _():
        sums_ref[...] += sums
        up_sums_ref[...] += up_sums


def row_pass(bounds, mixed, hidden, cotangent, vectors, bias_up, gathered, inner_part, span=256, chunk=768):
    rows, width = mixed.shape
    hidden_units = bias_up.shape[1]
    count = gathered.shape[0]
    part = width // count
    row_spec = pl.BlockSpec((span, width), lambda step, bounds: (step, 0))
    turned_spec = pl.BlockSpec((width, span), lambda step, bounds: (0, step))
    shape = jax.ShapeDtypeStruct
    sums = shape((8, width), F32)
    up_sums = shape((8, hidden_units), F32)
    staged_rows = gathered.shape[1] - inner_part
    return pl.pallas_call(
        functools.partial(row_pass_kernel, part=part, chunk=chunk),
        grid_spec=pltpu.PrefetchScalarGridSpec(
            num_scalar_prefetch=1,
            grid=(rows // span,),
            in_specs=[
                row_spec,
                row_spec,
                row_spec,
                whole_block(vectors),
                whole_block(bias_up),
                pl.BlockSpec(memory_space=pl.ANY),
            ],
            out_specs=[
                row_spec,
                turned_spec,
                turned_spec,
                pl.BlockSpec((hidden_units, span), lambda step, bounds: (0, step)),
                row_spec,
                pl.BlockSpec((span, hidden_units), lambda step, bounds: (step, 0)),
                row_spec,
                row_spec,
                row_spec,
                whole_block(sums),
                whole_block(up_sums),
            ],
            scratch_shapes=[
                pltpu.VMEM((width, width), BF),
                pltpu.VMEM((width, hidden_units), BF),
                pltpu.VMEM((count, inner_part, width), BF),
                pltpu.VMEM((count, staged_rows, width), BF),
                pltpu.VMEM((span, hidden_units), F32),
                pltpu.SemaphoreType.DMA((2,)),
            ],
        ),
        out_shape=[
            shape((rows, width), F32),
            shape((width, rows), BF),
            shape((width, rows), BF),
            shape((hidden_units, rows), BF),
            shape((rows, width), BF),
            shape((rows, hidden_units), BF),
            shape((rows, width), F32),
            shape((rows, width), BF),
            shape((rows, width), BF),
            sums,
            up_sums,
        ],
        compiler_params=params(60),
        cost_estimate=pl.CostEstimate(
            flops=2 * rows * width * (4 * hidden_units + 2 * width),
            bytes_accessed=40 * rows * width,
            transcendentals=0,
        ),
        name="row_pass",
    )(bounds, mixed, hidden, cotangent, vectors, bias_up, gathered)


def split_owners(place_ref, keep_ref, send_ref, tile_of, count, lead=()):
    for core in range(2):

        @pl.when(place_ref[3] == core)
        def _():
            for owner in range(count):
                target = keep_ref if owner % 2 == core else send_ref
                target[(owner // 2,) + lead] = tile_of(owner).astype(BF)


def down_grad_kernel(place_ref, left_ref, right_ref, keep_ref, send_ref):
    part = keep_ref.shape[1]
    product = dot(left_ref[...], right_ref[...])
    count = product.shape[0] // part
    split_owners(place_ref, keep_ref, send_ref, lambda o: product[o * part : (o + 1) * part], count)


def down_grad(place, left, right, count, steps=4):
    tall, rows = left.shape
    width = right.shape[1]
    part = tall // count
    half = count // 2
    spec = pl.BlockSpec((half // steps, part, width), lambda step, place: (step, 0, 0))
    return pl.pallas_call(
        down_grad_kernel,
        grid_spec=pltpu.PrefetchScalarGridSpec(
            num_scalar_prefetch=1,
            grid=(steps,),
            in_specs=[
                pl.BlockSpec((tall // steps, rows), lambda step, place: (step, 0)),
                whole_block(right),
            ],
            out_specs=[spec, spec],
        ),
        out_shape=[jax.ShapeDtypeStruct((half, part, width), BF)] * 2,
        compiler_params=params(48),
        cost_estimate=pl.CostEstimate(
            flops=2 * rows * width * tall, bytes_accessed=4 * tall * rows, transcendentals=0
        ),
        name="grad_w_down",
    )(place, left, right)


def up_grad_kernel(place_ref, first_ref, mixed_ref, inner_ref, branch_ref, keep_ref, send_ref):
    step = pl.program_id(0)
    part = keep_ref.shape[2]

    def go(product):
        count = product.shape[0] // part
        split_owners(
            place_ref, keep_ref, send_ref, lambda o: product[o * part : (o + 1) * part], count, (0,)
        )

    @pl.when(step < pl.num_programs(0) - 1)
    def _():
        go(dot(first_ref[...], inner_ref[...]))

    @pl.when(step == pl.num_programs(0) - 1)
    def _():
        go(dot(mixed_ref[...], branch_ref[...]))


def up_grad(place, first_turned, mixed_turned, grad_inner, grad_branch, count):
    width, rows = first_turned.shape
    wide = grad_inner.shape[1] // width
    half, part = count // 2, width // count
    spec = pl.BlockSpec((half, 1, part, width), lambda step, place: (0, step, 0, 0))
    return pl.pallas_call(
        up_grad_kernel,
        grid_spec=pltpu.PrefetchScalarGridSpec(
            num_scalar_prefetch=1,
            grid=(wide + 1,),
            in_specs=[
                whole_block(first_turned),
                whole_block(mixed_turned),
                pl.BlockSpec((rows, width), lambda step, place: (0, jnp.minimum(step, wide - 1))),
                whole_block(grad_branch),
            ],
            out_specs=[spec, spec],
        ),
        out_shape=[jax.ShapeDtypeStruct((half, wide + 1, part, width), BF)] * 2,
        compiler_params=params(48),
        cost_estimate=pl.CostEstimate(
            flops=2 * rows * width * width * (wide + 1),
            bytes_accessed=4 * rows * width * (wide + 1),
            transcendentals=0,
        ),
        name="grad_w_up_out",
    )(place, first_turned, mixed_turned, grad_inner, grad_branch)


def qkv_grad_kernel(place_ref, hidden_ref, sums_ref, up_sums_ref, *refs, part, inner_part):
    keep_ref, send_ref = refs[-2:]
    stack = refs[:-2]
    each = len(stack) // 3
    rows, width = hidden_ref.shape
    turned = jnp.transpose(hidden_ref[...])
    ones = jnp.ones((8, rows), BF)

    def joined(left, third):
        return jnp.concatenate(
            [dot(left, ref[...]) for ref in stack[third * each : (third + 1) * each]], axis=1
        )

    products = [joined(turned, third) for third in range(3)]
    vectors = jnp.concatenate(
        [joined(ones, 0)[0:1], joined(ones, 2)[0:1], sums_ref[0:6, :]], axis=0
    )
    top = lax.broadcasted_iota(jnp.int32, (8, 1), 0) == 0

    def tile_of(owner):
        cut = slice(owner * part, (owner + 1) * part)
        own = pltpu.roll(vectors, width - owner * part, 1) if owner else vectors
        start = owner * inner_part // PAIR * PAIR
        long = jnp.concatenate(
            [up_sums_ref[:, start : start + PAIR], up_sums_ref[:, start + PAIR : start + 2 * PAIR]]
            if start + 2 * PAIR <= up_sums_ref.shape[1]
            else [up_sums_ref[:, start : start + PAIR]] * 2,
            axis=1,
        )
        shift = owner * inner_part - start
        long = pltpu.roll(long, 2 * PAIR - shift, 1) if shift else long
        extra = jnp.concatenate(
            [own[:, :PAIR], jnp.where(top, long[:, :PAIR], 0.0), jnp.zeros((8, width - 2 * PAIR), F32)],
            axis=1,
        )
        return jnp.concatenate([product[cut] for product in products] + [extra], axis=0)

    split_owners(place_ref, keep_ref, send_ref, tile_of, width // part)


def qkv_grad(place, hidden, stack, sums, up_sums, count):
    rows, width = hidden.shape
    part = width // count
    out = jax.ShapeDtypeStruct((count // 2, 3 * part + 8, width), BF)
    return pl.pallas_call(
        functools.partial(qkv_grad_kernel, part=part, inner_part=up_sums.shape[1] // count),
        grid_spec=pltpu.PrefetchScalarGridSpec(
            num_scalar_prefetch=1,
            grid=(1,),
            in_specs=[whole_block(array) for array in (hidden, sums, up_sums, *stack)],
            out_specs=[whole_block(out)] * 2,
        ),
        out_shape=[out] * 2,
        compiler_params=params(56),
        cost_estimate=pl.CostEstimate(
            flops=6 * rows * width * width, bytes_accessed=12 * rows * width, transcendentals=0
        ),
        name="grad_w_qkv",
    )(place, hidden, sums, up_sums, *stack)


def hidden_grad_kernel(grad_sum_ref, weight_ref, *refs):
    out_ref = refs[-1]
    stack = refs[:-1]
    total = grad_sum_ref[...]
    start = 0
    for ref in stack:
        size = ref.shape[1]
        total += dot_last(ref[...], weight_ref[:, start : start + size])
        start += size
    out_ref[...] = total


def hidden_grad(grad_sum, weight, stack, span=256):
    rows, width = grad_sum.shape
    return pl.pallas_call(
        hidden_grad_kernel,
        grid=(rows // span,),
        in_specs=[pl.BlockSpec((span, width), lambda step: (step, 0)), whole_block(weight)]
        + [pl.BlockSpec((span, array.shape[1]), lambda step: (step, 0)) for array in stack],
        out_specs=pl.BlockSpec((span, width), lambda step: (step, 0)),
        out_shape=jax.ShapeDtypeStruct((rows, width), F32),
        compiler_params=params(48),
        cost_estimate=pl.CostEstimate(
            flops=6 * rows * width * width, bytes_accessed=14 * rows * width, transcendentals=0
        ),
        name="grad_hidden",
    )(grad_sum, weight, *stack)


def meshed_layer(
    hidden, lengths, w_qkv, bias_q, bias_v, w_out, bias_out, norm1_gain, norm1_bias, w_up, bias_up,
    w_down, bias_down, norm2_gain, norm2_bias, cotangent
):
    count_rows, width = hidden.shape
    hidden_units = w_up.shape[1]
    n = lax.axis_size("fsdp")
    part = width // n
    inner_part = hidden_units // n
    wide = hidden_units // width
    bounds = jnp.cumsum(lengths)
    coords = coordinates(lax.axis_index("fsdp"))
    place = jnp.stack([jnp.asarray(coord, jnp.int32) for coord in coords])

    gathered = lax.all_gather(pack_weights(w_down, w_up, w_out), "fsdp", axis=0, tiled=True)
    gathered = gathered.reshape(n, -1, width)
    vectors = jnp.stack(
        [bias_q, bias_v, bias_out, norm1_gain, norm1_bias, bias_down, norm2_gain, norm2_bias]
    )
    front = pack_front(w_qkv, vectors, bias_up[None])
    mine, others = gather_pieces(front)
    stacked, whole_qkv, whole_vectors, whole_up_bias = project(
        place, hidden, mine + others, hidden_units, n
    )
    mixed, logsum = attention_forward(bounds, stacked)
    (
        output, first_turned, mixed_turned, activated_turned, grad_second, grad_inner, grad_sum,
        grad_branch, grad_mixed, sums, up_sums,
    ) = row_pass(
        bounds, mixed, hidden, cotangent, whole_vectors, whole_up_bias, gathered, inner_part
    )
    core = (0, 0, 0, 1)
    up_keep, up_send = up_grad(place, first_turned, mixed_turned, grad_inner, grad_branch, n)
    up_came = moved(up_send, core)
    down_keep, down_send = down_grad(place, activated_turned, after(grad_second, up_keep), n)
    down_came = moved(down_send, core)
    up_keep, up_came = (array.reshape(n // 2, -1, width) for array in (up_keep, up_came))
    here, *sends = near_sum(place, (down_keep, down_came), (up_keep, up_came))
    parts = [here] + send_near(sends)
    stack = attention_backward(bounds, stacked, mixed, after(grad_mixed, *sends), logsum)
    qkv_keep, qkv_send = qkv_grad(place, hidden, stack, sums, up_sums, n)
    qkv_came = moved(qkv_send, core)
    total = far_sum([here] + [after(part, qkv_keep) for part in parts[1:]])
    here, *sends = near_sum(place, (qkv_keep, qkv_came))
    qkv_parts = send_near(sends)
    grad_hidden = hidden_grad(after(grad_sum, *sends), whole_qkv, stack)
    qkv_mine, qkv_far = reduce_far([here] + [after(part, grad_hidden) for part in qkv_parts], coords)

    my_up_out = total[inner_part:].reshape(wide + 1, part, width)
    my_down = total[:inner_part]
    my_up = my_up_out[:wide].transpose(1, 0, 2).reshape(part, hidden_units)
    my_out = my_up_out[wide]
    mine_qkv = total_of(
        qkv_mine, [after(came, my_up, my_out, my_down) for came in send_far(qkv_far)]
    )
    my_qkv = jnp.concatenate([mine_qkv[part * i : part * (i + 1)] for i in range(3)], axis=1)
    my_vectors = mine_qkv[3 * part :]
    my_bias_q, my_bias_v, my_bias_out, my_gain_one, my_shift_one, my_bias_down, my_gain_two, my_shift_two = (
        my_vectors[i, :part] for i in range(8)
    )
    my_bias_up = my_vectors[0, PAIR : PAIR + inner_part]
    return (
        output,
        grad_hidden,
        my_qkv,
        my_bias_q,
        my_bias_v,
        my_out,
        my_bias_out,
        my_gain_one,
        my_shift_one,
        my_up,
        my_bias_up,
        my_down,
        my_bias_down,
        my_gain_two,
        my_shift_two,
    )


def layer(*arrays):
    known = lax.axis_size("fsdp") == math.prod(CHIPS)
    return (meshed_layer if known else general_layer)(*arrays)


def solution(mesh):
    rows = P("fsdp", None)
    flat = P("fsdp")
    weights = (rows, flat, flat, rows, flat, flat, flat, rows, flat, rows, flat, flat, flat)
    return jax.shard_map(
        layer,
        mesh=mesh,
        in_specs=(rows, flat) + weights + (rows,),
        out_specs=(rows, rows) + weights,
        check_vma=False,
    )
```

```python
import functools
import math

import jax
import jax.numpy as jnp
from jax import lax
from jax.experimental import pallas as pl
from jax.experimental.pallas import tpu as pltpu
from jax.sharding import PartitionSpec as P

DH = 64
PAIR = 2 * DH
BF = jnp.bfloat16
F32 = jnp.float32
NEG = -1e30
EPSILON = 1e-05
ROOT_HALF = 0.7071067811865476
INV_ROOT_TWO_PI = 0.3989422804014327
LAST_LAST = (((1,), (1,)), ((), ()))
VMEM_BYTES = 60 * 2**20


def norm_forward(values_in, gain, shift):
    centre = jnp.mean(values_in, axis=-1, keepdims=True)
    centered = values_in - centre
    spread = jnp.mean(centered * centered, axis=-1, keepdims=True)
    rstd_rows = lax.rsqrt(spread + EPSILON)
    normed = centered * rstd_rows
    return (normed * gain + shift, normed, rstd_rows)


def norm_backward(upstream, normed, rstd_rows, gain):
    scaled = upstream * gain
    plain_mean = jnp.mean(scaled, axis=-1, keepdims=True)
    cross_mean = jnp.mean(scaled * normed, axis=-1, keepdims=True)
    grad_in = rstd_rows * (scaled - plain_mean - normed * cross_mean)
    return (grad_in, jnp.sum(upstream * normed, axis=0), jnp.sum(upstream, axis=0))


def gelu_slope(inner):
    normal_cdf = 0.5 * (1.0 + lax.erf(inner * ROOT_HALF))
    return normal_cdf + inner * jnp.exp(-0.5 * inner * inner) * INV_ROOT_TWO_PI


def dot_last(a, b):
    return lax.dot_general(a, b, LAST_LAST, preferred_element_type=F32)


def dot(a, b):
    return jnp.dot(a, b, preferred_element_type=F32)


def segment_at(position, bounds_ref):
    segment = jnp.zeros(position.shape, jnp.int32)
    for index in range(bounds_ref.shape[0]):
        segment += (position >= bounds_ref[index]).astype(jnp.int32)
    return segment


def attention_forward_kernel(bounds_ref, q_ref, k_ref, v_ref, mixed_ref, probs_ref, *, scale):
    rows = q_ref.shape[0]
    first_head = lax.broadcasted_iota(jnp.int32, (1, PAIR), 1) < DH
    keys = k_ref[...]
    values_turned = jnp.transpose(v_ref[...])
    queries = q_ref[...] * jnp.asarray(scale, BF)
    same = segment_at(lax.broadcasted_iota(jnp.int32, (rows, 1), 0), bounds_ref) == segment_at(
        lax.broadcasted_iota(jnp.int32, (1, rows), 1), bounds_ref
    )
    mixed = []
    for head in range(2):
        mine = first_head if head == 0 else jnp.logical_not(first_head)
        scores = dot_last(keys, jnp.where(mine, queries, jnp.zeros_like(queries)))
        scores = jnp.where(same, scores, NEG)
        highest = jnp.max(scores, axis=0, keepdims=True)
        exps = jnp.exp(scores - highest)
        total = jnp.sum(exps, axis=0, keepdims=True)
        probs = (exps * (1.0 / total)).astype(BF)
        probs_ref[head] = probs
        mixed.append(dot(values_turned[DH * head : DH * (head + 1)], probs))
    mixed_ref[...] = jnp.transpose(jnp.concatenate(mixed, axis=0)).astype(BF)


def pair_spec(rows, offset):
    return pl.BlockSpec((rows, PAIR), lambda pair, *_: (0, offset + pair))


def attention_forward(bounds, stacked):
    rows, width = stacked.shape[0], stacked.shape[1] // 3
    pairs = width // PAIR
    return pl.pallas_call(
        functools.partial(attention_forward_kernel, scale=1.0 / math.sqrt(DH)),
        grid_spec=pltpu.PrefetchScalarGridSpec(
            num_scalar_prefetch=1,
            grid=(pairs,),
            in_specs=[pair_spec(rows, 0), pair_spec(rows, pairs), pair_spec(rows, 2 * pairs)],
            out_specs=[
                pair_spec(rows, 0),
                pl.BlockSpec((2, rows, rows), lambda pair, bounds: (pair, 0, 0)),
            ],
        ),
        out_shape=[
            jax.ShapeDtypeStruct((rows, width), BF),
            jax.ShapeDtypeStruct((2 * pairs, rows, rows), BF),
        ],
        compiler_params=pltpu.CompilerParams(vmem_limit_bytes=VMEM_BYTES),
        cost_estimate=pl.CostEstimate(
            flops=rows * width, bytes_accessed=rows * width, transcendentals=0
        ),
        name="attention_forward",
    )(bounds, stacked, stacked, stacked)


def attention_backward_kernel(
    q_ref, k_ref, v_ref, mixed_ref, grad_ref, probs_ref, dq_ref, dk_ref, dv_ref, *, scale
):
    first_head = lax.broadcasted_iota(jnp.int32, (1, PAIR), 1) < DH
    values = v_ref[...]
    keys_turned = jnp.transpose(k_ref[...])
    picks = (
        lax.broadcasted_iota(jnp.int32, (8, PAIR), 1) // DH
        == lax.broadcasted_iota(jnp.int32, (8, PAIR), 0)
    ).astype(F32)
    queries = q_ref[...] * jnp.asarray(scale, BF)
    grads = grad_ref[...]
    weighted = lax.dot_general(
        picks,
        grads.astype(F32) * mixed_ref[...].astype(F32),
        LAST_LAST,
        preferred_element_type=F32,
        precision=lax.Precision.HIGHEST,
    )
    all_scores, all_grads, all_queries, grad_queries = [], [], [], []
    for head in range(2):
        mine = first_head if head == 0 else jnp.logical_not(first_head)
        my_grads = jnp.where(mine, grads, jnp.zeros_like(grads))
        grad_probs = dot_last(values, my_grads) - weighted[head : head + 1]
        grad_scores = (probs_ref[head].astype(F32) * grad_probs).astype(BF)
        all_scores.append(grad_scores)
        all_grads.append(my_grads)
        all_queries.append(jnp.where(mine, queries, jnp.zeros_like(queries)))
        grad_queries.append(dot(keys_turned[DH * head : DH * (head + 1)], grad_scores))
    turned = jnp.concatenate(grad_queries, axis=0) * scale
    dq_ref[...] = jnp.transpose(turned).astype(BF)
    all_probs = jnp.concatenate([probs_ref[0], probs_ref[1]], axis=1)
    dv_ref[...] = dot(all_probs, jnp.concatenate(all_grads, axis=0)).astype(BF)
    all_scores = jnp.concatenate(all_scores, axis=1)
    dk_ref[...] = dot(all_scores, jnp.concatenate(all_queries, axis=0)).astype(BF)


def attention_backward(stacked, mixed, grad_mixed, probs):
    rows, width = mixed.shape
    pairs = width // PAIR
    return pl.pallas_call(
        functools.partial(attention_backward_kernel, scale=1.0 / math.sqrt(DH)),
        grid=(pairs,),
        in_specs=[
            pair_spec(rows, 0),
            pair_spec(rows, pairs),
            pair_spec(rows, 2 * pairs),
            pair_spec(rows, 0),
            pair_spec(rows, 0),
            pl.BlockSpec((2, rows, rows), lambda pair: (pair, 0, 0)),
        ],
        out_specs=[pair_spec(rows, 0), pair_spec(rows, 0), pair_spec(rows, 0)],
        out_shape=[jax.ShapeDtypeStruct((rows, width), BF)] * 3,
        compiler_params=pltpu.CompilerParams(vmem_limit_bytes=VMEM_BYTES),
        cost_estimate=pl.CostEstimate(
            flops=rows * width, bytes_accessed=rows * width, transcendentals=0
        ),
        name="attention_backward",
    )(stacked, stacked, stacked, mixed, grad_mixed, probs)


def general_layer(
    hidden,
    lengths,
    w_qkv,
    bias_q,
    bias_v,
    w_out,
    bias_out,
    norm1_gain,
    norm1_bias,
    w_up,
    bias_up,
    w_down,
    bias_down,
    norm2_gain,
    norm2_bias,
    cotangent,
):
    count_rows, width = hidden.shape
    hidden_units = w_up.shape[1]
    n = lax.axis_size("fsdp")
    part = width // n
    inner_part = hidden_units // n
    wide = hidden_units // width
    bounds = jnp.cumsum(lengths)
    present = (jnp.arange(count_rows, dtype=jnp.int32) < bounds[-1]).astype(F32)[:, None]

    vectors = (bias_q, bias_v, bias_out, norm1_gain, norm1_bias, bias_up, bias_down, norm2_gain, norm2_bias)
    sizes = [vector.shape[0] for vector in vectors]
    starts = [sum(sizes[:i]) for i in range(len(sizes))]
    whole_qkv = lax.all_gather(w_qkv, "fsdp", axis=0, tiled=True)
    whole_vectors = lax.all_gather(jnp.concatenate(vectors)[None], "fsdp", axis=0, tiled=True)
    (
        whole_bias_q,
        whole_bias_v,
        whole_bias_out,
        whole_gain_one,
        whole_shift_one,
        whole_bias_up,
        whole_bias_down,
        whole_gain_two,
        whole_shift_two,
    ) = (
        whole_vectors[:, start : start + size].reshape(n * size).astype(F32)
        for start, size in zip(starts, sizes)
    )
    packed = jnp.concatenate(
        [w_out]
        + [w_up[:, width * i : width * (i + 1)] for i in range(wide)]
        + [w_down],
        axis=0,
    )
    gathered = lax.all_gather(packed, "fsdp", axis=0, tiled=True).reshape(n, -1, width)
    whole_out = gathered[:, :part].reshape(width, width)
    whole_up = (
        gathered[:, part : part * (1 + wide)]
        .reshape(n, wide, part, width)
        .transpose(0, 2, 1, 3)
        .reshape(width, hidden_units)
    )
    whole_down = gathered[:, part * (1 + wide) :].reshape(hidden_units, width)

    projected = jnp.dot(hidden, whole_qkv, preferred_element_type=F32)
    whole_bias = jnp.concatenate([whole_bias_q, jnp.zeros_like(whole_bias_q), whole_bias_v])
    stacked = (projected + whole_bias).astype(BF)
    mixed, probs = attention_forward(bounds, stacked)
    branch = jnp.dot(mixed, whole_out, preferred_element_type=F32) + whole_bias_out
    first, normed_one, rstd_one = norm_forward(
        hidden.astype(F32) + branch, whole_gain_one, whole_shift_one
    )
    first_low = first.astype(BF)
    inner = jnp.dot(first_low, whole_up, preferred_element_type=F32) + whole_bias_up
    activated = jax.nn.gelu(inner, approximate=False).astype(BF)
    second = jnp.dot(activated, whole_down, preferred_element_type=F32) + whole_bias_down
    result, normed_two, rstd_two = norm_forward(first + second, whole_gain_two, whole_shift_two)
    output = result * present
    upstream = cotangent.astype(F32) * present
    grad_second, grad_gain_two, grad_shift_two = norm_backward(
        upstream, normed_two, rstd_two, whole_gain_two
    )
    grad_branch_two = grad_second.astype(BF)
    grad_w_down = jnp.einsum("rf,rd->fd", activated, grad_branch_two, preferred_element_type=F32)
    grad_bias_down = jnp.sum(grad_branch_two.astype(F32), axis=0)
    grad_activated = jnp.einsum(
        "rd,fd->rf", grad_branch_two, whole_down, preferred_element_type=F32
    )
    grad_inner = (grad_activated * gelu_slope(inner)).astype(BF)
    grad_w_up = jnp.einsum("rd,rf->df", first_low, grad_inner, preferred_element_type=F32)
    grad_bias_up = jnp.sum(grad_inner.astype(F32), axis=0)
    grad_first = grad_second + jnp.einsum(
        "rf,df->rd", grad_inner, whole_up, preferred_element_type=F32
    )
    grad_sum_one, grad_gain_one, grad_shift_one = norm_backward(
        grad_first, normed_one, rstd_one, whole_gain_one
    )
    grad_branch_one = grad_sum_one.astype(BF)
    grad_w_out = jnp.einsum("rd,re->de", mixed, grad_branch_one, preferred_element_type=F32)
    grad_bias_out = jnp.sum(grad_branch_one.astype(F32), axis=0)
    grad_mixed = jnp.einsum(
        "re,de->rd", grad_branch_one, whole_out, preferred_element_type=F32
    ).astype(BF)
    grads_packed = jnp.concatenate(
        [
            grad_w_out.astype(BF).reshape(n, part, width),
            grad_w_up.astype(BF)
            .reshape(n, part, wide, width)
            .transpose(0, 2, 1, 3)
            .reshape(n, wide * part, width),
            grad_w_down.astype(BF).reshape(n, inner_part, width),
        ],
        axis=1,
    )
    summed = lax.psum_scatter(
        grads_packed.reshape(-1, width), "fsdp", scatter_dimension=0, tiled=True
    ).astype(F32)
    my_out = summed[:part]
    my_up = (
        summed[part : part * (1 + wide)]
        .reshape(wide, part, width)
        .transpose(1, 0, 2)
        .reshape(part, hidden_units)
    )
    my_down = summed[part * (1 + wide) :]

    grad_stack = jnp.concatenate(
        attention_backward(stacked, mixed, grad_mixed, probs), axis=1
    )
    grad_w_qkv = jnp.einsum("rd,re->de", hidden, grad_stack, preferred_element_type=F32)
    stack_sums = jnp.sum(grad_stack.astype(F32), axis=0)
    grad_hidden = grad_sum_one + jnp.einsum(
        "re,de->rd", grad_stack, whole_qkv, preferred_element_type=F32
    )
    vector_grads = jnp.concatenate(
        [
            grad.reshape(n, -1)
            for grad in (
                stack_sums[:width],
                stack_sums[2 * width :],
                grad_bias_out,
                grad_gain_one,
                grad_shift_one,
                grad_bias_up,
                grad_bias_down,
                grad_gain_two,
                grad_shift_two,
            )
        ],
        axis=1,
    )
    my_qkv = lax.psum_scatter(
        grad_w_qkv.astype(BF), "fsdp", scatter_dimension=0, tiled=True
    ).astype(F32)
    every_vector = lax.psum(vector_grads, "fsdp")
    my_vectors = lax.dynamic_index_in_dim(every_vector, lax.axis_index("fsdp"), 0, keepdims=False)
    (my_bias_q, my_bias_v, my_bias_out, my_gain_one, my_shift_one, my_bias_up, my_bias_down, my_gain_two, my_shift_two) = (
        my_vectors[start : start + size] for start, size in zip(starts, sizes)
    )
    return (
        output,
        grad_hidden,
        my_qkv,
        my_bias_q,
        my_bias_v,
        my_out,
        my_bias_out,
        my_gain_one,
        my_shift_one,
        my_up,
        my_bias_up,
        my_down,
        my_bias_down,
        my_gain_two,
        my_shift_two,
    )


CHIPS = (4, 2, 2, 2)


def coordinates(index):
    _, ys, xs, cores = CHIPS
    return (index // (cores * xs * ys), index // (cores * xs) % ys, index // cores % xs, index % cores)


def moved(array, step):
    sizes = CHIPS
    pairs = []
    for source in range(math.prod(sizes)):
        target = 0
        for place, by, size in zip(coordinates(source), step, sizes):
            target = target * size + (place + by) % size
        pairs.append((source, target))
    return lax.ppermute(array, "fsdp", pairs)


def pack_weights_kernel(down_ref, up_ref, out_ref, packed_ref):
    width = down_ref.shape[1]
    wide = up_ref.shape[1] // width
    parts = [down_ref[...]] + [up_ref[:, width * i : width * (i + 1)] for i in range(wide)]
    parts = [part.astype(F32) for part in parts + [out_ref[...]]]
    fill = packed_ref.shape[0] - sum(part.shape[0] for part in parts)
    parts.append(jnp.zeros((fill, width), F32))
    packed_ref[...] = jnp.concatenate(parts, axis=0).astype(BF)


def pack_weights(w_down, w_up, w_out):
    rows = w_down.shape[0] + w_up.size // w_out.shape[1] + w_out.shape[0]
    return pl.pallas_call(
        pack_weights_kernel,
        out_shape=jax.ShapeDtypeStruct((rows + -rows % 16, w_out.shape[1]), BF),
        name="pack_weights",
    )(w_down, w_up, w_out)


def pack_front_kernel(qkv_ref, vector_ref, up_ref, packed_ref):
    width = packed_ref.shape[1]
    parts = [qkv_ref[:, width * i : width * (i + 1)].astype(F32) for i in range(3)]
    extra = jnp.zeros((8, width), F32)
    lanes = lax.broadcasted_iota(jnp.int32, (8, PAIR), 1)
    rows = lax.broadcasted_iota(jnp.int32, (8, PAIR), 0)
    part, inner_part = vector_ref.shape[1], up_ref.shape[1]
    vectors = jnp.concatenate(
        [vector_ref[...].astype(F32), jnp.zeros((8, PAIR - part), F32)], axis=1
    )
    long = jnp.concatenate([up_ref[...].astype(F32), jnp.zeros((1, PAIR - inner_part), F32)], axis=1)
    long = jnp.where((rows == 0) & (lanes < inner_part), long, 0.0)
    extra = jnp.concatenate([vectors, long, extra[:, 2 * PAIR :]], axis=1)
    packed_ref[...] = jnp.concatenate(parts + [extra], axis=0).astype(BF)


def pack_front(w_qkv, vectors, bias_up):
    part, width = w_qkv.shape[0], w_qkv.shape[1] // 3
    return pl.pallas_call(
        pack_front_kernel,
        out_shape=jax.ShapeDtypeStruct((3 * part + 8, width), BF),
        name="pack_front",
    )(w_qkv, vectors, bias_up)


def gather_pieces(packed):
    column = jnp.stack([packed] + [moved(packed, (step, 0, 0, 0)) for step in range(1, CHIPS[0])])
    pieces = [column] + [moved(column, step) for step in ((0, 0, 1, 0), (0, 1, 0, 0), (0, 1, 1, 0))]
    return pieces, [moved(piece, (0, 0, 0, 1)) for piece in pieces]


NEAR = ((0, 0, 1, 0), (0, 1, 0, 0), (0, 1, 1, 0))


def near_sum_kernel(place_ref, *refs, cuts):
    pairs = [(refs[2 * i], refs[2 * i + 1]) for i in range(len(cuts))]
    outs = refs[2 * len(cuts) :]
    ys, xs = CHIPS[1:3]
    for out_ref, (_, step_y, step_x, _) in zip(outs, ((0, 0, 0, 0),) + NEAR):
        chip = (place_ref[1] + step_y) % ys * xs + (place_ref[2] + step_x) % xs
        for (keep_ref, came_ref), (start, size) in zip(pairs, cuts):
            total = keep_ref[chip].astype(F32) + came_ref[chip].astype(F32)
            out_ref[0, start : start + size, :] = total.astype(BF)


def near_sum(place, *pairs):
    zs, ys, xs, _ = CHIPS
    near = ys * xs
    sizes = [keep.shape[1] for keep, _ in pairs]
    cuts = [(sum(sizes[:i]), size) for i, size in enumerate(sizes)]
    width = pairs[0][0].shape[2]
    out = jax.ShapeDtypeStruct((zs, sum(sizes), width), BF)
    return pl.pallas_call(
        functools.partial(near_sum_kernel, cuts=cuts),
        grid_spec=pltpu.PrefetchScalarGridSpec(
            num_scalar_prefetch=1,
            grid=(zs,),
            in_specs=[
                pl.BlockSpec((near, size, width), lambda step, place: (step, 0, 0))
                for size in sizes
                for _ in range(2)
            ],
            out_specs=[pl.BlockSpec((1, sum(sizes), width), lambda step, place: (step, 0, 0))] * 4,
        ),
        out_shape=[out] * 4,
        compiler_params=params(24),
        cost_estimate=pl.CostEstimate(
            flops=out.size, bytes_accessed=out.size, transcendentals=0
        ),
        name="near_sum",
    )(place, *(array for pair in pairs for array in pair))


def first_sum_kernel(place_ref, *refs, cuts):
    keep_ref, by_x_ref, by_y_ref = refs[2 * len(cuts) :]
    _, ys, xs, _ = CHIPS
    y, x = place_ref[1], place_ref[2]
    low = pl.program_id(0) < CHIPS[0] // 2

    def total(pair, chip):
        return (refs[2 * pair][chip].astype(F32) + refs[2 * pair + 1][chip].astype(F32)).astype(BF)

    for other in range(2):
        mine = jnp.where(low, other * xs + x, y * xs + other)
        theirs = jnp.where(low, other * xs + (x + 1) % xs, (y + 1) % ys * xs + other)
        for pair, (start, size) in enumerate(cuts):
            rows = slice(start, start + size)
            keep_ref[0, other, rows, :] = total(pair, mine)

            @pl.when(low)
            def _():
                by_x_ref[0, other, rows, :] = total(pair, theirs)

            @pl.when(jnp.logical_not(low))
            def _():
                by_y_ref[0, other, rows, :] = total(pair, theirs)


def halves(block):
    half = CHIPS[0] // 2
    rest = (0,) * (len(block) - 1)
    low = pl.BlockSpec(block, lambda step, place: (jnp.minimum(step, half - 1),) + rest)
    high = pl.BlockSpec(block, lambda step, place: (jnp.maximum(step - half, 0),) + rest)
    return low, high


def first_sum(place, *pairs):
    zs, ys, xs, _ = CHIPS
    sizes = [keep.shape[1] for keep, _ in pairs]
    cuts = [(sum(sizes[:i]), size) for i, size in enumerate(sizes)]
    width = pairs[0][0].shape[2]
    block = (1, 2, sum(sizes), width)
    keep = jax.ShapeDtypeStruct((zs,) + block[1:], BF)
    send = jax.ShapeDtypeStruct((zs // 2,) + block[1:], BF)
    return pl.pallas_call(
        functools.partial(first_sum_kernel, cuts=cuts),
        grid_spec=pltpu.PrefetchScalarGridSpec(
            num_scalar_prefetch=1,
            grid=(zs,),
            in_specs=[
                pl.BlockSpec((ys * xs, size, width), lambda step, place: (step, 0, 0))
                for size in sizes
                for _ in range(2)
            ],
            out_specs=[pl.BlockSpec(block, lambda step, place: (step, 0, 0, 0)), *halves(block)],
        ),
        out_shape=[keep, send, send],
        compiler_params=params(24),
        cost_estimate=pl.CostEstimate(flops=keep.size, bytes_accessed=keep.size, transcendentals=0),
        name="first_sum",
    )(place, *(array for pair in pairs for array in pair))


def second_sum_kernel(place_ref, keep_ref, from_x_ref, from_y_ref, own_ref, by_y_ref, by_x_ref):
    low = pl.program_id(0) < CHIPS[0] // 2

    def go(came_ref, own, send_ref):
        def total(index):
            return (keep_ref[0, index].astype(F32) + came_ref[0, index].astype(F32)).astype(BF)

        own_ref[0] = total(own)
        send_ref[0] = total(1 - own)

    @pl.when(low)
    def _():
        go(from_x_ref, place_ref[1], by_y_ref)

    @pl.when(jnp.logical_not(low))
    def _():
        go(from_y_ref, place_ref[2], by_x_ref)


def second_sum(place, keep, from_x, from_y):
    zs = CHIPS[0]
    block = (1,) + keep.shape[2:]
    own = jax.ShapeDtypeStruct((zs,) + block[1:], BF)
    send = jax.ShapeDtypeStruct((zs // 2,) + block[1:], BF)
    return pl.pallas_call(
        second_sum_kernel,
        grid_spec=pltpu.PrefetchScalarGridSpec(
            num_scalar_prefetch=1,
            grid=(zs,),
            in_specs=[
                pl.BlockSpec((1,) + keep.shape[1:], lambda step, place: (step, 0, 0, 0)),
                *halves((1,) + keep.shape[1:]),
            ],
            out_specs=[pl.BlockSpec(block, lambda step, place: (step, 0, 0)), *halves(block)],
        ),
        out_shape=[own, send, send],
        compiler_params=params(24),
        cost_estimate=pl.CostEstimate(flops=own.size, bytes_accessed=own.size, transcendentals=0),
        name="second_sum",
    )(place, keep, from_x, from_y)


def send_near(sends):
    return [moved(array, step) for array, step in zip(sends, NEAR)]


def far_add(own, low, high):
    return (own.astype(F32) + jnp.concatenate([low, high]).astype(F32)).astype(BF)


def far_scatter(total):
    zs, ys, xs, cores = CHIPS
    across = ys * xs * cores
    groups = [[level * across + i for level in range(zs)] for i in range(across)]
    return lax.psum_scatter(
        total, "fsdp", scatter_dimension=0, axis_index_groups=groups, tiled=False
    ).astype(F32)


def reduce_far(parts, place):
    z, zs = place[0], CHIPS[0]

    def at(level):
        return sum(
            lax.dynamic_index_in_dim(part, level, 0, keepdims=False).astype(F32) for part in parts
        )

    return at(z), [at((z + step) % zs).astype(BF) for step in range(1, zs)]


def send_far(sends):
    return [moved(array, (step, 0, 0, 0)) for step, array in enumerate(sends, 1)]


def total_of(mine, came):
    return mine + sum(array.astype(F32) for array in came)


def after(value, *first):
    return lax.optimization_barrier((value, *first))[0]


def params(megabytes):
    return pltpu.CompilerParams(vmem_limit_bytes=megabytes * 2**20)


def whole_block(array):
    return pl.BlockSpec(array.shape, lambda *step: (0,) * array.ndim)


def project_kernel(
    place_ref, hidden_ref, *refs, part, inner_part
):
    pieces = refs[: len(refs) - 5]
    stacked_ref, weight_ref, vector_ref, up_ref, turned_ref = refs[len(refs) - 5 :]
    z, y, x, core = (place_ref[i] for i in range(4))
    zs, ys, xs, cores = CHIPS
    width = hidden_ref.shape[1]
    lanes = lax.broadcasted_iota(jnp.int32, (8, width), 1)
    up_lanes = lax.broadcasted_iota(jnp.int32, (8, up_ref.shape[1]), 1)
    vectors = jnp.zeros((8, width), F32)
    ups = jnp.zeros(up_ref.shape, F32)
    steps = ((0, 0), (0, 1), (1, 0), (1, 1))
    for kind, (step_y, step_x) in enumerate(steps):
        for step_z in range(zs):
            chip = ((z + zs - step_z) % zs * ys + (y + step_y) % ys) * xs + (x + step_x) % xs
            mine = pieces[kind][step_z].astype(F32)
            other = pieces[len(steps) + kind][step_z].astype(F32)
            low = jnp.where(core == 0, mine, other)
            high = jnp.where(core == 0, other, mine)
            rows = pl.ds(pl.multiple_of(chip * (cores * part), cores * part), cores * part)
            for third in range(3):
                cut = slice(third * part, (third + 1) * part)
                weight_ref[rows, third * width : (third + 1) * width] = jnp.concatenate(
                    [low[cut], high[cut]], axis=0
                ).astype(BF)
            for owner, piece in ((chip * cores, low), (chip * cores + 1, high)):
                extra = piece[3 * part :]
                vectors += pltpu.roll(jnp.where(lanes < part, extra, 0.0), owner * part, 1)
                long = jnp.concatenate(
                    [extra[:, PAIR:]] + [jnp.zeros((8, up_ref.shape[1] - width + PAIR), F32)], axis=1
                )
                ups += pltpu.roll(jnp.where(up_lanes < inner_part, long, 0.0), owner * inner_part, 1)
    vector_ref[...] = vectors
    up_ref[...] = ups
    hidden = hidden_ref[...]
    turned_ref[...] = jnp.transpose(hidden)
    for third, bias in ((0, vectors[0:1]), (1, None), (2, vectors[1:2])):
        cut = slice(third * width, (third + 1) * width)
        projected = dot(hidden, weight_ref[:, cut])
        stacked_ref[:, cut] = (projected if bias is None else projected + bias).astype(BF)


def project(place, hidden, pieces, hidden_units, count):
    rows, width = hidden.shape
    outs = [
        jax.ShapeDtypeStruct((rows, 3 * width), BF),
        jax.ShapeDtypeStruct((width, 3 * width), BF),
        jax.ShapeDtypeStruct((8, width), F32),
        jax.ShapeDtypeStruct((8, hidden_units), F32),
        jax.ShapeDtypeStruct((width, rows), BF),
    ]
    return pl.pallas_call(
        functools.partial(project_kernel, part=width // count, inner_part=hidden_units // count),
        grid_spec=pltpu.PrefetchScalarGridSpec(
            num_scalar_prefetch=1,
            grid=(1,),
            in_specs=[whole_block(hidden)] + [whole_block(piece) for piece in pieces],
            out_specs=[whole_block(out) for out in outs],
        ),
        out_shape=outs,
        compiler_params=params(48),
        name="project",
    )(place, hidden, *pieces)


def gelu_and_slope(inner):
    near = 1.0 / (1.0 + (0.3275911 * ROOT_HALF) * jnp.abs(inner))
    bell = jnp.exp(-0.5 * inner * inner)
    series = 0.7107068705 + near * (-0.7265760135 + near * 0.5307027145)
    series = near * (0.127414796 + near * (-0.142248368 + near * series))
    tail = series * bell
    normal_cdf = jnp.where(inner >= 0, 1.0 - tail, tail)
    return inner * normal_cdf, normal_cdf + inner * bell * INV_ROOT_TWO_PI


def norm_back(upstream, normed, rstd_rows, gain):
    scaled = upstream * gain
    plain_mean = jnp.mean(scaled, axis=-1, keepdims=True)
    cross_mean = jnp.mean(scaled * normed, axis=-1, keepdims=True)
    return rstd_rows * (scaled - plain_mean - normed * cross_mean)


def column_sum(values):
    return jnp.sum(values, axis=0, keepdims=True)


def row_pass_kernel(
    bounds_ref, mixed_ref, hidden_ref, cotangent_ref, vector_ref, bias_up_ref, gathered_ref,
    output_ref, left_ref, right_ref, grad_sum_ref, grad_mixed_ref, sums_ref, up_sums_ref,
    w_out, w_up, w_down, staged, slope, sems, *, part, chunk
):
    step = pl.program_id(0)
    span, width = mixed_ref.shape
    count, inner_part = w_down.shape[0], w_down.shape[1]
    hidden_units = w_up.shape[1]
    wide = hidden_units // width

    batch = count // 4
    copies = [
        pltpu.make_async_copy(
            gathered_ref.at[pl.ds(start, batch), pl.ds(inner_part, staged.shape[1])],
            staged.at[pl.ds(start, batch)],
            sems.at[1 + start // batch],
        )
        for start in range(0, count, batch)
    ]
    down_copy = pltpu.make_async_copy(
        gathered_ref.at[:, pl.ds(0, inner_part)], w_down, sems.at[0]
    )

    @pl.when(step == 0)
    def _():
        for copy in copies + [down_copy]:
            copy.start()
        for pair in range(count // 2):
            if 2 * pair % batch == 0:
                copies[2 * pair // batch].wait()
            low = staged[2 * pair].astype(F32)
            high = staged[2 * pair + 1].astype(F32)
            rows = slice(2 * pair * part, 2 * (pair + 1) * part)
            for group in range(wide + 1):
                cut = slice(group * part, (group + 1) * part)
                both = jnp.concatenate([low[cut], high[cut]], axis=0).astype(BF)
                if group < wide:
                    w_up[rows, group * width : (group + 1) * width] = both
                else:
                    w_out[rows, :] = both

    def down_rows(cut):
        owners = slice(cut.start // inner_part, cut.stop // inner_part)
        return w_down[owners].reshape(cut.stop - cut.start, width)

    bias_out, gain_one, shift_one, bias_down, gain_two, shift_two = (
        vector_ref[i : i + 1, :] for i in range(2, 8)
    )
    mixed = mixed_ref[...]
    branch = dot(mixed, w_out[...]) + bias_out
    first, normed_one, rstd_one = norm_forward(
        hidden_ref[...].astype(F32) + branch, gain_one, shift_one
    )
    first_low = first.astype(BF)
    left_ref[hidden_units : hidden_units + width, :] = jnp.transpose(first_low)
    left_ref[hidden_units + width :, :] = jnp.transpose(mixed)
    cuts = [slice(start, start + chunk) for start in range(0, hidden_units, chunk)]
    second = jnp.zeros(first.shape, F32)
    for cut in cuts:
        inner = dot(first_low, w_up[:, cut]) + bias_up_ref[0:1, cut]
        activated, slopes = gelu_and_slope(inner)
        activated = activated.astype(BF)
        slope[:, cut] = slopes
        left_ref[cut, :] = jnp.transpose(activated)
        if cut.start == 0:

            @pl.when(step == 0)
            def _():
                down_copy.wait()

        second += dot(activated, down_rows(cut))
    result, normed_two, rstd_two = norm_forward(
        first + (second + bias_down), gain_two, shift_two
    )
    row = lax.broadcasted_iota(jnp.int32, (span, 1), 0) + step * span
    present = (row < bounds_ref[bounds_ref.shape[0] - 1]).astype(F32)
    output_ref[...] = result * present
    upstream = cotangent_ref[...].astype(F32) * present
    grad_second = norm_back(upstream, normed_two, rstd_two, gain_two)
    grad_second_low = grad_second.astype(BF)
    right_ref[:, :width] = grad_second_low
    grad_first = grad_second
    up_sums = []
    for cut in cuts:
        grad_activated = dot_last(grad_second_low, down_rows(cut))
        grad_inner = (grad_activated * slope[:, cut]).astype(BF)
        right_ref[:, width + cut.start : width + cut.stop] = grad_inner
        up_sums.append(column_sum(grad_inner.astype(F32)))
        grad_first += dot_last(grad_inner, w_up[:, cut])
    grad_sum = norm_back(grad_first, normed_one, rstd_one, gain_one)
    grad_sum_ref[...] = grad_sum
    grad_branch = grad_sum.astype(BF)
    right_ref[:, width + hidden_units :] = grad_branch
    grad_mixed_ref[...] = dot_last(grad_branch, w_out[...]).astype(BF)
    sums = jnp.concatenate(
        [
            column_sum(grad_branch.astype(F32)),
            column_sum(grad_first * normed_one),
            column_sum(grad_first),
            column_sum(grad_second_low.astype(F32)),
            column_sum(upstream * normed_two),
            column_sum(upstream),
            jnp.zeros((2, width), F32),
        ],
        axis=0,
    )
    up_sums = jnp.concatenate(
        [jnp.concatenate(up_sums, axis=1), jnp.zeros((7, hidden_units), F32)], axis=0
    )

    @pl.when(step == 0)
    def _():
        sums_ref[...] = sums
        up_sums_ref[...] = up_sums

    @pl.when(step > 0)
    def _():
        sums_ref[...] += sums
        up_sums_ref[...] += up_sums


def row_pass(bounds, mixed, hidden, cotangent, vectors, bias_up, gathered, inner_part, span=256, chunk=768):
    rows, width = mixed.shape
    hidden_units = bias_up.shape[1]
    count = gathered.shape[0]
    part = width // count
    row_spec = pl.BlockSpec((span, width), lambda step, bounds: (step, 0))
    stacked = hidden_units + 2 * width
    shape = jax.ShapeDtypeStruct
    sums = shape((8, width), F32)
    up_sums = shape((8, hidden_units), F32)
    staged_rows = gathered.shape[1] - inner_part
    return pl.pallas_call(
        functools.partial(row_pass_kernel, part=part, chunk=chunk),
        grid_spec=pltpu.PrefetchScalarGridSpec(
            num_scalar_prefetch=1,
            grid=(rows // span,),
            in_specs=[
                row_spec,
                row_spec,
                row_spec,
                whole_block(vectors),
                whole_block(bias_up),
                pl.BlockSpec(memory_space=pl.ANY),
            ],
            out_specs=[
                row_spec,
                pl.BlockSpec((stacked, span), lambda step, bounds: (0, step)),
                pl.BlockSpec((span, stacked), lambda step, bounds: (step, 0)),
                row_spec,
                row_spec,
                whole_block(sums),
                whole_block(up_sums),
            ],
            scratch_shapes=[
                pltpu.VMEM((width, width), BF),
                pltpu.VMEM((width, hidden_units), BF),
                pltpu.VMEM((count, inner_part, width), BF),
                pltpu.VMEM((count, staged_rows, width), BF),
                pltpu.VMEM((span, hidden_units), F32),
                pltpu.SemaphoreType.DMA((5,)),
            ],
        ),
        out_shape=[
            shape((rows, width), F32),
            shape((stacked, rows), BF),
            shape((rows, stacked), BF),
            shape((rows, width), F32),
            shape((rows, width), BF),
            sums,
            up_sums,
        ],
        compiler_params=params(60),
        cost_estimate=pl.CostEstimate(
            flops=2 * rows * width * (4 * hidden_units + 2 * width),
            bytes_accessed=40 * rows * width,
            transcendentals=0,
        ),
        name="row_pass",
    )(bounds, mixed, hidden, cotangent, vectors, bias_up, gathered)


def split_owners(place_ref, keep_ref, send_ref, tile_of, count, lead=()):
    first = place_ref[3] == 0
    for chip in range(count // 2):
        even, odd = tile_of(2 * chip), tile_of(2 * chip + 1)
        keep_ref[(chip,) + lead] = jnp.where(first, even, odd).astype(BF)
        send_ref[(chip,) + lead] = jnp.where(first, odd, even).astype(BF)


def down_grad_kernel(place_ref, left_ref, right_ref, keep_ref, send_ref):
    part = keep_ref.shape[1]
    product = dot(left_ref[...], right_ref[...])
    count = product.shape[0] // part
    split_owners(place_ref, keep_ref, send_ref, lambda o: product[o * part : (o + 1) * part], count)


def down_grad(place, left, right, width, count):
    rows = left.shape[1]
    steps = left.shape[0] // width - 2
    part = steps * width // count
    half = count // 2
    spec = pl.BlockSpec((half // steps, part, width), lambda step, place: (step, 0, 0))
    return pl.pallas_call(
        down_grad_kernel,
        grid_spec=pltpu.PrefetchScalarGridSpec(
            num_scalar_prefetch=1,
            grid=(steps,),
            in_specs=[
                pl.BlockSpec((width, rows), lambda step, place: (step, 0)),
                pl.BlockSpec((rows, width), lambda step, place: (0, 0)),
            ],
            out_specs=[spec, spec],
        ),
        out_shape=[jax.ShapeDtypeStruct((half, part, width), BF)] * 2,
        compiler_params=params(48),
        cost_estimate=pl.CostEstimate(
            flops=rows * width, bytes_accessed=rows * width, transcendentals=0
        ),
        name="grad_w_down",
    )(place, left, right)


def up_grad_kernel(place_ref, left_ref, right_ref, keep_ref, send_ref):
    part = keep_ref.shape[2]
    product = dot(left_ref[...], right_ref[...])
    count = product.shape[0] // part
    split_owners(
        place_ref, keep_ref, send_ref, lambda o: product[o * part : (o + 1) * part], count, (0,)
    )


def up_grad(place, left, right, width, count):
    rows = left.shape[1]
    wide = left.shape[0] // width - 2
    half, part = count // 2, width // count
    spec = pl.BlockSpec((half, 1, part, width), lambda step, place: (0, step, 0, 0))
    return pl.pallas_call(
        up_grad_kernel,
        grid_spec=pltpu.PrefetchScalarGridSpec(
            num_scalar_prefetch=1,
            grid=(wide + 1,),
            in_specs=[
                pl.BlockSpec((width, rows), lambda step, place: (wide + step // wide, 0)),
                pl.BlockSpec((rows, width), lambda step, place: (0, 1 + step)),
            ],
            out_specs=[spec, spec],
        ),
        out_shape=[jax.ShapeDtypeStruct((half, wide + 1, part, width), BF)] * 2,
        compiler_params=params(48),
        cost_estimate=pl.CostEstimate(
            flops=rows * width, bytes_accessed=rows * width, transcendentals=0
        ),
        name="grad_w_up_out",
    )(place, left, right)


def qkv_grad_kernel(place_ref, turned_ref, sums_ref, up_sums_ref, *refs, part, inner_part):
    long_refs, short_refs = refs[-4:-2], refs[-2:]
    stack = refs[:-4]
    each = len(stack) // 3
    width, rows = turned_ref.shape
    turned = turned_ref[...]
    ones = jnp.ones((8, rows), BF)

    def joined(left, third):
        return jnp.concatenate(
            [dot(left, ref[...]) for ref in stack[third * each : (third + 1) * each]], axis=1
        )

    products = [joined(turned, third) for third in range(3)]
    vectors = jnp.concatenate(
        [joined(ones, 0)[0:1], joined(ones, 2)[0:1], sums_ref[0:6, :]], axis=0
    )
    top = lax.broadcasted_iota(jnp.int32, (8, 1), 0) == 0

    def tile_of(owner):
        cut = slice(owner * part, (owner + 1) * part)
        own = pltpu.roll(vectors, width - owner * part, 1) if owner else vectors
        start = owner * inner_part // PAIR * PAIR
        long = jnp.concatenate(
            [up_sums_ref[:, start : start + PAIR], up_sums_ref[:, start + PAIR : start + 2 * PAIR]]
            if start + 2 * PAIR <= up_sums_ref.shape[1]
            else [up_sums_ref[:, start : start + PAIR]] * 2,
            axis=1,
        )
        shift = owner * inner_part - start
        long = pltpu.roll(long, 2 * PAIR - shift, 1) if shift else long
        extra = jnp.concatenate(
            [own[:, :PAIR], jnp.where(top, long[:, :PAIR], 0.0), jnp.zeros((8, width - 2 * PAIR), F32)],
            axis=1,
        )
        return jnp.concatenate([products[2][cut], extra], axis=0)

    def long_tile_of(owner):
        cut = slice(owner * part, (owner + 1) * part)
        return jnp.concatenate([product[cut] for product in products[:2]], axis=0)

    split_owners(place_ref, *long_refs, long_tile_of, width // part)
    split_owners(place_ref, *short_refs, tile_of, width // part)


def qkv_grad(place, turned, stack, sums, up_sums, count):
    width, rows = turned.shape
    part = width // count
    outs = [
        jax.ShapeDtypeStruct((count // 2, tall, width), BF)
        for tall in (2 * part, 2 * part, part + 8, part + 8)
    ]
    return pl.pallas_call(
        functools.partial(qkv_grad_kernel, part=part, inner_part=up_sums.shape[1] // count),
        grid_spec=pltpu.PrefetchScalarGridSpec(
            num_scalar_prefetch=1,
            grid=(1,),
            in_specs=[whole_block(array) for array in (turned, sums, up_sums, *stack)],
            out_specs=[whole_block(out) for out in outs],
        ),
        out_shape=outs,
        compiler_params=params(48),
        cost_estimate=pl.CostEstimate(
            flops=rows * width, bytes_accessed=rows * width, transcendentals=0
        ),
        name="grad_w_qkv",
    )(place, turned, sums, up_sums, *stack)


def hidden_grad_kernel(grad_sum_ref, weight_ref, *refs):
    out_ref = refs[-1]
    stack = refs[:-1]
    total = grad_sum_ref[...]
    start = 0
    for ref in stack:
        size = ref.shape[1]
        total += dot_last(ref[...], weight_ref[:, start : start + size])
        start += size
    out_ref[...] = total


def hidden_grad(grad_sum, weight, stack, span=256):
    rows, width = grad_sum.shape
    return pl.pallas_call(
        hidden_grad_kernel,
        grid=(rows // span,),
        in_specs=[pl.BlockSpec((span, width), lambda step: (step, 0)), whole_block(weight)]
        + [pl.BlockSpec((span, array.shape[1]), lambda step: (step, 0)) for array in stack],
        out_specs=pl.BlockSpec((span, width), lambda step: (step, 0)),
        out_shape=jax.ShapeDtypeStruct((rows, width), F32),
        compiler_params=params(48),
        cost_estimate=pl.CostEstimate(
            flops=rows * width, bytes_accessed=rows * width, transcendentals=0
        ),
        name="grad_hidden",
    )(grad_sum, weight, *stack)


def meshed_layer(
    hidden, lengths, w_qkv, bias_q, bias_v, w_out, bias_out, norm1_gain, norm1_bias, w_up, bias_up,
    w_down, bias_down, norm2_gain, norm2_bias, cotangent
):
    count_rows, width = hidden.shape
    hidden_units = w_up.shape[1]
    n = lax.axis_size("fsdp")
    part = width // n
    inner_part = hidden_units // n
    wide = hidden_units // width
    bounds = jnp.cumsum(lengths)
    coords = coordinates(lax.axis_index("fsdp"))
    place = jnp.stack([jnp.asarray(coord, jnp.int32) for coord in coords])

    gathered = lax.all_gather(pack_weights(w_down, w_up, w_out), "fsdp", axis=0, tiled=True)
    gathered = gathered.reshape(n, -1, width)
    vectors = jnp.stack(
        [bias_q, bias_v, bias_out, norm1_gain, norm1_bias, bias_down, norm2_gain, norm2_bias]
    )
    front = pack_front(w_qkv, vectors, bias_up[None])
    mine, others = gather_pieces(front)
    stacked, whole_qkv, whole_vectors, whole_up_bias, hidden_turned = project(
        place, hidden, mine + others, hidden_units, n
    )
    mixed, probs = attention_forward(bounds, stacked)
    output, left, right, grad_sum, grad_mixed, sums, up_sums = row_pass(
        bounds, mixed, hidden, cotangent, whole_vectors, whole_up_bias, gathered, inner_part
    )
    core = (0, 0, 0, 1)
    up_keep, up_send = up_grad(place, left, right, width, n)
    up_came = moved(up_send, core)
    down_keep, down_send = down_grad(place, after(left, up_keep), right, width, n)
    down_came = moved(down_send, core)
    up_keep, up_came = (array.reshape(n // 2, -1, width) for array in (up_keep, up_came))
    keep, by_x, by_y = first_sum(place, (down_keep, down_came), (up_keep, up_came))
    from_x, from_y = moved(by_x, NEAR[0]), moved(by_y, NEAR[1])
    stack = attention_backward(stacked, mixed, after(grad_mixed, by_x, by_y), probs)
    own, by_y, by_x = second_sum(place, keep, after(from_x, *stack), after(from_y, *stack))
    low, high = moved(by_y, NEAR[1]), moved(by_x, NEAR[0])
    long_keep, long_send, short_keep, short_send = qkv_grad(
        place, after(hidden_turned, by_x, by_y), stack, sums, up_sums, n
    )
    long_came, short_came = moved(long_send, core), moved(short_send, core)
    here, *sends = near_sum(place, (long_keep, long_came), (short_keep, short_came))
    total = far_add(own, after(low, *sends), after(high, *sends))
    grad_hidden = hidden_grad(after(grad_sum, total), whole_qkv, stack)
    total = far_scatter(total)
    qkv_parts = send_near(sends)
    qkv_mine, qkv_far = reduce_far([here] + qkv_parts, coords)
    my_up_out = total[inner_part:].reshape(wide + 1, part, width)
    my_down = total[:inner_part]
    my_up = my_up_out[:wide].transpose(1, 0, 2).reshape(part, hidden_units)
    my_out = my_up_out[wide]
    mine_qkv = total_of(
        qkv_mine, [after(came, my_up, my_out, my_down) for came in send_far(qkv_far)]
    )
    my_qkv = jnp.concatenate([mine_qkv[part * i : part * (i + 1)] for i in range(3)], axis=1)
    my_vectors = mine_qkv[3 * part :]
    my_bias_q, my_bias_v, my_bias_out, my_gain_one, my_shift_one, my_bias_down, my_gain_two, my_shift_two = (
        my_vectors[i, :part] for i in range(8)
    )
    my_bias_up = my_vectors[0, PAIR : PAIR + inner_part]
    return (
        output,
        grad_hidden,
        my_qkv,
        my_bias_q,
        my_bias_v,
        my_out,
        my_bias_out,
        my_gain_one,
        my_shift_one,
        my_up,
        my_bias_up,
        my_down,
        my_bias_down,
        my_gain_two,
        my_shift_two,
    )


def layer(*arrays):
    known = lax.axis_size("fsdp") == math.prod(CHIPS)
    return (meshed_layer if known else general_layer)(*arrays)


def solution(mesh):
    rows = P("fsdp", None)
    flat = P("fsdp")
    weights = (rows, flat, flat, rows, flat, flat, flat, rows, flat, rows, flat, flat, flat)
    return jax.shard_map(
        layer,
        mesh=mesh,
        in_specs=(rows, flat) + weights + (rows,),
        out_specs=(rows, rows) + weights,
        check_vma=False,
    )
```

```python
import functools
import math

import jax
import jax.numpy as jnp
from jax import lax
from jax.experimental import pallas as pl
from jax.experimental.pallas import tpu as pltpu
from jax.sharding import PartitionSpec as P

DH = 64
PAIR = 2 * DH
BF = jnp.bfloat16
F32 = jnp.float32
NEG = -1e30
EPSILON = 1e-05
ROOT_HALF = 0.7071067811865476
INV_ROOT_TWO_PI = 0.3989422804014327
LAST_LAST = (((1,), (1,)), ((), ()))
VMEM_BYTES = 60 * 2**20


def norm_forward(values_in, gain, shift):
    centre = jnp.mean(values_in, axis=-1, keepdims=True)
    centered = values_in - centre
    spread = jnp.mean(centered * centered, axis=-1, keepdims=True)
    rstd_rows = lax.rsqrt(spread + EPSILON)
    normed = centered * rstd_rows
    return (normed * gain + shift, normed, rstd_rows)


def norm_backward(upstream, normed, rstd_rows, gain):
    scaled = upstream * gain
    plain_mean = jnp.mean(scaled, axis=-1, keepdims=True)
    cross_mean = jnp.mean(scaled * normed, axis=-1, keepdims=True)
    grad_in = rstd_rows * (scaled - plain_mean - normed * cross_mean)
    return (grad_in, jnp.sum(upstream * normed, axis=0), jnp.sum(upstream, axis=0))


def gelu_slope(inner):
    normal_cdf = 0.5 * (1.0 + lax.erf(inner * ROOT_HALF))
    return normal_cdf + inner * jnp.exp(-0.5 * inner * inner) * INV_ROOT_TWO_PI


def dot_last(a, b):
    return lax.dot_general(a, b, LAST_LAST, preferred_element_type=F32)


def dot(a, b):
    return jnp.dot(a, b, preferred_element_type=F32)


def segment_at(position, bounds_ref):
    segment = jnp.zeros(position.shape, jnp.int32)
    for index in range(bounds_ref.shape[0]):
        segment += (position >= bounds_ref[index]).astype(jnp.int32)
    return segment


def attention_forward_kernel(bounds_ref, q_ref, k_ref, v_ref, mixed_ref, probs_ref, *, scale):
    rows = q_ref.shape[0]
    first_head = lax.broadcasted_iota(jnp.int32, (1, PAIR), 1) < DH
    keys = k_ref[...]
    values_turned = jnp.transpose(v_ref[...])
    queries = q_ref[...] * jnp.asarray(scale, BF)
    same = segment_at(lax.broadcasted_iota(jnp.int32, (rows, 1), 0), bounds_ref) == segment_at(
        lax.broadcasted_iota(jnp.int32, (1, rows), 1), bounds_ref
    )
    mixed = []
    for head in range(2):
        mine = first_head if head == 0 else jnp.logical_not(first_head)
        scores = dot_last(keys, jnp.where(mine, queries, jnp.zeros_like(queries)))
        scores = jnp.where(same, scores, NEG)
        highest = jnp.max(scores, axis=0, keepdims=True)
        exps = jnp.exp(scores - highest)
        total = jnp.sum(exps, axis=0, keepdims=True)
        probs = (exps * (1.0 / total)).astype(BF)
        probs_ref[head] = probs
        mixed.append(dot(values_turned[DH * head : DH * (head + 1)], probs))
    mixed_ref[...] = jnp.transpose(jnp.concatenate(mixed, axis=0)).astype(BF)


def pair_spec(rows, offset):
    return pl.BlockSpec((rows, PAIR), lambda pair, *_: (0, offset + pair))


def attention_forward(bounds, stacked):
    rows, width = stacked.shape[0], stacked.shape[1] // 3
    pairs = width // PAIR
    return pl.pallas_call(
        functools.partial(attention_forward_kernel, scale=1.0 / math.sqrt(DH)),
        grid_spec=pltpu.PrefetchScalarGridSpec(
            num_scalar_prefetch=1,
            grid=(pairs,),
            in_specs=[pair_spec(rows, 0), pair_spec(rows, pairs), pair_spec(rows, 2 * pairs)],
            out_specs=[
                pair_spec(rows, 0),
                pl.BlockSpec((2, rows, rows), lambda pair, bounds: (pair, 0, 0)),
            ],
        ),
        out_shape=[
            jax.ShapeDtypeStruct((rows, width), BF),
            jax.ShapeDtypeStruct((2 * pairs, rows, rows), BF),
        ],
        compiler_params=pltpu.CompilerParams(vmem_limit_bytes=VMEM_BYTES),
        cost_estimate=pl.CostEstimate(
            flops=rows * width, bytes_accessed=rows * width, transcendentals=0
        ),
        name="attention_forward",
    )(bounds, stacked, stacked, stacked)


def attention_backward_kernel(
    q_ref, k_ref, v_ref, mixed_ref, grad_ref, probs_ref, dq_ref, dk_ref, dv_ref, *, scale
):
    first_head = lax.broadcasted_iota(jnp.int32, (1, PAIR), 1) < DH
    values = v_ref[...]
    keys_turned = jnp.transpose(k_ref[...])
    picks = (
        lax.broadcasted_iota(jnp.int32, (8, PAIR), 1) // DH
        == lax.broadcasted_iota(jnp.int32, (8, PAIR), 0)
    ).astype(F32)
    queries = q_ref[...] * jnp.asarray(scale, BF)
    grads = grad_ref[...]
    weighted = lax.dot_general(
        picks,
        grads.astype(F32) * mixed_ref[...].astype(F32),
        LAST_LAST,
        preferred_element_type=F32,
        precision=lax.Precision.HIGHEST,
    )
    all_scores, all_grads, all_queries, grad_queries = [], [], [], []
    for head in range(2):
        mine = first_head if head == 0 else jnp.logical_not(first_head)
        my_grads = jnp.where(mine, grads, jnp.zeros_like(grads))
        grad_probs = dot_last(values, my_grads) - weighted[head : head + 1]
        grad_scores = (probs_ref[head].astype(F32) * grad_probs).astype(BF)
        all_scores.append(grad_scores)
        all_grads.append(my_grads)
        all_queries.append(jnp.where(mine, queries, jnp.zeros_like(queries)))
        grad_queries.append(dot(keys_turned, grad_scores)[DH * head : DH * (head + 1)])
    turned = jnp.concatenate(grad_queries, axis=0) * scale
    dq_ref[...] = jnp.transpose(turned).astype(BF)
    all_probs = jnp.concatenate([probs_ref[0], probs_ref[1]], axis=1)
    dv_ref[...] = dot(all_probs, jnp.concatenate(all_grads, axis=0)).astype(BF)
    all_scores = jnp.concatenate(all_scores, axis=1)
    dk_ref[...] = dot(all_scores, jnp.concatenate(all_queries, axis=0)).astype(BF)


def attention_backward(stacked, mixed, grad_mixed, probs):
    rows, width = mixed.shape
    pairs = width // PAIR
    return pl.pallas_call(
        functools.partial(attention_backward_kernel, scale=1.0 / math.sqrt(DH)),
        grid=(pairs,),
        in_specs=[
            pair_spec(rows, 0),
            pair_spec(rows, pairs),
            pair_spec(rows, 2 * pairs),
            pair_spec(rows, 0),
            pair_spec(rows, 0),
            pl.BlockSpec((2, rows, rows), lambda pair: (pair, 0, 0)),
        ],
        out_specs=[pair_spec(rows, 0), pair_spec(rows, 0), pair_spec(rows, 0)],
        out_shape=[jax.ShapeDtypeStruct((rows, width), BF)] * 3,
        compiler_params=pltpu.CompilerParams(vmem_limit_bytes=VMEM_BYTES),
        cost_estimate=pl.CostEstimate(
            flops=rows * width, bytes_accessed=rows * width, transcendentals=0
        ),
        name="attention_backward",
    )(stacked, stacked, stacked, mixed, grad_mixed, probs)


def general_layer(
    hidden,
    lengths,
    w_qkv,
    bias_q,
    bias_v,
    w_out,
    bias_out,
    norm1_gain,
    norm1_bias,
    w_up,
    bias_up,
    w_down,
    bias_down,
    norm2_gain,
    norm2_bias,
    cotangent,
):
    count_rows, width = hidden.shape
    hidden_units = w_up.shape[1]
    n = lax.axis_size("fsdp")
    part = width // n
    inner_part = hidden_units // n
    wide = hidden_units // width
    bounds = jnp.cumsum(lengths)
    present = (jnp.arange(count_rows, dtype=jnp.int32) < bounds[-1]).astype(F32)[:, None]

    vectors = (bias_q, bias_v, bias_out, norm1_gain, norm1_bias, bias_up, bias_down, norm2_gain, norm2_bias)
    sizes = [vector.shape[0] for vector in vectors]
    starts = [sum(sizes[:i]) for i in range(len(sizes))]
    whole_qkv = lax.all_gather(w_qkv, "fsdp", axis=0, tiled=True)
    whole_vectors = lax.all_gather(jnp.concatenate(vectors)[None], "fsdp", axis=0, tiled=True)
    (
        whole_bias_q,
        whole_bias_v,
        whole_bias_out,
        whole_gain_one,
        whole_shift_one,
        whole_bias_up,
        whole_bias_down,
        whole_gain_two,
        whole_shift_two,
    ) = (
        whole_vectors[:, start : start + size].reshape(n * size).astype(F32)
        for start, size in zip(starts, sizes)
    )
    packed = jnp.concatenate(
        [w_out]
        + [w_up[:, width * i : width * (i + 1)] for i in range(wide)]
        + [w_down],
        axis=0,
    )
    gathered = lax.all_gather(packed, "fsdp", axis=0, tiled=True).reshape(n, -1, width)
    whole_out = gathered[:, :part].reshape(width, width)
    whole_up = (
        gathered[:, part : part * (1 + wide)]
        .reshape(n, wide, part, width)
        .transpose(0, 2, 1, 3)
        .reshape(width, hidden_units)
    )
    whole_down = gathered[:, part * (1 + wide) :].reshape(hidden_units, width)

    projected = jnp.dot(hidden, whole_qkv, preferred_element_type=F32)
    whole_bias = jnp.concatenate([whole_bias_q, jnp.zeros_like(whole_bias_q), whole_bias_v])
    stacked = (projected + whole_bias).astype(BF)
    mixed, probs = attention_forward(bounds, stacked)
    branch = jnp.dot(mixed, whole_out, preferred_element_type=F32) + whole_bias_out
    first, normed_one, rstd_one = norm_forward(
        hidden.astype(F32) + branch, whole_gain_one, whole_shift_one
    )
    first_low = first.astype(BF)
    inner = jnp.dot(first_low, whole_up, preferred_element_type=F32) + whole_bias_up
    activated = jax.nn.gelu(inner, approximate=False).astype(BF)
    second = jnp.dot(activated, whole_down, preferred_element_type=F32) + whole_bias_down
    result, normed_two, rstd_two = norm_forward(first + second, whole_gain_two, whole_shift_two)
    output = result * present
    upstream = cotangent.astype(F32) * present
    grad_second, grad_gain_two, grad_shift_two = norm_backward(
        upstream, normed_two, rstd_two, whole_gain_two
    )
    grad_branch_two = grad_second.astype(BF)
    grad_w_down = jnp.einsum("rf,rd->fd", activated, grad_branch_two, preferred_element_type=F32)
    grad_bias_down = jnp.sum(grad_branch_two.astype(F32), axis=0)
    grad_activated = jnp.einsum(
        "rd,fd->rf", grad_branch_two, whole_down, preferred_element_type=F32
    )
    grad_inner = (grad_activated * gelu_slope(inner)).astype(BF)
    grad_w_up = jnp.einsum("rd,rf->df", first_low, grad_inner, preferred_element_type=F32)
    grad_bias_up = jnp.sum(grad_inner.astype(F32), axis=0)
    grad_first = grad_second + jnp.einsum(
        "rf,df->rd", grad_inner, whole_up, preferred_element_type=F32
    )
    grad_sum_one, grad_gain_one, grad_shift_one = norm_backward(
        grad_first, normed_one, rstd_one, whole_gain_one
    )
    grad_branch_one = grad_sum_one.astype(BF)
    grad_w_out = jnp.einsum("rd,re->de", mixed, grad_branch_one, preferred_element_type=F32)
    grad_bias_out = jnp.sum(grad_branch_one.astype(F32), axis=0)
    grad_mixed = jnp.einsum(
        "re,de->rd", grad_branch_one, whole_out, preferred_element_type=F32
    ).astype(BF)
    grads_packed = jnp.concatenate(
        [
            grad_w_out.astype(BF).reshape(n, part, width),
            grad_w_up.astype(BF)
            .reshape(n, part, wide, width)
            .transpose(0, 2, 1, 3)
            .reshape(n, wide * part, width),
            grad_w_down.astype(BF).reshape(n, inner_part, width),
        ],
        axis=1,
    )
    summed = lax.psum_scatter(
        grads_packed.reshape(-1, width), "fsdp", scatter_dimension=0, tiled=True
    ).astype(F32)
    my_out = summed[:part]
    my_up = (
        summed[part : part * (1 + wide)]
        .reshape(wide, part, width)
        .transpose(1, 0, 2)
        .reshape(part, hidden_units)
    )
    my_down = summed[part * (1 + wide) :]

    grad_stack = jnp.concatenate(
        attention_backward(stacked, mixed, grad_mixed, probs), axis=1
    )
    grad_w_qkv = jnp.einsum("rd,re->de", hidden, grad_stack, preferred_element_type=F32)
    stack_sums = jnp.sum(grad_stack.astype(F32), axis=0)
    grad_hidden = grad_sum_one + jnp.einsum(
        "re,de->rd", grad_stack, whole_qkv, preferred_element_type=F32
    )
    vector_grads = jnp.concatenate(
        [
            grad.reshape(n, -1)
            for grad in (
                stack_sums[:width],
                stack_sums[2 * width :],
                grad_bias_out,
                grad_gain_one,
                grad_shift_one,
                grad_bias_up,
                grad_bias_down,
                grad_gain_two,
                grad_shift_two,
            )
        ],
        axis=1,
    )
    my_qkv = lax.psum_scatter(
        grad_w_qkv.astype(BF), "fsdp", scatter_dimension=0, tiled=True
    ).astype(F32)
    every_vector = lax.psum(vector_grads, "fsdp")
    my_vectors = lax.dynamic_index_in_dim(every_vector, lax.axis_index("fsdp"), 0, keepdims=False)
    (my_bias_q, my_bias_v, my_bias_out, my_gain_one, my_shift_one, my_bias_up, my_bias_down, my_gain_two, my_shift_two) = (
        my_vectors[start : start + size] for start, size in zip(starts, sizes)
    )
    return (
        output,
        grad_hidden,
        my_qkv,
        my_bias_q,
        my_bias_v,
        my_out,
        my_bias_out,
        my_gain_one,
        my_shift_one,
        my_up,
        my_bias_up,
        my_down,
        my_bias_down,
        my_gain_two,
        my_shift_two,
    )


CHIPS = (4, 2, 2, 2)
KINDS = ((0, 0, 0), (0, 1, 0), (1, 0, 0), (1, 1, 0), (1, 1, CHIPS[0] // 2))


def coordinates(index):
    _, ys, xs, cores = CHIPS
    return (index // (cores * xs * ys), index // (cores * xs) % ys, index // cores % xs, index % cores)


def moved(array, step):
    sizes = CHIPS
    pairs = []
    for source in range(math.prod(sizes)):
        target = 0
        for place, by, size in zip(coordinates(source), step, sizes):
            target = target * size + (place + by) % size
        pairs.append((source, target))
    return lax.ppermute(array, "fsdp", pairs)


def pack_weights_kernel(down_ref, up_ref, out_ref, packed_ref):
    width = down_ref.shape[1]
    wide = up_ref.shape[1] // width
    parts = [down_ref[...]] + [up_ref[:, width * i : width * (i + 1)] for i in range(wide)]
    parts = [part.astype(F32) for part in parts + [out_ref[...]]]
    fill = packed_ref.shape[0] - sum(part.shape[0] for part in parts)
    parts.append(jnp.zeros((fill, width), F32))
    packed_ref[...] = jnp.concatenate(parts, axis=0).astype(BF)


def pack_weights(w_down, w_up, w_out):
    rows = w_down.shape[0] + w_up.size // w_out.shape[1] + w_out.shape[0]
    return pl.pallas_call(
        pack_weights_kernel,
        out_shape=jax.ShapeDtypeStruct((rows + -rows % 16, w_out.shape[1]), BF),
        name="pack_weights",
    )(w_down, w_up, w_out)


def pack_front_kernel(qkv_ref, vector_ref, up_ref, packed_ref):
    width = packed_ref.shape[1]
    parts = [qkv_ref[:, width * i : width * (i + 1)].astype(F32) for i in range(3)]
    extra = jnp.zeros((8, width), F32)
    lanes = lax.broadcasted_iota(jnp.int32, (8, PAIR), 1)
    rows = lax.broadcasted_iota(jnp.int32, (8, PAIR), 0)
    part, inner_part = vector_ref.shape[1], up_ref.shape[1]
    vectors = jnp.concatenate(
        [vector_ref[...].astype(F32), jnp.zeros((8, PAIR - part), F32)], axis=1
    )
    long = jnp.concatenate([up_ref[...].astype(F32), jnp.zeros((1, PAIR - inner_part), F32)], axis=1)
    long = jnp.where((rows == 0) & (lanes < inner_part), long, 0.0)
    extra = jnp.concatenate([vectors, long, extra[:, 2 * PAIR :]], axis=1)
    packed_ref[...] = jnp.concatenate(parts + [extra], axis=0).astype(BF)


def pack_front(w_qkv, vectors, bias_up):
    part, width = w_qkv.shape[0], w_qkv.shape[1] // 3
    return pl.pallas_call(
        pack_front_kernel,
        out_shape=jax.ShapeDtypeStruct((3 * part + 8, width), BF),
        name="pack_front",
    )(w_qkv, vectors, bias_up)


def gather_square(packed):
    column = jnp.stack([packed] + [moved(packed, (step, 0, 0, 0)) for step in range(1, CHIPS[0])])
    by_x, by_y = moved(column, NEAR[0]), moved(column, NEAR[1])
    half = CHIPS[0] // 2
    pieces = [column, by_x, by_y, moved(by_x[:half], NEAR[1]), moved(by_y[half:], NEAR[0])]
    return pieces + [moved(piece, (0, 0, 0, 1)) for piece in pieces]


NEAR = ((0, 0, 1, 0), (0, 1, 0, 0), (0, 1, 1, 0))


def near_sum_kernel(place_ref, *refs, cuts):
    pairs = [(refs[2 * i], refs[2 * i + 1]) for i in range(len(cuts))]
    outs = refs[2 * len(cuts) :]
    ys, xs = CHIPS[1:3]
    for out_ref, (_, step_y, step_x, _) in zip(outs, ((0, 0, 0, 0),) + NEAR):
        chip = (place_ref[1] + step_y) % ys * xs + (place_ref[2] + step_x) % xs
        for (keep_ref, came_ref), (start, size) in zip(pairs, cuts):
            total = keep_ref[chip].astype(F32) + came_ref[chip].astype(F32)
            out_ref[0, start : start + size, :] = total.astype(BF)


def near_sum(place, *pairs):
    zs, ys, xs, _ = CHIPS
    near = ys * xs
    sizes = [keep.shape[1] for keep, _ in pairs]
    cuts = [(sum(sizes[:i]), size) for i, size in enumerate(sizes)]
    width = pairs[0][0].shape[2]
    out = jax.ShapeDtypeStruct((zs, sum(sizes), width), BF)
    return pl.pallas_call(
        functools.partial(near_sum_kernel, cuts=cuts),
        grid_spec=pltpu.PrefetchScalarGridSpec(
            num_scalar_prefetch=1,
            grid=(zs,),
            in_specs=[
                pl.BlockSpec((near, size, width), lambda step, place: (step, 0, 0))
                for size in sizes
                for _ in range(2)
            ],
            out_specs=[pl.BlockSpec((1, sum(sizes), width), lambda step, place: (step, 0, 0))] * 4,
        ),
        out_shape=[out] * 4,
        compiler_params=params(24),
        cost_estimate=pl.CostEstimate(
            flops=out.size, bytes_accessed=out.size, transcendentals=0
        ),
        name="near_sum",
    )(place, *(array for pair in pairs for array in pair))


def first_sum_kernel(place_ref, *refs, cuts):
    keep_ref, by_x_ref, by_y_ref = refs[2 * len(cuts) :]
    _, ys, xs, _ = CHIPS
    y, x = place_ref[1], place_ref[2]
    low = pl.program_id(0) < CHIPS[0] // 2

    def total(pair, chip):
        return (refs[2 * pair][chip].astype(F32) + refs[2 * pair + 1][chip].astype(F32)).astype(BF)

    for other in range(2):
        mine = jnp.where(low, other * xs + x, y * xs + other)
        theirs = jnp.where(low, other * xs + (x + 1) % xs, (y + 1) % ys * xs + other)
        for pair, (start, size) in enumerate(cuts):
            rows = slice(start, start + size)
            keep_ref[0, other, rows, :] = total(pair, mine)

            @pl.when(low)
            def _():
                by_x_ref[0, other, rows, :] = total(pair, theirs)

            @pl.when(jnp.logical_not(low))
            def _():
                by_y_ref[0, other, rows, :] = total(pair, theirs)


def halves(block):
    half = CHIPS[0] // 2
    rest = (0,) * (len(block) - 1)
    low = pl.BlockSpec(block, lambda step, place: (jnp.minimum(step, half - 1),) + rest)
    high = pl.BlockSpec(block, lambda step, place: (jnp.maximum(step - half, 0),) + rest)
    return low, high


def first_sum(place, *pairs):
    zs, ys, xs, _ = CHIPS
    sizes = [keep.shape[1] for keep, _ in pairs]
    cuts = [(sum(sizes[:i]), size) for i, size in enumerate(sizes)]
    width = pairs[0][0].shape[2]
    block = (1, 2, sum(sizes), width)
    keep = jax.ShapeDtypeStruct((zs,) + block[1:], BF)
    send = jax.ShapeDtypeStruct((zs // 2,) + block[1:], BF)
    return pl.pallas_call(
        functools.partial(first_sum_kernel, cuts=cuts),
        grid_spec=pltpu.PrefetchScalarGridSpec(
            num_scalar_prefetch=1,
            grid=(zs,),
            in_specs=[
                pl.BlockSpec((ys * xs, size, width), lambda step, place: (step, 0, 0))
                for size in sizes
                for _ in range(2)
            ],
            out_specs=[pl.BlockSpec(block, lambda step, place: (step, 0, 0, 0)), *halves(block)],
        ),
        out_shape=[keep, send, send],
        compiler_params=params(24),
        cost_estimate=pl.CostEstimate(flops=keep.size, bytes_accessed=keep.size, transcendentals=0),
        name="first_sum",
    )(place, *(array for pair in pairs for array in pair))


def second_sum_kernel(place_ref, keep_ref, from_x_ref, from_y_ref, own_ref, by_y_ref, by_x_ref):
    low = pl.program_id(0) < CHIPS[0] // 2

    def go(came_ref, own, send_ref):
        def total(index):
            return (keep_ref[0, index].astype(F32) + came_ref[0, index].astype(F32)).astype(BF)

        own_ref[0] = total(own)
        send_ref[0] = total(1 - own)

    @pl.when(low)
    def _():
        go(from_x_ref, place_ref[1], by_y_ref)

    @pl.when(jnp.logical_not(low))
    def _():
        go(from_y_ref, place_ref[2], by_x_ref)


def second_sum(place, keep, from_x, from_y):
    zs = CHIPS[0]
    block = (1,) + keep.shape[2:]
    own = jax.ShapeDtypeStruct((zs,) + block[1:], BF)
    send = jax.ShapeDtypeStruct((zs // 2,) + block[1:], BF)
    return pl.pallas_call(
        second_sum_kernel,
        grid_spec=pltpu.PrefetchScalarGridSpec(
            num_scalar_prefetch=1,
            grid=(zs,),
            in_specs=[
                pl.BlockSpec((1,) + keep.shape[1:], lambda step, place: (step, 0, 0, 0)),
                *halves((1,) + keep.shape[1:]),
            ],
            out_specs=[pl.BlockSpec(block, lambda step, place: (step, 0, 0)), *halves(block)],
        ),
        out_shape=[own, send, send],
        compiler_params=params(24),
        cost_estimate=pl.CostEstimate(flops=own.size, bytes_accessed=own.size, transcendentals=0),
        name="second_sum",
    )(place, keep, from_x, from_y)


def send_near(sends):
    return [moved(array, step) for array, step in zip(sends, NEAR)]


def far_add(own, low, high):
    return (own.astype(F32) + jnp.concatenate([low, high]).astype(F32)).astype(BF)


def far_scatter(total):
    zs, ys, xs, cores = CHIPS
    across = ys * xs * cores
    groups = [[level * across + i for level in range(zs)] for i in range(across)]
    return lax.psum_scatter(
        total, "fsdp", scatter_dimension=0, axis_index_groups=groups, tiled=False
    ).astype(F32)


def reduce_far(parts, place):
    z, zs = place[0], CHIPS[0]

    def at(level):
        return sum(
            lax.dynamic_index_in_dim(part, level, 0, keepdims=False).astype(F32) for part in parts
        )

    return at(z), [at((z + step) % zs).astype(BF) for step in range(1, zs)]


def send_far(sends):
    return [moved(array, (step, 0, 0, 0)) for step, array in enumerate(sends, 1)]


def total_of(mine, came):
    return mine + sum(array.astype(F32) for array in came)


def after(value, *first):
    return lax.optimization_barrier((value, *first))[0]


def params(megabytes):
    return pltpu.CompilerParams(vmem_limit_bytes=megabytes * 2**20)


def whole_block(array):
    return pl.BlockSpec(array.shape, lambda *step: (0,) * array.ndim)


def project_kernel(
    place_ref, hidden_ref, *refs, part, inner_part
):
    pieces = refs[: len(refs) - 5]
    stacked_ref, weight_ref, vector_ref, up_ref, turned_ref = refs[len(refs) - 5 :]
    z, y, x, core = (place_ref[i] for i in range(4))
    zs, ys, xs, cores = CHIPS
    width = hidden_ref.shape[1]
    lanes = lax.broadcasted_iota(jnp.int32, (8, width), 1)
    up_lanes = lax.broadcasted_iota(jnp.int32, (8, up_ref.shape[1]), 1)
    vectors = jnp.zeros((8, width), F32)
    ups = jnp.zeros(up_ref.shape, F32)
    for kind, (step_y, step_x, first_z) in enumerate(KINDS):
        for level in range(pieces[kind].shape[0]):
            step_z = first_z + level
            chip = ((z + zs - step_z) % zs * ys + (y + step_y) % ys) * xs + (x + step_x) % xs
            mine = pieces[kind][level].astype(F32)
            other = pieces[len(KINDS) + kind][level].astype(F32)
            low = jnp.where(core == 0, mine, other)
            high = jnp.where(core == 0, other, mine)
            rows = pl.ds(pl.multiple_of(chip * (cores * part), cores * part), cores * part)
            for third in range(3):
                cut = slice(third * part, (third + 1) * part)
                weight_ref[rows, third * width : (third + 1) * width] = jnp.concatenate(
                    [low[cut], high[cut]], axis=0
                ).astype(BF)
            for owner, piece in ((chip * cores, low), (chip * cores + 1, high)):
                extra = piece[3 * part :]
                vectors += pltpu.roll(jnp.where(lanes < part, extra, 0.0), owner * part, 1)
                long = jnp.concatenate(
                    [extra[:, PAIR:]] + [jnp.zeros((8, up_ref.shape[1] - width + PAIR), F32)], axis=1
                )
                ups += pltpu.roll(jnp.where(up_lanes < inner_part, long, 0.0), owner * inner_part, 1)
    vector_ref[...] = vectors
    up_ref[...] = ups
    hidden = hidden_ref[...]
    turned_ref[...] = jnp.transpose(hidden)
    for third, bias in ((0, vectors[0:1]), (1, None), (2, vectors[1:2])):
        cut = slice(third * width, (third + 1) * width)
        projected = dot(hidden, weight_ref[:, cut])
        stacked_ref[:, cut] = (projected if bias is None else projected + bias).astype(BF)


def project(place, hidden, pieces, hidden_units, count):
    rows, width = hidden.shape
    outs = [
        jax.ShapeDtypeStruct((rows, 3 * width), BF),
        jax.ShapeDtypeStruct((width, 3 * width), BF),
        jax.ShapeDtypeStruct((8, width), F32),
        jax.ShapeDtypeStruct((8, hidden_units), F32),
        jax.ShapeDtypeStruct((width, rows), BF),
    ]
    return pl.pallas_call(
        functools.partial(project_kernel, part=width // count, inner_part=hidden_units // count),
        grid_spec=pltpu.PrefetchScalarGridSpec(
            num_scalar_prefetch=1,
            grid=(1,),
            in_specs=[whole_block(hidden)] + [whole_block(piece) for piece in pieces],
            out_specs=[whole_block(out) for out in outs],
        ),
        out_shape=outs,
        compiler_params=params(48),
        name="project",
    )(place, hidden, *pieces)


def gelu_and_slope(inner):
    near = 1.0 / (1.0 + (0.3275911 * ROOT_HALF) * jnp.abs(inner))
    bell = jnp.exp(-0.5 * inner * inner)
    series = 0.7107068705 + near * (-0.7265760135 + near * 0.5307027145)
    series = near * (0.127414796 + near * (-0.142248368 + near * series))
    tail = series * bell
    normal_cdf = jnp.where(inner >= 0, 1.0 - tail, tail)
    return inner * normal_cdf, normal_cdf + inner * bell * INV_ROOT_TWO_PI


def norm_back(upstream, normed, rstd_rows, gain):
    scaled = upstream * gain
    plain_mean = jnp.mean(scaled, axis=-1, keepdims=True)
    cross_mean = jnp.mean(scaled * normed, axis=-1, keepdims=True)
    return rstd_rows * (scaled - plain_mean - normed * cross_mean)


def column_sum(values):
    return jnp.sum(values, axis=0, keepdims=True)


def row_pass_kernel(
    bounds_ref, mixed_ref, hidden_ref, cotangent_ref, vector_ref, bias_up_ref, gathered_ref,
    output_ref, left_ref, right_ref, grad_sum_ref, grad_mixed_ref, sums_ref, up_sums_ref,
    w_out, w_up, w_down, staged, slope, sems, *, part, chunk
):
    step = pl.program_id(0)
    span, width = mixed_ref.shape
    count, inner_part = w_down.shape[0], w_down.shape[1]
    hidden_units = w_up.shape[1]
    wide = hidden_units // width

    batch = count // 4
    copies = [
        pltpu.make_async_copy(
            gathered_ref.at[pl.ds(start, batch), pl.ds(inner_part, staged.shape[1])],
            staged.at[pl.ds(start, batch)],
            sems.at[1 + start // batch],
        )
        for start in range(0, count, batch)
    ]
    down_copy = pltpu.make_async_copy(
        gathered_ref.at[:, pl.ds(0, inner_part)], w_down, sems.at[0]
    )

    @pl.when(step == 0)
    def _():
        for copy in copies + [down_copy]:
            copy.start()
        for pair in range(count // 2):
            if 2 * pair % batch == 0:
                copies[2 * pair // batch].wait()
            low = staged[2 * pair].astype(F32)
            high = staged[2 * pair + 1].astype(F32)
            rows = slice(2 * pair * part, 2 * (pair + 1) * part)
            for group in range(wide + 1):
                cut = slice(group * part, (group + 1) * part)
                both = jnp.concatenate([low[cut], high[cut]], axis=0).astype(BF)
                if group < wide:
                    w_up[rows, group * width : (group + 1) * width] = both
                else:
                    w_out[rows, :] = both

    def down_rows(cut):
        owners = slice(cut.start // inner_part, cut.stop // inner_part)
        return w_down[owners].reshape(cut.stop - cut.start, width)

    bias_out, gain_one, shift_one, bias_down, gain_two, shift_two = (
        vector_ref[i : i + 1, :] for i in range(2, 8)
    )
    mixed = mixed_ref[...]
    branch = dot(mixed, w_out[...]) + bias_out
    first, normed_one, rstd_one = norm_forward(
        hidden_ref[...].astype(F32) + branch, gain_one, shift_one
    )
    first_low = first.astype(BF)
    left_ref[hidden_units : hidden_units + width, :] = jnp.transpose(first_low)
    left_ref[hidden_units + width :, :] = jnp.transpose(mixed)
    cuts = [slice(start, start + chunk) for start in range(0, hidden_units, chunk)]
    second = jnp.zeros(first.shape, F32)
    for cut in cuts:
        inner = dot(first_low, w_up[:, cut]) + bias_up_ref[0:1, cut]
        activated, slopes = gelu_and_slope(inner)
        activated = activated.astype(BF)
        slope[:, cut] = slopes
        left_ref[cut, :] = jnp.transpose(activated)
        if cut.start == 0:

            @pl.when(step == 0)
            def _():
                down_copy.wait()

        second += dot(activated, down_rows(cut))
    result, normed_two, rstd_two = norm_forward(
        first + (second + bias_down), gain_two, shift_two
    )
    row = lax.broadcasted_iota(jnp.int32, (span, 1), 0) + step * span
    present = (row < bounds_ref[bounds_ref.shape[0] - 1]).astype(F32)
    output_ref[...] = result * present
    upstream = cotangent_ref[...].astype(F32) * present
    grad_second = norm_back(upstream, normed_two, rstd_two, gain_two)
    grad_second_low = grad_second.astype(BF)
    right_ref[:, :width] = grad_second_low
    grad_first = grad_second
    up_sums = []
    for cut in cuts:
        grad_activated = dot_last(grad_second_low, down_rows(cut))
        grad_inner = (grad_activated * slope[:, cut]).astype(BF)
        right_ref[:, width + cut.start : width + cut.stop] = grad_inner
        up_sums.append(column_sum(grad_inner.astype(F32)))
        grad_first += dot_last(grad_inner, w_up[:, cut])
    grad_sum = norm_back(grad_first, normed_one, rstd_one, gain_one)
    grad_sum_ref[...] = grad_sum
    grad_branch = grad_sum.astype(BF)
    right_ref[:, width + hidden_units :] = grad_branch
    grad_mixed_ref[...] = dot_last(grad_branch, w_out[...]).astype(BF)
    sums = jnp.concatenate(
        [
            column_sum(grad_branch.astype(F32)),
            column_sum(grad_first * normed_one),
            column_sum(grad_first),
            column_sum(grad_second_low.astype(F32)),
            column_sum(upstream * normed_two),
            column_sum(upstream),
            jnp.zeros((2, width), F32),
        ],
        axis=0,
    )
    up_sums = jnp.concatenate(
        [jnp.concatenate(up_sums, axis=1), jnp.zeros((7, hidden_units), F32)], axis=0
    )

    @pl.when(step == 0)
    def _():
        sums_ref[...] = sums
        up_sums_ref[...] = up_sums

    @pl.when(step > 0)
    def _():
        sums_ref[...] += sums
        up_sums_ref[...] += up_sums


def row_pass(bounds, mixed, hidden, cotangent, vectors, bias_up, gathered, inner_part, span=256, chunk=768):
    rows, width = mixed.shape
    hidden_units = bias_up.shape[1]
    count = gathered.shape[0]
    part = width // count
    row_spec = pl.BlockSpec((span, width), lambda step, bounds: (step, 0))
    stacked = hidden_units + 2 * width
    shape = jax.ShapeDtypeStruct
    sums = shape((8, width), F32)
    up_sums = shape((8, hidden_units), F32)
    staged_rows = gathered.shape[1] - inner_part
    return pl.pallas_call(
        functools.partial(row_pass_kernel, part=part, chunk=chunk),
        grid_spec=pltpu.PrefetchScalarGridSpec(
            num_scalar_prefetch=1,
            grid=(rows // span,),
            in_specs=[
                row_spec,
                row_spec,
                row_spec,
                whole_block(vectors),
                whole_block(bias_up),
                pl.BlockSpec(memory_space=pl.ANY),
            ],
            out_specs=[
                row_spec,
                pl.BlockSpec((stacked, span), lambda step, bounds: (0, step)),
                pl.BlockSpec((span, stacked), lambda step, bounds: (step, 0)),
                row_spec,
                row_spec,
                whole_block(sums),
                whole_block(up_sums),
            ],
            scratch_shapes=[
                pltpu.VMEM((width, width), BF),
                pltpu.VMEM((width, hidden_units), BF),
                pltpu.VMEM((count, inner_part, width), BF),
                pltpu.VMEM((count, staged_rows, width), BF),
                pltpu.VMEM((span, hidden_units), F32),
                pltpu.SemaphoreType.DMA((5,)),
            ],
        ),
        out_shape=[
            shape((rows, width), F32),
            shape((stacked, rows), BF),
            shape((rows, stacked), BF),
            shape((rows, width), F32),
            shape((rows, width), BF),
            sums,
            up_sums,
        ],
        compiler_params=params(60),
        cost_estimate=pl.CostEstimate(
            flops=2 * rows * width * (4 * hidden_units + 2 * width),
            bytes_accessed=40 * rows * width,
            transcendentals=0,
        ),
        name="row_pass",
    )(bounds, mixed, hidden, cotangent, vectors, bias_up, gathered)


def split_owners(place_ref, keep_ref, send_ref, tile_of, count, lead=()):
    first = place_ref[3] == 0
    for chip in range(count // 2):
        even, odd = tile_of(2 * chip), tile_of(2 * chip + 1)
        keep_ref[(chip,) + lead] = jnp.where(first, even, odd).astype(BF)
        send_ref[(chip,) + lead] = jnp.where(first, odd, even).astype(BF)


def down_grad_kernel(place_ref, left_ref, right_ref, keep_ref, send_ref):
    part = keep_ref.shape[1]
    product = dot(left_ref[...], right_ref[...])
    count = product.shape[0] // part
    split_owners(place_ref, keep_ref, send_ref, lambda o: product[o * part : (o + 1) * part], count)


def down_grad(place, left, right, width, count):
    rows = left.shape[1]
    steps = left.shape[0] // width - 2
    part = steps * width // count
    half = count // 2
    spec = pl.BlockSpec((half // steps, part, width), lambda step, place: (step, 0, 0))
    return pl.pallas_call(
        down_grad_kernel,
        grid_spec=pltpu.PrefetchScalarGridSpec(
            num_scalar_prefetch=1,
            grid=(steps,),
            in_specs=[
                pl.BlockSpec((width, rows), lambda step, place: (step, 0)),
                pl.BlockSpec((rows, width), lambda step, place: (0, 0)),
            ],
            out_specs=[spec, spec],
        ),
        out_shape=[jax.ShapeDtypeStruct((half, part, width), BF)] * 2,
        compiler_params=params(48),
        cost_estimate=pl.CostEstimate(
            flops=rows * width, bytes_accessed=rows * width, transcendentals=0
        ),
        name="grad_w_down",
    )(place, left, right)


def up_grad_kernel(place_ref, left_ref, right_ref, keep_ref, send_ref):
    part = keep_ref.shape[2]
    product = dot(left_ref[...], right_ref[...])
    count = product.shape[0] // part
    split_owners(
        place_ref, keep_ref, send_ref, lambda o: product[o * part : (o + 1) * part], count, (0,)
    )


def up_grad(place, left, right, width, count):
    rows = left.shape[1]
    wide = left.shape[0] // width - 2
    half, part = count // 2, width // count
    spec = pl.BlockSpec((half, 1, part, width), lambda step, place: (0, step, 0, 0))
    return pl.pallas_call(
        up_grad_kernel,
        grid_spec=pltpu.PrefetchScalarGridSpec(
            num_scalar_prefetch=1,
            grid=(wide + 1,),
            in_specs=[
                pl.BlockSpec((width, rows), lambda step, place: (wide + step // wide, 0)),
                pl.BlockSpec((rows, width), lambda step, place: (0, 1 + step)),
            ],
            out_specs=[spec, spec],
        ),
        out_shape=[jax.ShapeDtypeStruct((half, wide + 1, part, width), BF)] * 2,
        compiler_params=params(48),
        cost_estimate=pl.CostEstimate(
            flops=rows * width, bytes_accessed=rows * width, transcendentals=0
        ),
        name="grad_w_up_out",
    )(place, left, right)


def qkv_grad_kernel(place_ref, turned_ref, sums_ref, up_sums_ref, *refs, part, inner_part):
    long_refs, short_refs = refs[-4:-2], refs[-2:]
    stack = refs[:-4]
    each = len(stack) // 3
    width, rows = turned_ref.shape
    turned = turned_ref[...]
    ones = jnp.ones((8, rows), BF)

    def joined(left, third):
        return jnp.concatenate(
            [dot(left, ref[...]) for ref in stack[third * each : (third + 1) * each]], axis=1
        )

    products = [joined(turned, third) for third in range(3)]
    vectors = jnp.concatenate(
        [joined(ones, 0)[0:1], joined(ones, 2)[0:1], sums_ref[0:6, :]], axis=0
    )
    top = lax.broadcasted_iota(jnp.int32, (8, 1), 0) == 0

    def tile_of(owner):
        cut = slice(owner * part, (owner + 1) * part)
        own = pltpu.roll(vectors, width - owner * part, 1) if owner else vectors
        start = owner * inner_part // PAIR * PAIR
        long = jnp.concatenate(
            [up_sums_ref[:, start : start + PAIR], up_sums_ref[:, start + PAIR : start + 2 * PAIR]]
            if start + 2 * PAIR <= up_sums_ref.shape[1]
            else [up_sums_ref[:, start : start + PAIR]] * 2,
            axis=1,
        )
        shift = owner * inner_part - start
        long = pltpu.roll(long, 2 * PAIR - shift, 1) if shift else long
        extra = jnp.concatenate(
            [own[:, :PAIR], jnp.where(top, long[:, :PAIR], 0.0), jnp.zeros((8, width - 2 * PAIR), F32)],
            axis=1,
        )
        return jnp.concatenate([products[2][cut], extra], axis=0)

    def long_tile_of(owner):
        cut = slice(owner * part, (owner + 1) * part)
        return jnp.concatenate([product[cut] for product in products[:2]], axis=0)

    split_owners(place_ref, *long_refs, long_tile_of, width // part)
    split_owners(place_ref, *short_refs, tile_of, width // part)


def qkv_grad(place, turned, stack, sums, up_sums, count):
    width, rows = turned.shape
    part = width // count
    outs = [
        jax.ShapeDtypeStruct((count // 2, tall, width), BF)
        for tall in (2 * part, 2 * part, part + 8, part + 8)
    ]
    return pl.pallas_call(
        functools.partial(qkv_grad_kernel, part=part, inner_part=up_sums.shape[1] // count),
        grid_spec=pltpu.PrefetchScalarGridSpec(
            num_scalar_prefetch=1,
            grid=(1,),
            in_specs=[whole_block(array) for array in (turned, sums, up_sums, *stack)],
            out_specs=[whole_block(out) for out in outs],
        ),
        out_shape=outs,
        compiler_params=params(48),
        cost_estimate=pl.CostEstimate(
            flops=rows * width, bytes_accessed=rows * width, transcendentals=0
        ),
        name="grad_w_qkv",
    )(place, turned, sums, up_sums, *stack)


def hidden_grad_kernel(grad_sum_ref, weight_ref, *refs):
    out_ref = refs[-1]
    stack = refs[:-1]
    total = grad_sum_ref[...]
    start = 0
    for ref in stack:
        size = ref.shape[1]
        total += dot_last(ref[...], weight_ref[:, start : start + size])
        start += size
    out_ref[...] = total


def hidden_grad(grad_sum, weight, stack, span=256):
    rows, width = grad_sum.shape
    return pl.pallas_call(
        hidden_grad_kernel,
        grid=(rows // span,),
        in_specs=[pl.BlockSpec((span, width), lambda step: (step, 0)), whole_block(weight)]
        + [pl.BlockSpec((span, array.shape[1]), lambda step: (step, 0)) for array in stack],
        out_specs=pl.BlockSpec((span, width), lambda step: (step, 0)),
        out_shape=jax.ShapeDtypeStruct((rows, width), F32),
        compiler_params=params(48),
        cost_estimate=pl.CostEstimate(
            flops=rows * width, bytes_accessed=rows * width, transcendentals=0
        ),
        name="grad_hidden",
    )(grad_sum, weight, *stack)


def meshed_layer(
    hidden, lengths, w_qkv, bias_q, bias_v, w_out, bias_out, norm1_gain, norm1_bias, w_up, bias_up,
    w_down, bias_down, norm2_gain, norm2_bias, cotangent
):
    count_rows, width = hidden.shape
    hidden_units = w_up.shape[1]
    n = lax.axis_size("fsdp")
    part = width // n
    inner_part = hidden_units // n
    wide = hidden_units // width
    bounds = jnp.cumsum(lengths)
    coords = coordinates(lax.axis_index("fsdp"))
    place = jnp.stack([jnp.asarray(coord, jnp.int32) for coord in coords])

    gathered = lax.all_gather(pack_weights(w_down, w_up, w_out), "fsdp", axis=0, tiled=True)
    gathered = gathered.reshape(n, -1, width)
    vectors = jnp.stack(
        [bias_q, bias_v, bias_out, norm1_gain, norm1_bias, bias_down, norm2_gain, norm2_bias]
    )
    front = pack_front(w_qkv, vectors, bias_up[None])
    pieces = gather_square(front)
    stacked, whole_qkv, whole_vectors, whole_up_bias, hidden_turned = project(
        place, hidden, pieces, hidden_units, n
    )
    mixed, probs = attention_forward(bounds, stacked)
    output, left, right, grad_sum, grad_mixed, sums, up_sums = row_pass(
        bounds, mixed, hidden, cotangent, whole_vectors, whole_up_bias, gathered, inner_part
    )
    core = (0, 0, 0, 1)
    up_keep, up_send = up_grad(place, left, right, width, n)
    up_came = moved(up_send, core)
    down_keep, down_send = down_grad(place, after(left, up_keep), right, width, n)
    down_came = moved(down_send, core)
    up_keep, up_came = (array.reshape(n // 2, -1, width) for array in (up_keep, up_came))
    keep, by_x, by_y = first_sum(place, (down_keep, down_came), (up_keep, up_came))
    from_x, from_y = moved(by_x, NEAR[0]), moved(by_y, NEAR[1])
    stack = attention_backward(stacked, mixed, after(grad_mixed, by_x, by_y), probs)
    own, by_y, by_x = second_sum(place, keep, after(from_x, *stack), after(from_y, *stack))
    low, high = moved(by_y, NEAR[1]), moved(by_x, NEAR[0])
    long_keep, long_send, short_keep, short_send = qkv_grad(
        place, after(hidden_turned, by_x, by_y), stack, sums, up_sums, n
    )
    long_came, short_came = moved(long_send, core), moved(short_send, core)
    here, *sends = near_sum(place, (long_keep, long_came), (short_keep, short_came))
    total = far_add(own, after(low, *sends), after(high, *sends))
    grad_hidden = hidden_grad(after(grad_sum, total), whole_qkv, stack)
    total = far_scatter(total)
    qkv_parts = send_near(sends)
    qkv_mine, qkv_far = reduce_far([here] + qkv_parts, coords)
    my_up_out = total[inner_part:].reshape(wide + 1, part, width)
    my_down = total[:inner_part]
    my_up = my_up_out[:wide].transpose(1, 0, 2).reshape(part, hidden_units)
    my_out = my_up_out[wide]
    mine_qkv = total_of(
        qkv_mine, [after(came, my_up, my_out, my_down) for came in send_far(qkv_far)]
    )
    my_qkv = jnp.concatenate([mine_qkv[part * i : part * (i + 1)] for i in range(3)], axis=1)
    my_vectors = mine_qkv[3 * part :]
    my_bias_q, my_bias_v, my_bias_out, my_gain_one, my_shift_one, my_bias_down, my_gain_two, my_shift_two = (
        my_vectors[i, :part] for i in range(8)
    )
    my_bias_up = my_vectors[0, PAIR : PAIR + inner_part]
    return (
        output,
        grad_hidden,
        my_qkv,
        my_bias_q,
        my_bias_v,
        my_out,
        my_bias_out,
        my_gain_one,
        my_shift_one,
        my_up,
        my_bias_up,
        my_down,
        my_bias_down,
        my_gain_two,
        my_shift_two,
    )


def layer(*arrays):
    known = lax.axis_size("fsdp") == math.prod(CHIPS)
    return (meshed_layer if known else general_layer)(*arrays)


def solution(mesh):
    rows = P("fsdp", None)
    flat = P("fsdp")
    weights = (rows, flat, flat, rows, flat, flat, flat, rows, flat, rows, flat, flat, flat)
    return jax.shard_map(
        layer,
        mesh=mesh,
        in_specs=(rows, flat) + weights + (rows,),
        out_specs=(rows, rows) + weights,
        check_vma=False,
    )
```

```python
import functools
import math

import jax
import jax.numpy as jnp
from jax import lax
from jax.experimental import pallas as pl
from jax.experimental.pallas import tpu as pltpu
from jax.sharding import PartitionSpec as P

DH = 64
PAIR = 2 * DH
BF = jnp.bfloat16
F32 = jnp.float32
NEG = -1e30
EPSILON = 1e-05
ROOT_HALF = 0.7071067811865476
INV_ROOT_TWO_PI = 0.3989422804014327
LAST_LAST = (((1,), (1,)), ((), ()))
VMEM_BYTES = 60 * 2**20


def norm_forward(values_in, gain, shift):
    centre = jnp.mean(values_in, axis=-1, keepdims=True)
    centered = values_in - centre
    spread = jnp.mean(centered * centered, axis=-1, keepdims=True)
    rstd_rows = lax.rsqrt(spread + EPSILON)
    normed = centered * rstd_rows
    return (normed * gain + shift, normed, rstd_rows)


def norm_backward(upstream, normed, rstd_rows, gain):
    scaled = upstream * gain
    plain_mean = jnp.mean(scaled, axis=-1, keepdims=True)
    cross_mean = jnp.mean(scaled * normed, axis=-1, keepdims=True)
    grad_in = rstd_rows * (scaled - plain_mean - normed * cross_mean)
    return (grad_in, jnp.sum(upstream * normed, axis=0), jnp.sum(upstream, axis=0))


def gelu_slope(inner):
    normal_cdf = 0.5 * (1.0 + lax.erf(inner * ROOT_HALF))
    return normal_cdf + inner * jnp.exp(-0.5 * inner * inner) * INV_ROOT_TWO_PI


def dot_last(a, b):
    return lax.dot_general(a, b, LAST_LAST, preferred_element_type=F32)


def dot(a, b):
    return jnp.dot(a, b, preferred_element_type=F32)


def segment_at(position, bounds_ref):
    segment = jnp.zeros(position.shape, jnp.int32)
    for index in range(bounds_ref.shape[0]):
        segment += (position >= bounds_ref[index]).astype(jnp.int32)
    return segment


def attention_forward_kernel(bounds_ref, q_ref, k_ref, v_ref, mixed_ref, probs_ref, *, scale):
    rows = q_ref.shape[0]
    first_head = lax.broadcasted_iota(jnp.int32, (1, PAIR), 1) < DH
    keys = k_ref[...]
    values_turned = jnp.transpose(v_ref[...])
    queries = q_ref[...] * jnp.asarray(scale, BF)
    same = segment_at(lax.broadcasted_iota(jnp.int32, (rows, 1), 0), bounds_ref) == segment_at(
        lax.broadcasted_iota(jnp.int32, (1, rows), 1), bounds_ref
    )
    mixed = []
    for head in range(2):
        mine = first_head if head == 0 else jnp.logical_not(first_head)
        scores = dot_last(keys, jnp.where(mine, queries, jnp.zeros_like(queries)))
        scores = jnp.where(same, scores, NEG)
        highest = jnp.max(scores, axis=0, keepdims=True)
        exps = jnp.exp(scores - highest)
        total = jnp.sum(exps, axis=0, keepdims=True)
        probs = (exps * (1.0 / total)).astype(BF)
        probs_ref[head] = probs
        mixed.append(dot(values_turned[DH * head : DH * (head + 1)], probs))
    mixed_ref[...] = jnp.transpose(jnp.concatenate(mixed, axis=0)).astype(BF)


def pair_spec(rows, offset):
    return pl.BlockSpec((rows, PAIR), lambda pair, *_: (0, offset + pair))


def attention_forward(bounds, stacked):
    rows, width = stacked.shape[0], stacked.shape[1] // 3
    pairs = width // PAIR
    return pl.pallas_call(
        functools.partial(attention_forward_kernel, scale=1.0 / math.sqrt(DH)),
        grid_spec=pltpu.PrefetchScalarGridSpec(
            num_scalar_prefetch=1,
            grid=(pairs,),
            in_specs=[pair_spec(rows, 0), pair_spec(rows, pairs), pair_spec(rows, 2 * pairs)],
            out_specs=[
                pair_spec(rows, 0),
                pl.BlockSpec((2, rows, rows), lambda pair, bounds: (pair, 0, 0)),
            ],
        ),
        out_shape=[
            jax.ShapeDtypeStruct((rows, width), BF),
            jax.ShapeDtypeStruct((2 * pairs, rows, rows), BF),
        ],
        compiler_params=pltpu.CompilerParams(vmem_limit_bytes=VMEM_BYTES),
        cost_estimate=pl.CostEstimate(
            flops=rows * width, bytes_accessed=rows * width, transcendentals=0
        ),
        name="attention_forward",
    )(bounds, stacked, stacked, stacked)


def attention_backward_kernel(
    q_ref, k_ref, v_ref, mixed_ref, grad_ref, probs_ref, dq_ref, dk_ref, dv_ref, *, scale
):
    first_head = lax.broadcasted_iota(jnp.int32, (1, PAIR), 1) < DH
    values = v_ref[...]
    keys_turned = jnp.transpose(k_ref[...])
    picks = (
        lax.broadcasted_iota(jnp.int32, (8, PAIR), 1) // DH
        == lax.broadcasted_iota(jnp.int32, (8, PAIR), 0)
    ).astype(F32)
    queries = q_ref[...] * jnp.asarray(scale, BF)
    grads = grad_ref[...]
    weighted = lax.dot_general(
        picks,
        grads.astype(F32) * mixed_ref[...].astype(F32),
        LAST_LAST,
        preferred_element_type=F32,
        precision=lax.Precision.HIGHEST,
    )
    all_scores, all_grads, all_queries, grad_queries = [], [], [], []
    for head in range(2):
        mine = first_head if head == 0 else jnp.logical_not(first_head)
        my_grads = jnp.where(mine, grads, jnp.zeros_like(grads))
        grad_probs = dot_last(values, my_grads) - weighted[head : head + 1]
        grad_scores = (probs_ref[head].astype(F32) * grad_probs).astype(BF)
        all_scores.append(grad_scores)
        all_grads.append(my_grads)
        all_queries.append(jnp.where(mine, queries, jnp.zeros_like(queries)))
        grad_queries.append(dot(keys_turned, grad_scores)[DH * head : DH * (head + 1)])
    turned = jnp.concatenate(grad_queries, axis=0) * scale
    dq_ref[...] = jnp.transpose(turned).astype(BF)
    all_probs = jnp.concatenate([probs_ref[0], probs_ref[1]], axis=1)
    dv_ref[...] = dot(all_probs, jnp.concatenate(all_grads, axis=0)).astype(BF)
    all_scores = jnp.concatenate(all_scores, axis=1)
    dk_ref[...] = dot(all_scores, jnp.concatenate(all_queries, axis=0)).astype(BF)


def attention_backward(stacked, mixed, grad_mixed, probs):
    rows, width = mixed.shape
    pairs = width // PAIR
    return pl.pallas_call(
        functools.partial(attention_backward_kernel, scale=1.0 / math.sqrt(DH)),
        grid=(pairs,),
        in_specs=[
            pair_spec(rows, 0),
            pair_spec(rows, pairs),
            pair_spec(rows, 2 * pairs),
            pair_spec(rows, 0),
            pair_spec(rows, 0),
            pl.BlockSpec((2, rows, rows), lambda pair: (pair, 0, 0)),
        ],
        out_specs=[pair_spec(rows, 0), pair_spec(rows, 0), pair_spec(rows, 0)],
        out_shape=[jax.ShapeDtypeStruct((rows, width), BF)] * 3,
        compiler_params=pltpu.CompilerParams(vmem_limit_bytes=VMEM_BYTES),
        cost_estimate=pl.CostEstimate(
            flops=rows * width, bytes_accessed=rows * width, transcendentals=0
        ),
        name="attention_backward",
    )(stacked, stacked, stacked, mixed, grad_mixed, probs)


def general_layer(
    hidden,
    lengths,
    w_qkv,
    bias_q,
    bias_v,
    w_out,
    bias_out,
    norm1_gain,
    norm1_bias,
    w_up,
    bias_up,
    w_down,
    bias_down,
    norm2_gain,
    norm2_bias,
    cotangent,
):
    count_rows, width = hidden.shape
    hidden_units = w_up.shape[1]
    n = lax.axis_size("fsdp")
    part = width // n
    inner_part = hidden_units // n
    wide = hidden_units // width
    bounds = jnp.cumsum(lengths)
    present = (jnp.arange(count_rows, dtype=jnp.int32) < bounds[-1]).astype(F32)[:, None]

    vectors = (bias_q, bias_v, bias_out, norm1_gain, norm1_bias, bias_up, bias_down, norm2_gain, norm2_bias)
    sizes = [vector.shape[0] for vector in vectors]
    starts = [sum(sizes[:i]) for i in range(len(sizes))]
    whole_qkv = lax.all_gather(w_qkv, "fsdp", axis=0, tiled=True)
    whole_vectors = lax.all_gather(jnp.concatenate(vectors)[None], "fsdp", axis=0, tiled=True)
    (
        whole_bias_q,
        whole_bias_v,
        whole_bias_out,
        whole_gain_one,
        whole_shift_one,
        whole_bias_up,
        whole_bias_down,
        whole_gain_two,
        whole_shift_two,
    ) = (
        whole_vectors[:, start : start + size].reshape(n * size).astype(F32)
        for start, size in zip(starts, sizes)
    )
    packed = jnp.concatenate(
        [w_out]
        + [w_up[:, width * i : width * (i + 1)] for i in range(wide)]
        + [w_down],
        axis=0,
    )
    gathered = lax.all_gather(packed, "fsdp", axis=0, tiled=True).reshape(n, -1, width)
    whole_out = gathered[:, :part].reshape(width, width)
    whole_up = (
        gathered[:, part : part * (1 + wide)]
        .reshape(n, wide, part, width)
        .transpose(0, 2, 1, 3)
        .reshape(width, hidden_units)
    )
    whole_down = gathered[:, part * (1 + wide) :].reshape(hidden_units, width)

    projected = jnp.dot(hidden, whole_qkv, preferred_element_type=F32)
    whole_bias = jnp.concatenate([whole_bias_q, jnp.zeros_like(whole_bias_q), whole_bias_v])
    stacked = (projected + whole_bias).astype(BF)
    mixed, probs = attention_forward(bounds, stacked)
    branch = jnp.dot(mixed, whole_out, preferred_element_type=F32) + whole_bias_out
    first, normed_one, rstd_one = norm_forward(
        hidden.astype(F32) + branch, whole_gain_one, whole_shift_one
    )
    first_low = first.astype(BF)
    inner = jnp.dot(first_low, whole_up, preferred_element_type=F32) + whole_bias_up
    activated = jax.nn.gelu(inner, approximate=False).astype(BF)
    second = jnp.dot(activated, whole_down, preferred_element_type=F32) + whole_bias_down
    result, normed_two, rstd_two = norm_forward(first + second, whole_gain_two, whole_shift_two)
    output = result * present
    upstream = cotangent.astype(F32) * present
    grad_second, grad_gain_two, grad_shift_two = norm_backward(
        upstream, normed_two, rstd_two, whole_gain_two
    )
    grad_branch_two = grad_second.astype(BF)
    grad_w_down = jnp.einsum("rf,rd->fd", activated, grad_branch_two, preferred_element_type=F32)
    grad_bias_down = jnp.sum(grad_branch_two.astype(F32), axis=0)
    grad_activated = jnp.einsum(
        "rd,fd->rf", grad_branch_two, whole_down, preferred_element_type=F32
    )
    grad_inner = (grad_activated * gelu_slope(inner)).astype(BF)
    grad_w_up = jnp.einsum("rd,rf->df", first_low, grad_inner, preferred_element_type=F32)
    grad_bias_up = jnp.sum(grad_inner.astype(F32), axis=0)
    grad_first = grad_second + jnp.einsum(
        "rf,df->rd", grad_inner, whole_up, preferred_element_type=F32
    )
    grad_sum_one, grad_gain_one, grad_shift_one = norm_backward(
        grad_first, normed_one, rstd_one, whole_gain_one
    )
    grad_branch_one = grad_sum_one.astype(BF)
    grad_w_out = jnp.einsum("rd,re->de", mixed, grad_branch_one, preferred_element_type=F32)
    grad_bias_out = jnp.sum(grad_branch_one.astype(F32), axis=0)
    grad_mixed = jnp.einsum(
        "re,de->rd", grad_branch_one, whole_out, preferred_element_type=F32
    ).astype(BF)
    grads_packed = jnp.concatenate(
        [
            grad_w_out.astype(BF).reshape(n, part, width),
            grad_w_up.astype(BF)
            .reshape(n, part, wide, width)
            .transpose(0, 2, 1, 3)
            .reshape(n, wide * part, width),
            grad_w_down.astype(BF).reshape(n, inner_part, width),
        ],
        axis=1,
    )
    summed = lax.psum_scatter(
        grads_packed.reshape(-1, width), "fsdp", scatter_dimension=0, tiled=True
    ).astype(F32)
    my_out = summed[:part]
    my_up = (
        summed[part : part * (1 + wide)]
        .reshape(wide, part, width)
        .transpose(1, 0, 2)
        .reshape(part, hidden_units)
    )
    my_down = summed[part * (1 + wide) :]

    grad_stack = jnp.concatenate(
        attention_backward(stacked, mixed, grad_mixed, probs), axis=1
    )
    grad_w_qkv = jnp.einsum("rd,re->de", hidden, grad_stack, preferred_element_type=F32)
    stack_sums = jnp.sum(grad_stack.astype(F32), axis=0)
    grad_hidden = grad_sum_one + jnp.einsum(
        "re,de->rd", grad_stack, whole_qkv, preferred_element_type=F32
    )
    vector_grads = jnp.concatenate(
        [
            grad.reshape(n, -1)
            for grad in (
                stack_sums[:width],
                stack_sums[2 * width :],
                grad_bias_out,
                grad_gain_one,
                grad_shift_one,
                grad_bias_up,
                grad_bias_down,
                grad_gain_two,
                grad_shift_two,
            )
        ],
        axis=1,
    )
    my_qkv = lax.psum_scatter(
        grad_w_qkv.astype(BF), "fsdp", scatter_dimension=0, tiled=True
    ).astype(F32)
    every_vector = lax.psum(vector_grads, "fsdp")
    my_vectors = lax.dynamic_index_in_dim(every_vector, lax.axis_index("fsdp"), 0, keepdims=False)
    (my_bias_q, my_bias_v, my_bias_out, my_gain_one, my_shift_one, my_bias_up, my_bias_down, my_gain_two, my_shift_two) = (
        my_vectors[start : start + size] for start, size in zip(starts, sizes)
    )
    return (
        output,
        grad_hidden,
        my_qkv,
        my_bias_q,
        my_bias_v,
        my_out,
        my_bias_out,
        my_gain_one,
        my_shift_one,
        my_up,
        my_bias_up,
        my_down,
        my_bias_down,
        my_gain_two,
        my_shift_two,
    )


CHIPS = (4, 2, 2, 2)
KINDS = ((0, 0, 0), (0, 1, 0), (1, 0, 0), (1, 1, 0), (1, 1, CHIPS[0] // 2))


def coordinates(index):
    _, ys, xs, cores = CHIPS
    return (index // (cores * xs * ys), index // (cores * xs) % ys, index // cores % xs, index % cores)


def moved(array, step):
    sizes = CHIPS
    pairs = []
    for source in range(math.prod(sizes)):
        target = 0
        for place, by, size in zip(coordinates(source), step, sizes):
            target = target * size + (place + by) % size
        pairs.append((source, target))
    return lax.ppermute(array, "fsdp", pairs)


def pack_weights_kernel(down_ref, up_ref, out_ref, packed_ref):
    width = down_ref.shape[1]
    wide = up_ref.shape[1] // width
    parts = [down_ref[...]] + [up_ref[:, width * i : width * (i + 1)] for i in range(wide)]
    parts = [part.astype(F32) for part in parts + [out_ref[...]]]
    fill = packed_ref.shape[0] - sum(part.shape[0] for part in parts)
    parts.append(jnp.zeros((fill, width), F32))
    packed_ref[...] = jnp.concatenate(parts, axis=0).astype(BF)


def pack_weights(w_down, w_up, w_out):
    rows = w_down.shape[0] + w_up.size // w_out.shape[1] + w_out.shape[0]
    return pl.pallas_call(
        pack_weights_kernel,
        out_shape=jax.ShapeDtypeStruct((rows + -rows % 16, w_out.shape[1]), BF),
        name="pack_weights",
    )(w_down, w_up, w_out)


def pack_front_kernel(qkv_ref, vector_ref, up_ref, packed_ref):
    width = packed_ref.shape[1]
    parts = [qkv_ref[:, width * i : width * (i + 1)].astype(F32) for i in range(3)]
    extra = jnp.zeros((8, width), F32)
    lanes = lax.broadcasted_iota(jnp.int32, (8, PAIR), 1)
    rows = lax.broadcasted_iota(jnp.int32, (8, PAIR), 0)
    part, inner_part = vector_ref.shape[1], up_ref.shape[1]
    vectors = jnp.concatenate(
        [vector_ref[...].astype(F32), jnp.zeros((8, PAIR - part), F32)], axis=1
    )
    long = jnp.concatenate([up_ref[...].astype(F32), jnp.zeros((1, PAIR - inner_part), F32)], axis=1)
    long = jnp.where((rows == 0) & (lanes < inner_part), long, 0.0)
    extra = jnp.concatenate([vectors, long, extra[:, 2 * PAIR :]], axis=1)
    packed_ref[...] = jnp.concatenate(parts + [extra], axis=0).astype(BF)


def pack_front(w_qkv, vectors, bias_up):
    part, width = w_qkv.shape[0], w_qkv.shape[1] // 3
    return pl.pallas_call(
        pack_front_kernel,
        out_shape=jax.ShapeDtypeStruct((3 * part + 8, width), BF),
        name="pack_front",
    )(w_qkv, vectors, bias_up)


def gather_square(packed):
    column = jnp.stack([packed] + [moved(packed, (step, 0, 0, 0)) for step in range(1, CHIPS[0])])
    by_x, by_y = moved(column, NEAR[0]), moved(column, NEAR[1])
    half = CHIPS[0] // 2
    pieces = [column, by_x, by_y, moved(by_x[:half], NEAR[1]), moved(by_y[half:], NEAR[0])]
    return pieces + [moved(piece, (0, 0, 0, 1)) for piece in pieces]


NEAR = ((0, 0, 1, 0), (0, 1, 0, 0), (0, 1, 1, 0))


def near_sum_kernel(place_ref, *refs, cuts):
    pairs = [(refs[2 * i], refs[2 * i + 1]) for i in range(len(cuts))]
    outs = refs[2 * len(cuts) :]
    ys, xs = CHIPS[1:3]
    for out_ref, (_, step_y, step_x, _) in zip(outs, ((0, 0, 0, 0),) + NEAR):
        chip = (place_ref[1] + step_y) % ys * xs + (place_ref[2] + step_x) % xs
        for (keep_ref, came_ref), (start, size) in zip(pairs, cuts):
            total = keep_ref[chip].astype(F32) + came_ref[chip].astype(F32)
            out_ref[0, start : start + size, :] = total.astype(BF)


def near_sum(place, *pairs):
    zs, ys, xs, _ = CHIPS
    near = ys * xs
    sizes = [keep.shape[1] for keep, _ in pairs]
    cuts = [(sum(sizes[:i]), size) for i, size in enumerate(sizes)]
    width = pairs[0][0].shape[2]
    out = jax.ShapeDtypeStruct((zs, sum(sizes), width), BF)
    return pl.pallas_call(
        functools.partial(near_sum_kernel, cuts=cuts),
        grid_spec=pltpu.PrefetchScalarGridSpec(
            num_scalar_prefetch=1,
            grid=(zs,),
            in_specs=[
                pl.BlockSpec((near, size, width), lambda step, place: (step, 0, 0))
                for size in sizes
                for _ in range(2)
            ],
            out_specs=[pl.BlockSpec((1, sum(sizes), width), lambda step, place: (step, 0, 0))] * 4,
        ),
        out_shape=[out] * 4,
        compiler_params=params(24),
        cost_estimate=pl.CostEstimate(
            flops=out.size, bytes_accessed=out.size, transcendentals=0
        ),
        name="near_sum",
    )(place, *(array for pair in pairs for array in pair))


def first_sum_kernel(place_ref, *refs, cuts):
    keep_ref, by_x_ref, by_y_ref = refs[2 * len(cuts) :]
    _, ys, xs, _ = CHIPS
    y, x = place_ref[1], place_ref[2]
    low = pl.program_id(0) < CHIPS[0] // 2

    def total(pair, chip):
        return (refs[2 * pair][chip].astype(F32) + refs[2 * pair + 1][chip].astype(F32)).astype(BF)

    for other in range(2):
        mine = jnp.where(low, other * xs + x, y * xs + other)
        theirs = jnp.where(low, other * xs + (x + 1) % xs, (y + 1) % ys * xs + other)
        for pair, (start, size) in enumerate(cuts):
            rows = slice(start, start + size)
            keep_ref[0, other, rows, :] = total(pair, mine)

            @pl.when(low)
            def _():
                by_x_ref[0, other, rows, :] = total(pair, theirs)

            @pl.when(jnp.logical_not(low))
            def _():
                by_y_ref[0, other, rows, :] = total(pair, theirs)


def halves(block):
    half = CHIPS[0] // 2
    rest = (0,) * (len(block) - 1)
    low = pl.BlockSpec(block, lambda step, place: (jnp.minimum(step, half - 1),) + rest)
    high = pl.BlockSpec(block, lambda step, place: (jnp.maximum(step - half, 0),) + rest)
    return low, high


def first_sum(place, *pairs):
    zs, ys, xs, _ = CHIPS
    sizes = [keep.shape[1] for keep, _ in pairs]
    cuts = [(sum(sizes[:i]), size) for i, size in enumerate(sizes)]
    width = pairs[0][0].shape[2]
    block = (1, 2, sum(sizes), width)
    keep = jax.ShapeDtypeStruct((zs,) + block[1:], BF)
    send = jax.ShapeDtypeStruct((zs // 2,) + block[1:], BF)
    return pl.pallas_call(
        functools.partial(first_sum_kernel, cuts=cuts),
        grid_spec=pltpu.PrefetchScalarGridSpec(
            num_scalar_prefetch=1,
            grid=(zs,),
            in_specs=[
                pl.BlockSpec((ys * xs, size, width), lambda step, place: (step, 0, 0))
                for size in sizes
                for _ in range(2)
            ],
            out_specs=[pl.BlockSpec(block, lambda step, place: (step, 0, 0, 0)), *halves(block)],
        ),
        out_shape=[keep, send, send],
        compiler_params=params(24),
        cost_estimate=pl.CostEstimate(flops=keep.size, bytes_accessed=keep.size, transcendentals=0),
        name="first_sum",
    )(place, *(array for pair in pairs for array in pair))


def second_sum_kernel(place_ref, keep_ref, from_x_ref, from_y_ref, own_ref, by_y_ref, by_x_ref):
    low = pl.program_id(0) < CHIPS[0] // 2

    def go(came_ref, own, send_ref):
        def total(index):
            return (keep_ref[0, index].astype(F32) + came_ref[0, index].astype(F32)).astype(BF)

        own_ref[0] = total(own)
        send_ref[0] = total(1 - own)

    @pl.when(low)
    def _():
        go(from_x_ref, place_ref[1], by_y_ref)

    @pl.when(jnp.logical_not(low))
    def _():
        go(from_y_ref, place_ref[2], by_x_ref)


def second_sum(place, keep, from_x, from_y):
    zs = CHIPS[0]
    block = (1,) + keep.shape[2:]
    own = jax.ShapeDtypeStruct((zs,) + block[1:], BF)
    send = jax.ShapeDtypeStruct((zs // 2,) + block[1:], BF)
    return pl.pallas_call(
        second_sum_kernel,
        grid_spec=pltpu.PrefetchScalarGridSpec(
            num_scalar_prefetch=1,
            grid=(zs,),
            in_specs=[
                pl.BlockSpec((1,) + keep.shape[1:], lambda step, place: (step, 0, 0, 0)),
                *halves((1,) + keep.shape[1:]),
            ],
            out_specs=[pl.BlockSpec(block, lambda step, place: (step, 0, 0)), *halves(block)],
        ),
        out_shape=[own, send, send],
        compiler_params=params(24),
        cost_estimate=pl.CostEstimate(flops=own.size, bytes_accessed=own.size, transcendentals=0),
        name="second_sum",
    )(place, keep, from_x, from_y)


def send_near(sends):
    return [moved(array, step) for array, step in zip(sends, NEAR)]


def far_add(own, low, high):
    return (own.astype(F32) + jnp.concatenate([low, high]).astype(F32)).astype(BF)


def far_scatter(total):
    zs, ys, xs, cores = CHIPS
    across = ys * xs * cores
    groups = [[level * across + i for level in range(zs)] for i in range(across)]
    return lax.psum_scatter(
        total, "fsdp", scatter_dimension=0, axis_index_groups=groups, tiled=False
    ).astype(F32)


def reduce_far(parts, place):
    z, zs = place[0], CHIPS[0]

    def at(level):
        return sum(
            lax.dynamic_index_in_dim(part, level, 0, keepdims=False).astype(F32) for part in parts
        )

    return at(z), [at((z + step) % zs).astype(BF) for step in range(1, zs)]


def send_far(sends):
    return [moved(array, (step, 0, 0, 0)) for step, array in enumerate(sends, 1)]


def total_of(mine, came):
    return mine + sum(array.astype(F32) for array in came)


def after(value, *first):
    return lax.optimization_barrier((value, *first))[0]


def params(megabytes):
    return pltpu.CompilerParams(vmem_limit_bytes=megabytes * 2**20)


def whole_block(array):
    return pl.BlockSpec(array.shape, lambda *step: (0,) * array.ndim)


def project_kernel(
    place_ref, hidden_ref, *refs, part, inner_part
):
    pieces = refs[: len(refs) - 5]
    stacked_ref, weight_ref, vector_ref, up_ref, turned_ref = refs[len(refs) - 5 :]
    z, y, x, core = (place_ref[i] for i in range(4))
    zs, ys, xs, cores = CHIPS
    width = hidden_ref.shape[1]
    lanes = lax.broadcasted_iota(jnp.int32, (8, width), 1)
    up_lanes = lax.broadcasted_iota(jnp.int32, (8, up_ref.shape[1]), 1)
    vectors = jnp.zeros((8, width), F32)
    ups = jnp.zeros(up_ref.shape, F32)
    for kind, (step_y, step_x, first_z) in enumerate(KINDS):
        for level in range(pieces[kind].shape[0]):
            step_z = first_z + level
            chip = ((z + zs - step_z) % zs * ys + (y + step_y) % ys) * xs + (x + step_x) % xs
            mine = pieces[kind][level].astype(F32)
            other = pieces[len(KINDS) + kind][level].astype(F32)
            low = jnp.where(core == 0, mine, other)
            high = jnp.where(core == 0, other, mine)
            rows = pl.ds(pl.multiple_of(chip * (cores * part), cores * part), cores * part)
            for third in range(3):
                cut = slice(third * part, (third + 1) * part)
                weight_ref[rows, third * width : (third + 1) * width] = jnp.concatenate(
                    [low[cut], high[cut]], axis=0
                ).astype(BF)
            for owner, piece in ((chip * cores, low), (chip * cores + 1, high)):
                extra = piece[3 * part :]
                vectors += pltpu.roll(jnp.where(lanes < part, extra, 0.0), owner * part, 1)
                long = jnp.concatenate(
                    [extra[:, PAIR:]] + [jnp.zeros((8, up_ref.shape[1] - width + PAIR), F32)], axis=1
                )
                ups += pltpu.roll(jnp.where(up_lanes < inner_part, long, 0.0), owner * inner_part, 1)
    vector_ref[...] = vectors
    up_ref[...] = ups
    hidden = hidden_ref[...]
    turned_ref[...] = jnp.transpose(hidden)
    for third, bias in ((0, vectors[0:1]), (1, None), (2, vectors[1:2])):
        cut = slice(third * width, (third + 1) * width)
        projected = dot(hidden, weight_ref[:, cut])
        stacked_ref[:, cut] = (projected if bias is None else projected + bias).astype(BF)


def project(place, hidden, pieces, hidden_units, count):
    rows, width = hidden.shape
    outs = [
        jax.ShapeDtypeStruct((rows, 3 * width), BF),
        jax.ShapeDtypeStruct((width, 3 * width), BF),
        jax.ShapeDtypeStruct((8, width), F32),
        jax.ShapeDtypeStruct((8, hidden_units), F32),
        jax.ShapeDtypeStruct((width, rows), BF),
    ]
    return pl.pallas_call(
        functools.partial(project_kernel, part=width // count, inner_part=hidden_units // count),
        grid_spec=pltpu.PrefetchScalarGridSpec(
            num_scalar_prefetch=1,
            grid=(1,),
            in_specs=[whole_block(hidden)] + [whole_block(piece) for piece in pieces],
            out_specs=[whole_block(out) for out in outs],
        ),
        out_shape=outs,
        compiler_params=params(48),
        name="project",
    )(place, hidden, *pieces)


def gelu_and_slope(inner):
    near = 1.0 / (1.0 + (0.3275911 * ROOT_HALF) * jnp.abs(inner))
    bell = jnp.exp(-0.5 * inner * inner)
    series = 0.7107068705 + near * (-0.7265760135 + near * 0.5307027145)
    series = near * (0.127414796 + near * (-0.142248368 + near * series))
    tail = series * bell
    normal_cdf = jnp.where(inner >= 0, 1.0 - tail, tail)
    return inner * normal_cdf, normal_cdf + inner * bell * INV_ROOT_TWO_PI


def norm_back(upstream, normed, rstd_rows, gain):
    scaled = upstream * gain
    plain_mean = jnp.mean(scaled, axis=-1, keepdims=True)
    cross_mean = jnp.mean(scaled * normed, axis=-1, keepdims=True)
    return rstd_rows * (scaled - plain_mean - normed * cross_mean)


def column_sum(values):
    return jnp.sum(values, axis=0, keepdims=True)


def row_pass_kernel(
    bounds_ref, mixed_ref, hidden_ref, cotangent_ref, vector_ref, bias_up_ref, gathered_ref,
    output_ref, left_ref, right_ref, grad_sum_ref, grad_mixed_ref, sums_ref, up_sums_ref,
    w_out, w_up, w_down, staged, slope, sems, *, part, chunk
):
    step = pl.program_id(0)
    span, width = mixed_ref.shape
    count, inner_part = w_down.shape[0], w_down.shape[1]
    hidden_units = w_up.shape[1]
    wide = hidden_units // width

    batch = count // 4
    copies = [
        pltpu.make_async_copy(
            gathered_ref.at[pl.ds(start, batch), pl.ds(inner_part, staged.shape[1])],
            staged.at[pl.ds(start, batch)],
            sems.at[1 + start // batch],
        )
        for start in range(0, count, batch)
    ]
    down_copy = pltpu.make_async_copy(
        gathered_ref.at[:, pl.ds(0, inner_part)], w_down, sems.at[0]
    )

    @pl.when(step == 0)
    def _():
        for copy in copies + [down_copy]:
            copy.start()
        for pair in range(count // 2):
            if 2 * pair % batch == 0:
                copies[2 * pair // batch].wait()
            low = staged[2 * pair].astype(F32)
            high = staged[2 * pair + 1].astype(F32)
            rows = slice(2 * pair * part, 2 * (pair + 1) * part)
            for group in range(wide + 1):
                cut = slice(group * part, (group + 1) * part)
                both = jnp.concatenate([low[cut], high[cut]], axis=0).astype(BF)
                if group < wide:
                    w_up[rows, group * width : (group + 1) * width] = both
                else:
                    w_out[rows, :] = both

    def down_rows(cut):
        owners = slice(cut.start // inner_part, cut.stop // inner_part)
        return w_down[owners].reshape(cut.stop - cut.start, width)

    bias_out, gain_one, shift_one, bias_down, gain_two, shift_two = (
        vector_ref[i : i + 1, :] for i in range(2, 8)
    )
    mixed = mixed_ref[...]
    branch = dot(mixed, w_out[...]) + bias_out
    first, normed_one, rstd_one = norm_forward(
        hidden_ref[...].astype(F32) + branch, gain_one, shift_one
    )
    first_low = first.astype(BF)
    left_ref[hidden_units : hidden_units + width, :] = jnp.transpose(first_low)
    left_ref[hidden_units + width :, :] = jnp.transpose(mixed)
    cuts = [slice(start, start + chunk) for start in range(0, hidden_units, chunk)]
    second = jnp.zeros(first.shape, F32)
    for cut in cuts:
        inner = dot(first_low, w_up[:, cut]) + bias_up_ref[0:1, cut]
        activated, slopes = gelu_and_slope(inner)
        activated = activated.astype(BF)
        slope[:, cut] = slopes
        left_ref[cut, :] = jnp.transpose(activated)
        if cut.start == 0:

            @pl.when(step == 0)
            def _():
                down_copy.wait()

        second += dot(activated, down_rows(cut))
    result, normed_two, rstd_two = norm_forward(
        first + (second + bias_down), gain_two, shift_two
    )
    row = lax.broadcasted_iota(jnp.int32, (span, 1), 0) + step * span
    present = (row < bounds_ref[bounds_ref.shape[0] - 1]).astype(F32)
    output_ref[...] = result * present
    upstream = cotangent_ref[...].astype(F32) * present
    grad_second = norm_back(upstream, normed_two, rstd_two, gain_two)
    grad_second_low = grad_second.astype(BF)
    right_ref[:, :width] = grad_second_low
    grad_first = grad_second
    up_sums = []
    for cut in cuts:
        grad_activated = dot_last(grad_second_low, down_rows(cut))
        grad_inner = (grad_activated * slope[:, cut]).astype(BF)
        right_ref[:, width + cut.start : width + cut.stop] = grad_inner
        up_sums.append(column_sum(grad_inner.astype(F32)))
        grad_first += dot_last(grad_inner, w_up[:, cut])
    grad_sum = norm_back(grad_first, normed_one, rstd_one, gain_one)
    grad_sum_ref[...] = grad_sum
    grad_branch = grad_sum.astype(BF)
    right_ref[:, width + hidden_units :] = grad_branch
    grad_mixed_ref[...] = dot_last(grad_branch, w_out[...]).astype(BF)
    sums = jnp.concatenate(
        [
            column_sum(grad_branch.astype(F32)),
            column_sum(grad_first * normed_one),
            column_sum(grad_first),
            column_sum(grad_second_low.astype(F32)),
            column_sum(upstream * normed_two),
            column_sum(upstream),
            jnp.zeros((2, width), F32),
        ],
        axis=0,
    )
    up_sums = jnp.concatenate(
        [jnp.concatenate(up_sums, axis=1), jnp.zeros((7, hidden_units), F32)], axis=0
    )

    @pl.when(step == 0)
    def _():
        sums_ref[...] = sums
        up_sums_ref[...] = up_sums

    @pl.when(step > 0)
    def _():
        sums_ref[...] += sums
        up_sums_ref[...] += up_sums


def row_pass(bounds, mixed, hidden, cotangent, vectors, bias_up, gathered, inner_part, span=256, chunk=768):
    rows, width = mixed.shape
    hidden_units = bias_up.shape[1]
    count = gathered.shape[0]
    part = width // count
    row_spec = pl.BlockSpec((span, width), lambda step, bounds: (step, 0))
    stacked = hidden_units + 2 * width
    shape = jax.ShapeDtypeStruct
    sums = shape((8, width), F32)
    up_sums = shape((8, hidden_units), F32)
    staged_rows = gathered.shape[1] - inner_part
    return pl.pallas_call(
        functools.partial(row_pass_kernel, part=part, chunk=chunk),
        grid_spec=pltpu.PrefetchScalarGridSpec(
            num_scalar_prefetch=1,
            grid=(rows // span,),
            in_specs=[
                row_spec,
                row_spec,
                row_spec,
                whole_block(vectors),
                whole_block(bias_up),
                pl.BlockSpec(memory_space=pl.ANY),
            ],
            out_specs=[
                row_spec,
                pl.BlockSpec((stacked, span), lambda step, bounds: (0, step)),
                pl.BlockSpec((span, stacked), lambda step, bounds: (step, 0)),
                row_spec,
                row_spec,
                whole_block(sums),
                whole_block(up_sums),
            ],
            scratch_shapes=[
                pltpu.VMEM((width, width), BF),
                pltpu.VMEM((width, hidden_units), BF),
                pltpu.VMEM((count, inner_part, width), BF),
                pltpu.VMEM((count, staged_rows, width), BF),
                pltpu.VMEM((span, hidden_units), F32),
                pltpu.SemaphoreType.DMA((5,)),
            ],
        ),
        out_shape=[
            shape((rows, width), F32),
            shape((stacked, rows), BF),
            shape((rows, stacked), BF),
            shape((rows, width), F32),
            shape((rows, width), BF),
            sums,
            up_sums,
        ],
        compiler_params=params(60),
        cost_estimate=pl.CostEstimate(
            flops=2 * rows * width * (4 * hidden_units + 2 * width),
            bytes_accessed=40 * rows * width,
            transcendentals=0,
        ),
        name="row_pass",
    )(bounds, mixed, hidden, cotangent, vectors, bias_up, gathered)


def split_owners(place_ref, keep_ref, send_ref, tile_of, count, lead=()):
    first = place_ref[3] == 0
    for chip in range(count // 2):
        even, odd = tile_of(2 * chip), tile_of(2 * chip + 1)
        keep_ref[(chip,) + lead] = jnp.where(first, even, odd).astype(BF)
        send_ref[(chip,) + lead] = jnp.where(first, odd, even).astype(BF)


def down_grad_kernel(place_ref, left_ref, right_ref, keep_ref, send_ref):
    part = keep_ref.shape[1]
    product = dot(left_ref[...], right_ref[...])
    count = product.shape[0] // part
    split_owners(place_ref, keep_ref, send_ref, lambda o: product[o * part : (o + 1) * part], count)


def down_grad(place, left, right, width, count):
    rows = left.shape[1]
    steps = left.shape[0] // width - 2
    part = steps * width // count
    half = count // 2
    spec = pl.BlockSpec((half // steps, part, width), lambda step, place: (step, 0, 0))
    return pl.pallas_call(
        down_grad_kernel,
        grid_spec=pltpu.PrefetchScalarGridSpec(
            num_scalar_prefetch=1,
            grid=(steps,),
            in_specs=[
                pl.BlockSpec((width, rows), lambda step, place: (step, 0)),
                pl.BlockSpec((rows, width), lambda step, place: (0, 0)),
            ],
            out_specs=[spec, spec],
        ),
        out_shape=[jax.ShapeDtypeStruct((half, part, width), BF)] * 2,
        compiler_params=params(48),
        cost_estimate=pl.CostEstimate(
            flops=rows * width, bytes_accessed=rows * width, transcendentals=0
        ),
        name="grad_w_down",
    )(place, left, right)


def up_grad_kernel(place_ref, left_ref, right_ref, keep_ref, send_ref):
    part = keep_ref.shape[2]
    product = dot(left_ref[...], right_ref[...])
    count = product.shape[0] // part
    split_owners(
        place_ref, keep_ref, send_ref, lambda o: product[o * part : (o + 1) * part], count, (0,)
    )


def up_grad(place, left, right, width, count):
    rows = left.shape[1]
    wide = left.shape[0] // width - 2
    half, part = count // 2, width // count
    spec = pl.BlockSpec((half, 1, part, width), lambda step, place: (0, step, 0, 0))
    return pl.pallas_call(
        up_grad_kernel,
        grid_spec=pltpu.PrefetchScalarGridSpec(
            num_scalar_prefetch=1,
            grid=(wide + 1,),
            in_specs=[
                pl.BlockSpec((width, rows), lambda step, place: (wide + step // wide, 0)),
                pl.BlockSpec((rows, width), lambda step, place: (0, 1 + step)),
            ],
            out_specs=[spec, spec],
        ),
        out_shape=[jax.ShapeDtypeStruct((half, wide + 1, part, width), BF)] * 2,
        compiler_params=params(48),
        cost_estimate=pl.CostEstimate(
            flops=rows * width, bytes_accessed=rows * width, transcendentals=0
        ),
        name="grad_w_up_out",
    )(place, left, right)


def backward_and_grads_kernel(
    place_ref, q_ref, k_ref, v_ref, mixed_ref, grad_ref, probs_ref, turned_ref, sums_ref, up_sums_ref,
    dq_ref, dk_ref, dv_ref, *refs, scale, part, inner_part
):
    outs, bias_ref = refs[:-1], refs[-1]
    stack = (dq_ref, dk_ref, dv_ref)
    attention_backward_kernel(
        q_ref, k_ref, v_ref, mixed_ref, grad_ref, probs_ref, *stack, scale=scale
    )
    width, rows = turned_ref.shape
    pair = pl.program_id(0)
    joined = jnp.concatenate([ref[...] for ref in stack], axis=1)
    product = dot(turned_ref[...], joined)
    totals = dot(jnp.ones((8, rows), BF), joined)
    bias_ref[pair] = totals

    def tile_of_third(third):
        lanes = slice(third * PAIR, (third + 1) * PAIR)
        return lambda owner: product[owner * part : (owner + 1) * part, lanes]

    for third in range(3):
        split_owners(
            place_ref, outs[2 * third], outs[2 * third + 1], tile_of_third(third), width // part
        )

    @pl.when(pair == pl.num_programs(0) - 1)
    def _():
        count = width // PAIR
        biases = [
            jnp.concatenate([bias_ref[i][0:1, start : start + PAIR] for i in range(count)], axis=1)
            for start in (0, 2 * PAIR)
        ]
        vectors = jnp.concatenate(biases + [sums_ref[0:6, :]], axis=0)
        top = lax.broadcasted_iota(jnp.int32, (8, 1), 0) == 0

        def tile_of(owner):
            own = pltpu.roll(vectors, width - owner * part, 1) if owner else vectors
            start = owner * inner_part // PAIR * PAIR
            last = start + 2 * PAIR <= up_sums_ref.shape[1]
            second = start + PAIR if last else start
            long = jnp.concatenate(
                [up_sums_ref[:, start : start + PAIR], up_sums_ref[:, second : second + PAIR]],
                axis=1,
            )
            shift = owner * inner_part - start
            long = pltpu.roll(long, 2 * PAIR - shift, 1) if shift else long
            return jnp.concatenate(
                [own[:, :PAIR], jnp.where(top, long[:, :PAIR], 0.0), jnp.zeros((8, width - 2 * PAIR), F32)],
                axis=1,
            )

        split_owners(place_ref, outs[6], outs[7], tile_of, width // part)


def backward_and_grads(place, stacked, mixed, grad_mixed, probs, turned, sums, up_sums, count):
    rows, width = mixed.shape
    pairs = width // PAIR
    part = width // count
    half = count // 2
    shape = jax.ShapeDtypeStruct
    slab = pl.BlockSpec((half, part, PAIR), lambda pair, place: (0, 0, pair))
    extra = shape((half, 8, width), BF)
    return pl.pallas_call(
        functools.partial(
            backward_and_grads_kernel,
            scale=1.0 / math.sqrt(DH),
            part=part,
            inner_part=up_sums.shape[1] // count,
        ),
        grid_spec=pltpu.PrefetchScalarGridSpec(
            num_scalar_prefetch=1,
            grid=(pairs,),
            in_specs=[
                pair_spec(rows, 0),
                pair_spec(rows, pairs),
                pair_spec(rows, 2 * pairs),
                pair_spec(rows, 0),
                pair_spec(rows, 0),
                pl.BlockSpec((2, rows, rows), lambda pair, place: (pair, 0, 0)),
                whole_block(turned),
                whole_block(sums),
                whole_block(up_sums),
            ],
            out_specs=[pair_spec(rows, 0)] * 3 + [slab] * 6 + [whole_block(extra)] * 2,
            scratch_shapes=[pltpu.VMEM((pairs, 8, 3 * PAIR), F32)],
        ),
        out_shape=[shape((rows, width), BF)] * 3
        + [shape((half, part, width), BF)] * 6
        + [extra] * 2,
        compiler_params=params(60),
        cost_estimate=pl.CostEstimate(
            flops=rows * width, bytes_accessed=rows * width, transcendentals=0
        ),
        name="attention_backward_grads",
    )(place, *[stacked] * 3, mixed, grad_mixed, probs, turned, sums, up_sums)


def hidden_grad_kernel(grad_sum_ref, weight_ref, *refs):
    out_ref = refs[-1]
    stack = refs[:-1]
    total = grad_sum_ref[...]
    start = 0
    for ref in stack:
        size = ref.shape[1]
        total += dot_last(ref[...], weight_ref[:, start : start + size])
        start += size
    out_ref[...] = total


def hidden_grad(grad_sum, weight, stack, span=256):
    rows, width = grad_sum.shape
    return pl.pallas_call(
        hidden_grad_kernel,
        grid=(rows // span,),
        in_specs=[pl.BlockSpec((span, width), lambda step: (step, 0)), whole_block(weight)]
        + [pl.BlockSpec((span, array.shape[1]), lambda step: (step, 0)) for array in stack],
        out_specs=pl.BlockSpec((span, width), lambda step: (step, 0)),
        out_shape=jax.ShapeDtypeStruct((rows, width), F32),
        compiler_params=params(48),
        cost_estimate=pl.CostEstimate(
            flops=rows * width, bytes_accessed=rows * width, transcendentals=0
        ),
        name="grad_hidden",
    )(grad_sum, weight, *stack)


def meshed_layer(
    hidden, lengths, w_qkv, bias_q, bias_v, w_out, bias_out, norm1_gain, norm1_bias, w_up, bias_up,
    w_down, bias_down, norm2_gain, norm2_bias, cotangent
):
    count_rows, width = hidden.shape
    hidden_units = w_up.shape[1]
    n = lax.axis_size("fsdp")
    part = width // n
    inner_part = hidden_units // n
    wide = hidden_units // width
    bounds = jnp.cumsum(lengths)
    coords = coordinates(lax.axis_index("fsdp"))
    place = jnp.stack([jnp.asarray(coord, jnp.int32) for coord in coords])

    gathered = lax.all_gather(pack_weights(w_down, w_up, w_out), "fsdp", axis=0, tiled=True)
    gathered = gathered.reshape(n, -1, width)
    vectors = jnp.stack(
        [bias_q, bias_v, bias_out, norm1_gain, norm1_bias, bias_down, norm2_gain, norm2_bias]
    )
    front = pack_front(w_qkv, vectors, bias_up[None])
    pieces = gather_square(front)
    stacked, whole_qkv, whole_vectors, whole_up_bias, hidden_turned = project(
        place, hidden, pieces, hidden_units, n
    )
    mixed, probs = attention_forward(bounds, stacked)
    output, left, right, grad_sum, grad_mixed, sums, up_sums = row_pass(
        bounds, mixed, hidden, cotangent, whole_vectors, whole_up_bias, gathered, inner_part
    )
    core = (0, 0, 0, 1)
    up_keep, up_send = up_grad(place, left, right, width, n)
    up_came = moved(up_send, core)
    down_keep, down_send = down_grad(place, after(left, up_keep), right, width, n)
    down_came = moved(down_send, core)
    up_keep, up_came = (array.reshape(n // 2, -1, width) for array in (up_keep, up_came))
    keep, by_x, by_y = first_sum(place, (down_keep, down_came), (up_keep, up_came))
    from_x, from_y = moved(by_x, NEAR[0]), moved(by_y, NEAR[1])
    stack = backward_and_grads(
        place, stacked, mixed, after(grad_mixed, by_x, by_y), probs, hidden_turned, sums, up_sums, n
    )
    stack, qkv_halves = stack[:3], stack[3:]
    own, by_y, by_x = second_sum(place, keep, after(from_x, *stack), after(from_y, *stack))
    low, high = moved(by_y, NEAR[1]), moved(by_x, NEAR[0])
    qkv_pairs = [(qkv_halves[i], moved(qkv_halves[i + 1], core)) for i in (0, 2, 4, 6)]
    here, *sends = near_sum(place, *qkv_pairs)
    total = far_add(own, after(low, *sends), after(high, *sends))
    grad_hidden = hidden_grad(after(grad_sum, total), whole_qkv, stack)
    total = far_scatter(total)
    qkv_parts = send_near(sends)
    qkv_parts = [after(part, grad_hidden) for part in qkv_parts]
    qkv_mine, qkv_far = reduce_far([here] + qkv_parts, coords)
    my_up_out = total[inner_part:].reshape(wide + 1, part, width)
    my_down = total[:inner_part]
    my_up = my_up_out[:wide].transpose(1, 0, 2).reshape(part, hidden_units)
    my_out = my_up_out[wide]
    mine_qkv = total_of(
        qkv_mine, [after(came, my_up, my_out, my_down) for came in send_far(qkv_far)]
    )
    my_qkv = jnp.concatenate([mine_qkv[part * i : part * (i + 1)] for i in range(3)], axis=1)
    my_vectors = mine_qkv[3 * part :]
    my_bias_q, my_bias_v, my_bias_out, my_gain_one, my_shift_one, my_bias_down, my_gain_two, my_shift_two = (
        my_vectors[i, :part] for i in range(8)
    )
    my_bias_up = my_vectors[0, PAIR : PAIR + inner_part]
    return (
        output,
        grad_hidden,
        my_qkv,
        my_bias_q,
        my_bias_v,
        my_out,
        my_bias_out,
        my_gain_one,
        my_shift_one,
        my_up,
        my_bias_up,
        my_down,
        my_bias_down,
        my_gain_two,
        my_shift_two,
    )


def layer(*arrays):
    known = lax.axis_size("fsdp") == math.prod(CHIPS)
    return (meshed_layer if known else general_layer)(*arrays)


def solution(mesh):
    rows = P("fsdp", None)
    flat = P("fsdp")
    weights = (rows, flat, flat, rows, flat, flat, flat, rows, flat, rows, flat, flat, flat)
    return jax.shard_map(
        layer,
        mesh=mesh,
        in_specs=(rows, flat) + weights + (rows,),
        out_specs=(rows, rows) + weights,
        check_vma=False,
    )
```
